256 devices in a mesh: ctx: 16 (over z, core), head: 16 (over x, y).
Axes of the slice: x: 4, y: 4, z: 8, core: 2. Of those that a mesh axis runs over, the one named last changes fastest.
Arguments:
- queries: bfloat16 [16384, 2048], P(('ctx', 'head')), may hold values from -6 to 6
- keys: bfloat16 [16384, 2048], P(('ctx', 'head')), may hold values from -3 to 3
- values: bfloat16 [16384, 4096], P(('ctx', 'head')), may hold values from -6 to 6
- out_grad: bfloat16 [16384, 4096], P(('ctx', 'head')), may hold values from -6 to 6
- log_gates: bfloat16 [16384, 2048], P(('ctx', 'head')), may hold values from -1 to 0, as said below
- live_blocks: int32 [16], P('ctx'), may hold values from 1 to 16, 160 in all
- block_doc: int32 [256], P('ctx'), may hold values from 0 to 3, never falling along the last dimension, each value on 1 to 128 neighbouring positions
Outputs:
- query_grad: bfloat16 [16384, 2048], P(('ctx', 'head'))
- key_grad: bfloat16 [16384, 2048], P(('ctx', 'head'))
- value_grad: bfloat16 [16384, 4096], P(('ctx', 'head'))
- gate_grad: bfloat16 [16384, 2048], P(('ctx', 'head'))
The draws below stay inside these ranges and needn't reach their ends.
Inputs may be any that keep to these rules, and one draw needn't show every extreme that they name: `live_blocks`: live blocks of each context owner's 16 blocks; an owner's live blocks come first in its part of the sequence and its padding blocks after; together they number 16 * 16 * 5 // 8, and some owner has all of its blocks live. `block_doc`: ids never fall along the sequence and start at 0; each of the 4 documents covers 1 to 128 blocks, one exactly 128. `log_gates`: never positive.
All inputs are finite; a program needn't handle non-finite values.
Results may differ from the reference program's by a relative error of at most 0.001.
Values may be sent and summed in bfloat16 or wider, within the bound.
No kernel may reach another device: no remote copies, remote signals or barrier semaphores. Data moves between devices by JAX's collectives and lax.ppermute only.
A program may use at most 64 MiB of HBM per device.

```python
import math
import jax
import jax.numpy as jnp
import numpy as np
from jax import lax

DK = 128
DV = 256
BLOCK = 64
DOCS = 4
TOK_DEV = 1024
HEADS = 16
BLOCKS_DEV = 16
TOKEN_TOTAL = 16384
NBLOCK = 256
SHARDS = 16


def draw_log_gates(key, part):
    key = jax.random.fold_in(key, 7)
    key_pieces = jax.random.split(key, 7)
    feature_channels = HEADS * DK
    slow_pick = jax.random.uniform(key_pieces[1], (feature_channels,)) < 0.5
    gradual_logarithm = jax.random.uniform(key_pieces[0], (feature_channels,), jnp.float32, math.log(0.1 / TOKEN_TOTAL), math.log(0.5 / TOKEN_TOTAL))
    fast_log = jax.random.uniform(key_pieces[6], (feature_channels,), jnp.float32, math.log(0.5 / TOK_DEV), math.log(1.0 / 30.0))
    log_decay_rate = jnp.where(slow_pick, gradual_logarithm, fast_log)
    jitter_level = jax.random.uniform(key_pieces[2], (TOKEN_TOTAL, feature_channels), jnp.float32, 0.5, 1.5)
    blocks = jnp.exp(jax.random.uniform(key_pieces[3], (TOKEN_TOTAL // TOK_DEV, feature_channels), jnp.float32, math.log(0.5), math.log(2.0)))
    rows_per_block = jnp.repeat(blocks, TOK_DEV, axis=0)
    spike_positions = jax.random.randint(key_pieces[4], (3,), 0, TOKEN_TOTAL)
    spike_rows = jnp.any(jnp.arange(TOKEN_TOTAL)[:, None] == spike_positions[None, :], axis=1).astype(jnp.float32)
    spike_depth = jax.random.uniform(key_pieces[5], (feature_channels,), jnp.float32, 0.22, 0.69)
    logged_values = -jnp.exp(log_decay_rate)[None, :] * jitter_level * rows_per_block - spike_rows[:, None] * spike_depth[None, :]
    return logged_values.astype(jnp.bfloat16)


def block_scale(stream_key, extent, pieces, smallest, largest):
    def one(axis_at, blocks):
        heights = jax.random.uniform(jax.random.fold_in(jax.random.fold_in(stream_key, 6), axis_at), (blocks,), jnp.float32, smallest / len(pieces), largest / len(pieces))
        return jnp.repeat(jnp.exp(heights), extent[axis_at] // blocks).reshape((-1,) + (1,) * (len(extent) - axis_at - 1))

    loudness = one(*pieces[0])
    for cut in pieces[1:]:
        loudness = loudness * one(*cut)
    return loudness


def split_up(count, total, reach, slope):
    portions = [(1 << 20) // math.isqrt(grade ** slope) + 1 for grade in range(2, count + 1)]
    surplus, holding = total - reach - (count - 1), [1] * (count - 1)
    while surplus > 0:
        free = [i for i in range(count - 1) if holding[i] < reach]
        pool, budget = sum([portions[i] for i in free]), surplus
        for i in free:
            extra = min(reach - holding[i], max(1, budget * portions[i] // pool), surplus)
            holding[i] = holding[i] + extra
            surplus = surplus - extra
    return np.array([reach] + holding)


def uneven(rng, count, total, most, slope):
    if count == 2:
        one = jax.random.randint(rng, (), max(1, total - most), min(most, total - 1) + 1)
        return jnp.stack([one, total - one])
    tallies = jnp.asarray(split_up(count, total, most, slope), jnp.int32)
    pairs = (count - 1) // 2
    donor, sink = tallies[1:1 + 2 * pairs:2], tallies[2:2 + 2 * pairs:2]
    slack = jnp.minimum(donor - 1, most - sink)
    shifted = jax.random.randint(jax.random.fold_in(rng, 1), (pairs,), 0, 1 << 20) % (slack + 1)
    tallies = tallies.at[1:1 + 2 * pairs:2].set(donor - shifted).at[2:2 + 2 * pairs:2].set(sink + shifted)
    return tallies[jax.random.permutation(jax.random.fold_in(rng, 2), count)]


def bell_draw(rng, shape, scale, most, cuts=(), held_as=jnp.bfloat16):
    factor_of = block_scale(rng, shape, cuts, -0.22, 0.18) if cuts else 1.0
    drawn = jax.random.normal(rng, shape, jnp.float32) * scale * factor_of
    return jnp.minimum(jnp.maximum(drawn, -most), most).astype(held_as)


def setup_inputs(seed: int = 0) -> dict:
    splits = jax.random.split(jax.random.key(seed), 8)
    return {
        "queries": bell_draw(splits[0], (TOKEN_TOTAL, HEADS * DK), 1.0, 6.0, ((0, 256),)),
        "keys": bell_draw(splits[1], (TOKEN_TOTAL, HEADS * DK), 0.5, 3.0, ((0, 256),)),
        "values": bell_draw(splits[2], (TOKEN_TOTAL, HEADS * DV), 1.0, 6.0, ((0, 256),)),
        "out_grad": bell_draw(splits[3], (TOKEN_TOTAL, HEADS * DV), 1.0, 6.0, ((0, 256),)),
        "log_gates": draw_log_gates(jax.random.fold_in(splits[7], 71), 0),
        "live_blocks": uneven(splits[5], SHARDS, SHARDS * BLOCKS_DEV * 5 // 8, BLOCKS_DEV, 2).astype(jnp.int32),
        "block_doc": jnp.searchsorted(jnp.cumsum(uneven(splits[6], DOCS, NBLOCK, NBLOCK // 2, 1)), jnp.arange(NBLOCK), side="right").astype(jnp.int32),
    }


FINEST_ARITHMETIC = lax.Precision.HIGHEST

def head_loss(query_rows, key_rows, payload_array, grad_rows, forgetting_entries, live_flag, keep_flag):
    active_tensor_mask = live_flag[:, None, None]
    log_cumul = jnp.cumsum(forgetting_entries * active_tensor_mask, axis=1)
    final_log = log_cumul[:, -1]
    masked_key = key_rows * active_tensor_mask
    grad_out = grad_rows * active_tensor_mask
    query_scaled = DK ** (-0.5) * query_rows * jnp.exp(log_cumul)
    rising_key = masked_key * jnp.exp(-log_cumul)
    faded_lookup_vector = masked_key * jnp.exp(final_log[:, None, :] - log_cumul)
    causal = jnp.tril(jnp.ones((BLOCK, BLOCK), jnp.float32))
    scores = jnp.einsum('nik,njk->nij', query_scaled, rising_key, precision=FINEST_ARITHMETIC) * causal
    within = jnp.einsum('nij,njv->niv', scores, payload_array, precision=FINEST_ARITHMETIC)
    memory_increment = jnp.einsum('oqz,oqg->ozg', faded_lookup_vector, payload_array, precision=FINEST_ARITHMETIC)
    decays = keep_flag[:, None] * jnp.exp(final_log)

    def advance(state_now, inputs):
        return (inputs[0][:, None] * state_now + inputs[1], state_now)
    _, before = lax.scan(advance, jnp.zeros((DK, DV), jnp.float32), (decays, memory_increment))
    incoming_state = keep_flag[:, None, None] * before
    across_blocks = jnp.einsum('yor,yrs->yos', query_scaled, incoming_state, precision=FINEST_ARITHMETIC)
    return jnp.sum(grad_out * (across_blocks + within))

def reference(queries, keys, values, out_grad, log_gates, live_blocks, block_doc):
    block_total = TOKEN_TOTAL // BLOCK
    position = jnp.arange(block_total).astype(jnp.int32)
    owner_index = (position // BLOCKS_DEV).astype(jnp.int32)
    live_flag = (position % BLOCKS_DEV < live_blocks[owner_index]).astype(jnp.float32)
    previous = jnp.concatenate([block_doc[:1], block_doc[:-1]])
    keep_flag = jnp.where((position > 0) & (previous == block_doc), 1.0, 0.0).astype(jnp.float32)

    def head_grads(head_index):

        def columns(matrix, span_width):
            begin = (head_index * span_width).astype(jnp.int32)
            picked = lax.dynamic_slice_in_dim(matrix, begin, span_width, 1)
            return picked.astype(jnp.float32).reshape(block_total, BLOCK, span_width)
        gradients = jax.grad(head_loss, argnums=(0, 1, 2, 4))(columns(queries, DK), columns(keys, DK), columns(values, DV), columns(out_grad, DV), columns(log_gates, DK), live_flag, keep_flag)
        return (gradients[0].reshape(TOKEN_TOTAL, DK).astype(jnp.bfloat16), gradients[1].reshape(TOKEN_TOTAL, DK).astype(jnp.bfloat16), gradients[2].reshape(TOKEN_TOTAL, DV).astype(jnp.bfloat16), gradients[3].reshape(TOKEN_TOTAL, DK).astype(jnp.bfloat16))
    stacked = lax.map(head_grads, jnp.arange(HEADS).astype(jnp.int32))

    def merge_heads(matrix):
        return jnp.transpose(matrix, (1, 0, 2)).reshape(TOKEN_TOTAL, HEADS * matrix.shape[-1])
    return (merge_heads(stacked[0]), merge_heads(stacked[1]), merge_heads(stacked[2]), merge_heads(stacked[3]))
```

```python
import functools

import jax
import jax.numpy as jnp
from jax import lax
from jax.experimental import pallas as pl
from jax.experimental.pallas import tpu as pltpu
from jax.sharding import PartitionSpec as P

DK = 128
DV = 256
BLOCK = 64
HEADS = 16
NB = 16
IN_W = 3 * DK + 2 * DV
OUT_W = 3 * DK + DV
QC, KC, GC, VC, UC = 0, DK, 2 * DK, 3 * DK, 3 * DK + DV
MSG = DV + 8
SCALE = DK ** (-0.5)
BF = jnp.bfloat16
F32 = jnp.float32
VMEM = pltpu.VMEM
SMEM = pltpu.SMEM


def vspec():
    return pl.BlockSpec(memory_space=VMEM)


def sspec():
    return pl.BlockSpec(memory_space=SMEM)


def split(x):
    hi = x.astype(BF)
    lo = (x - hi.astype(F32)).astype(BF)
    return hi, lo


def dot(a, b, ca, cb):
    return lax.dot_general(a, b, (((ca,), (cb,)), ((), ())), preferred_element_type=F32)


def halves(r):
    return r[:, :DK] + r[:, DK:]


def triangle(lower, strict):
    i = lax.broadcasted_iota(jnp.int32, (BLOCK, BLOCK), 0)
    j = lax.broadcasted_iota(jnp.int32, (BLOCK, BLOCK), 1)
    if lower:
        return (j < i) if strict else (j <= i)
    return j >= i


def flags(live_ref, doc_ref, prev_ref):
    live = live_ref[0]
    lives, keeps = [], []
    for b in range(NB):
        lives.append(jnp.where(b < live, 1.0, 0.0).astype(F32))
        before = prev_ref[0] if b == 0 else doc_ref[b - 1] + 1
        keeps.append(jnp.where(before == doc_ref[b] + 1, 1.0, 0.0).astype(F32))
    return lives, keeps


def pack_kernel(q, k, g, v, u, out):
    for h in range(HEADS):
        kc = slice(h * DK, (h + 1) * DK)
        vc = slice(h * DV, (h + 1) * DV)
        out[h, :, QC : QC + DK] = q[:, kc]
        out[h, :, KC : KC + DK] = k[:, kc]
        out[h, :, GC : GC + DK] = g[:, kc]
        out[h, :, VC : VC + DV] = v[:, vc]
        out[h, :, UC : UC + DV] = u[:, vc]


def pack(q, k, g, v, u):
    return pl.pallas_call(
        pack_kernel,
        out_shape=jax.ShapeDtypeStruct((HEADS, BLOCK, IN_W), BF),
        in_specs=[vspec()] * 5,
        out_specs=vspec(),
        name="pack",
    )(q, k, g, v, u)


def unpack_kernel(x, dq, dk, dv, dg):
    for h in range(HEADS):
        kc = slice(h * DK, (h + 1) * DK)
        vc = slice(h * DV, (h + 1) * DV)
        dq[:, kc] = x[h, :, 0:DK]
        dk[:, kc] = x[h, :, DK : 2 * DK]
        dg[:, kc] = x[h, :, 2 * DK : 3 * DK]
        dv[:, vc] = x[h, :, 3 * DK :]


def unpack(x):
    narrow = jax.ShapeDtypeStruct((BLOCK, HEADS * DK), BF)
    wide = jax.ShapeDtypeStruct((BLOCK, HEADS * DV), BF)
    return pl.pallas_call(
        unpack_kernel,
        out_shape=(narrow, narrow, wide, narrow),
        in_specs=[vspec()],
        out_specs=(vspec(),) * 4,
        name="unpack",
    )(x)


def totals_kernel(live_ref, doc_ref, prev_ref, x, fwd, bwd, kw, qw, cs):
    lives, keeps = flags(live_ref, doc_ref, prev_ref)
    tri = jnp.where(triangle(True, False), 1.0, 0.0).astype(BF)
    for b in range(NB):
        cs[b] = dot(tri, x[b, :, GC : GC + DK], 1, 0) * lives[b]
    suffix = jnp.ones((1, DK), F32)
    for b in reversed(range(NB)):
        c = cs[b]
        last = c[BLOCK - 1 : BLOCK, :]
        kf = x[b, :, KC : KC + DK].astype(F32) * (jnp.exp(last - c) * (suffix * lives[b]))
        kw[b, :, :DK], kw[b, :, DK:] = split(kf)
        suffix = suffix * (keeps[b] * jnp.exp(last))
    prefix = jnp.ones((1, DK), F32)
    for b in range(NB):
        c = cs[b]
        last = c[BLOCK - 1 : BLOCK, :]
        qt = x[b, :, QC : QC + DK].astype(F32) * (
            jnp.exp(c) * (prefix * (keeps[b] * lives[b] * SCALE))
        )
        qw[b, :, :DK], qw[b, :, DK:] = split(qt)
        prefix = prefix * (keeps[b] * jnp.exp(last))
    rows = NB * BLOCK
    v = x[:, :, VC : VC + DV].reshape(rows, DV)
    u = x[:, :, UC : UC + DV].reshape(rows, DV)
    fwd[:DV] = halves(dot(v, kw[...].reshape(rows, 2 * DK), 0, 0))
    bwd[:DV] = halves(dot(u, qw[...].reshape(rows, 2 * DK), 0, 0))
    fwd[DV:] = jnp.broadcast_to(prefix, (MSG - DV, DK))
    bwd[DV:] = jnp.broadcast_to(prefix, (MSG - DV, DK))


def totals(live, doc, prev, x):
    msg = jax.ShapeDtypeStruct((MSG, DK), F32)
    return pl.pallas_call(
        totals_kernel,
        out_shape=(msg, msg),
        in_specs=[sspec()] * 3 + [vspec()],
        out_specs=(vspec(),) * 2,
        scratch_shapes=[
            VMEM((NB, BLOCK, 2 * DK), BF),
            VMEM((NB, BLOCK, 2 * DK), BF),
            VMEM((NB, BLOCK, DK), F32),
        ],
        compiler_params=pltpu.CompilerParams(vmem_limit_bytes=40 * 1024 * 1024),
        name="totals",
    )(live, doc, prev, x)


def joined(near, far):
    return jnp.concatenate(
        [near[DV : DV + 1] * far[:DV] + near[:DV], near[DV:] * far[DV:]], axis=0
    )


def shift(x, by):
    n = lax.axis_size("ctx")
    return lax.ppermute(x, "ctx", [(i, i + by) for i in range(n) if 0 <= i + by < n])


def window(fwd, bwd):
    f1, f2 = shift(fwd, 1), shift(fwd, 2)
    b1, b2 = shift(bwd, -1), shift(bwd, -2)
    f, b = joined(f1, f2), joined(b1, b2)
    f2, b2 = shift(f, 2), shift(b, -2)
    f, b = joined(f, f2), joined(b, b2)
    return f, shift(f, 4), b, shift(b, -4)


def grads_kernel(live_ref, doc_ref, prev_ref, x, fn, ff, bn, bf, out, states):
    lives, keeps = flags(live_ref, doc_ref, prev_ref)
    tri = jnp.where(triangle(True, False), 1.0, 0.0).astype(BF)
    causal = triangle(True, False)
    anti = triangle(False, False)
    upper = jnp.where(anti, 1.0, 0.0).astype(BF)
    strict = jnp.where(triangle(True, True), 1.0, 0.0).astype(BF)

    def cumul(b):
        return dot(tri, x[b, :, GC : GC + DK], 1, 0) * lives[b]

    state = fn[DV : DV + 1] * ff[:DV] + fn[:DV]
    for b in range(NB):
        entering = keeps[b] * state
        states[b] = entering
        if b < NB - 1:
            c = cumul(b)
            last = c[BLOCK - 1 : BLOCK, :]
            kf = x[b, :, KC : KC + DK].astype(F32) * (jnp.exp(last - c) * lives[b])
            kfs = jnp.concatenate(split(kf), axis=1)
            state = jnp.exp(last) * entering + halves(dot(x[b, :, VC : VC + DV], kfs, 0, 0))

    grad = bn[DV : DV + 1] * bf[:DV] + bn[:DV]
    for b in reversed(range(NB)):
        c = cumul(b)
        last = c[BLOCK - 1 : BLOCK, :]
        up, down, fade = jnp.exp(c), jnp.exp(-c), jnp.exp(last - c)
        k = x[b, :, KC : KC + DK].astype(F32) * lives[b]
        qt = x[b, :, QC : QC + DK].astype(F32) * (up * SCALE)
        kt = k * down
        kf = k * fade
        v = x[b, :, VC : VC + DV]
        u = x[b, :, UC : UC + DV] * lives[b].astype(BF)
        qh, ql = split(qt)
        kh, kl = split(kt)
        fh, fl = split(kf)
        st = dot(kh, qh, 1, 1) + dot(kh, ql, 1, 1) + dot(kl, qh, 1, 1)
        st = jnp.where(anti, st, 0.0)
        ds = jnp.where(causal, dot(u, v, 1, 1), 0.0)
        dst = jnp.where(anti, dot(v, u, 1, 1), 0.0)
        sh, sl = split(st)
        dh, dl = split(ds)
        th, tl = split(dst)
        entering = states[b]
        eh, el = split(entering)
        gh, gl = split(grad)
        kk = jnp.concatenate([kh, kl], axis=1)
        qq = jnp.concatenate([qh, ql], axis=1)
        query_part = (
            halves(dot(u, jnp.concatenate([eh, el], axis=1), 1, 0))
            + halves(dot(dh, kk, 1, 0))
            + dot(dl, kh, 1, 0)
        )
        rising = halves(dot(th, qq, 1, 0)) + dot(tl, qh, 1, 0)
        falling = halves(dot(v, jnp.concatenate([gh, gl], axis=1), 1, 0))
        value_grad = (
            dot(sh, u, 1, 0)
            + dot(sl, u, 1, 0)
            + dot(fh, gh, 1, 1)
            + dot(fh, gl, 1, 1)
            + dot(fl, gh, 1, 1)
        )
        carry = jnp.sum(grad * entering, axis=0, keepdims=True) * jnp.exp(last)
        ah, al = split(query_part * qt - rising * kt)
        bh, bl = split(falling * kf)
        gate = (
            dot(upper, ah, 1, 0) + dot(upper, al, 1, 0) + dot(strict, bh, 1, 0) + dot(strict, bl, 1, 0)
        )
        out[b, :, 0:DK] = (query_part * (up * SCALE)).astype(BF)
        out[b, :, DK : 2 * DK] = ((rising * down + falling * fade) * lives[b]).astype(BF)
        out[b, :, 2 * DK : 3 * DK] = ((gate + carry) * lives[b]).astype(BF)
        out[b, :, 3 * DK :] = value_grad.astype(BF)
        if b > 0:
            grad = keeps[b] * (jnp.exp(last) * grad + halves(dot(u, qq, 0, 0)))


def grads(live, doc, prev, x, fn, ff, bn, bf):
    return pl.pallas_call(
        grads_kernel,
        out_shape=jax.ShapeDtypeStruct((NB, BLOCK, OUT_W), BF),
        in_specs=[sspec()] * 3 + [vspec()] * 5,
        out_specs=vspec(),
        scratch_shapes=[VMEM((NB, DV, DK), F32)],
        compiler_params=pltpu.CompilerParams(vmem_limit_bytes=40 * 1024 * 1024),
        name="grads",
    )(live, doc, prev, x, fn, ff, bn, bf)


def per_device(queries, keys, values, out_grad, log_gates, live_blocks, block_doc):
    prev = shift(block_doc[NB - 1 :] + 1, 1)
    packed = pack(queries, keys, log_gates, values, out_grad)
    x = lax.all_to_all(packed, "head", split_axis=0, concat_axis=0, tiled=True)
    fwd, bwd = totals(live_blocks, block_doc, prev, x)
    fn, ff, bn, bf = window(fwd, bwd)
    y = grads(live_blocks, block_doc, prev, x, fn, ff, bn, bf)
    return unpack(lax.all_to_all(y, "head", split_axis=0, concat_axis=0, tiled=True))


def solution(mesh):
    rows = P(("ctx", "head"), None)
    return jax.shard_map(
        per_device,
        mesh=mesh,
        in_specs=(rows,) * 5 + (P("ctx"), P("ctx")),
        out_specs=(rows,) * 4,
        check_vma=False,
    )
```

```python
import functools

import jax
import jax.numpy as jnp
from jax import lax
from jax.experimental import pallas as pl
from jax.experimental.pallas import tpu as pltpu
from jax.sharding import PartitionSpec as P

DK = 128
DV = 256
BLOCK = 64
HEADS = 16
NB = 16
IN_W = 3 * DK + 2 * DV
OUT_W = 3 * DK + DV
QC, KC, GC, VC, UC = 0, DK, 2 * DK, 3 * DK, 3 * DK + DV
MSG = DV + 8
SCALE = DK ** (-0.5)
BF = jnp.bfloat16
F32 = jnp.float32
VMEM = pltpu.VMEM
SMEM = pltpu.SMEM


def vspec():
    return pl.BlockSpec(memory_space=VMEM)


def sspec():
    return pl.BlockSpec(memory_space=SMEM)


def split(x):
    hi = x.astype(BF)
    lo = (x - hi.astype(F32)).astype(BF)
    return hi, lo


def dot(a, b, ca, cb):
    return lax.dot_general(a, b, (((ca,), (cb,)), ((), ())), preferred_element_type=F32)


def halves(r):
    return r[:, :DK] + r[:, DK:]


def triangle(lower, strict):
    i = lax.broadcasted_iota(jnp.int32, (BLOCK, BLOCK), 0)
    j = lax.broadcasted_iota(jnp.int32, (BLOCK, BLOCK), 1)
    if lower:
        return (j < i) if strict else (j <= i)
    return j >= i


def flags(live_ref, doc_ref, prev_ref, pos_ref):
    live = live_ref[0]
    first = pos_ref[0] == 0
    lives, keeps = [], []
    for b in range(NB):
        lives.append(jnp.where(b < live, 1.0, 0.0).astype(F32))
        same = (prev_ref[NB - 1] if b == 0 else doc_ref[b - 1]) == doc_ref[b]
        if b == 0:
            same = same & jnp.logical_not(first)
        keeps.append(jnp.where(same, 1.0, 0.0).astype(F32))
    return lives, keeps


def pack_kernel(q, k, g, v, u, out):
    for h in range(HEADS):
        kc = slice(h * DK, (h + 1) * DK)
        vc = slice(h * DV, (h + 1) * DV)
        out[h, :, QC : QC + DK] = q[:, kc]
        out[h, :, KC : KC + DK] = k[:, kc]
        out[h, :, GC : GC + DK] = g[:, kc]
        out[h, :, VC : VC + DV] = v[:, vc]
        out[h, :, UC : UC + DV] = u[:, vc]


def pack(q, k, g, v, u):
    return pl.pallas_call(
        pack_kernel,
        out_shape=jax.ShapeDtypeStruct((HEADS, BLOCK, IN_W), BF),
        in_specs=[vspec()] * 5,
        out_specs=vspec(),
        name="pack",
    )(q, k, g, v, u)


def unpack_kernel(x, dq, dk, dv, dg):
    for h in range(HEADS):
        kc = slice(h * DK, (h + 1) * DK)
        vc = slice(h * DV, (h + 1) * DV)
        dq[:, kc] = x[h, :, 0:DK]
        dk[:, kc] = x[h, :, DK : 2 * DK]
        dg[:, kc] = x[h, :, 2 * DK : 3 * DK]
        dv[:, vc] = x[h, :, 3 * DK :]


def unpack(x):
    narrow = jax.ShapeDtypeStruct((BLOCK, HEADS * DK), BF)
    wide = jax.ShapeDtypeStruct((BLOCK, HEADS * DV), BF)
    return pl.pallas_call(
        unpack_kernel,
        out_shape=(narrow, narrow, wide, narrow),
        in_specs=[vspec()],
        out_specs=(vspec(),) * 4,
        name="unpack",
    )(x)


def totals_kernel(live_ref, doc_ref, prev_ref, pos_ref, x, kept, sent, kw, qw, cs):
    lives, keeps = flags(live_ref, doc_ref, prev_ref, pos_ref)
    tri = jnp.where(triangle(True, False), 1.0, 0.0).astype(BF)
    for b in range(NB):
        cs[b] = dot(tri, x[b, :, GC : GC + DK], 1, 0) * lives[b]
    suffix = jnp.ones((1, DK), F32)
    for b in reversed(range(NB)):
        c = cs[b]
        last = c[BLOCK - 1 : BLOCK, :]
        kf = x[b, :, KC : KC + DK].astype(F32) * (jnp.exp(last - c) * (suffix * lives[b]))
        kw[b, :, :DK], kw[b, :, DK:] = split(kf)
        suffix = suffix * (keeps[b] * jnp.exp(last))
    prefix = jnp.ones((1, DK), F32)
    for b in range(NB):
        c = cs[b]
        last = c[BLOCK - 1 : BLOCK, :]
        qt = x[b, :, QC : QC + DK].astype(F32) * (
            jnp.exp(c) * (prefix * (keeps[b] * lives[b] * SCALE))
        )
        qw[b, :, :DK], qw[b, :, DK:] = split(qt)
        prefix = prefix * (keeps[b] * jnp.exp(last))
    rows = NB * BLOCK
    v = x[:, :, VC : VC + DV].reshape(rows, DV)
    u = x[:, :, UC : UC + DV].reshape(rows, DV)
    fwd = halves(dot(v, kw[...].reshape(rows, 2 * DK), 0, 0))
    bwd = halves(dot(u, qw[...].reshape(rows, 2 * DK), 0, 0))
    even = lax.rem(pos_ref[0], 2) == 0
    kept[:DV] = jnp.where(even, fwd, bwd)
    sent[:DV] = jnp.where(even, bwd, fwd)
    kept[DV:] = jnp.broadcast_to(prefix, (MSG - DV, DK))
    sent[DV:] = jnp.broadcast_to(prefix, (MSG - DV, DK))


def totals(live, doc, prev, pos, x):
    msg = jax.ShapeDtypeStruct((MSG, DK), F32)
    return pl.pallas_call(
        totals_kernel,
        out_shape=(msg, msg),
        in_specs=[sspec()] * 4 + [vspec()],
        out_specs=(vspec(),) * 2,
        scratch_shapes=[
            VMEM((NB, BLOCK, 2 * DK), BF),
            VMEM((NB, BLOCK, 2 * DK), BF),
            VMEM((NB, BLOCK, DK), F32),
        ],
        compiler_params=pltpu.CompilerParams(vmem_limit_bytes=40 * 1024 * 1024),
        name="totals",
    )(live, doc, prev, pos, x)


def joined(near, far):
    return jnp.concatenate(
        [near[DV : DV + 1] * far[:DV] + near[:DV], near[DV:] * far[DV:]], axis=0
    )


def swapped(x):
    n = lax.axis_size("ctx")
    return lax.ppermute(x, "ctx", [(i, i ^ 1) for i in range(n)])


def upstream(x, index, by):
    n = lax.axis_size("ctx")
    moved = lax.ppermute(
        x, "ctx", [(i, (i + (2 * by if i % 2 == 0 else -2 * by)) % n) for i in range(n)]
    )
    source = jnp.where(index % 2 == 0, index - 2 * by, index + 2 * by)
    return jnp.where((source >= 0) & (source < n), moved, 0.0)


def window(kept, sent, index):
    other = swapped(sent)
    chip = joined(other, kept)
    e = joined(upstream(chip, index, 1), upstream(chip, index, 2))
    e = joined(e, upstream(e, index, 2))
    return e, swapped(joined(kept, e))


def grads_kernel(live_ref, doc_ref, prev_ref, pos_ref, x, own, other, out, states):
    lives, keeps = flags(live_ref, doc_ref, prev_ref, pos_ref)
    tri = jnp.where(triangle(True, False), 1.0, 0.0).astype(BF)
    causal = triangle(True, False)
    anti = triangle(False, False)
    upper = jnp.where(anti, 1.0, 0.0).astype(BF)
    strict = jnp.where(triangle(True, True), 1.0, 0.0).astype(BF)

    def cumul(b):
        return dot(tri, x[b, :, GC : GC + DK], 1, 0) * lives[b]

    even = lax.rem(pos_ref[0], 2) == 0
    state = jnp.where(even, own[:DV], other[:DV])
    for b in range(NB):
        entering = keeps[b] * state
        states[b] = entering
        if b < NB - 1:
            c = cumul(b)
            last = c[BLOCK - 1 : BLOCK, :]
            kf = x[b, :, KC : KC + DK].astype(F32) * (jnp.exp(last - c) * lives[b])
            kfs = jnp.concatenate(split(kf), axis=1)
            state = jnp.exp(last) * entering + halves(dot(x[b, :, VC : VC + DV], kfs, 0, 0))

    grad = jnp.where(even, other[:DV], own[:DV])
    for b in reversed(range(NB)):
        c = cumul(b)
        last = c[BLOCK - 1 : BLOCK, :]
        up, down, fade = jnp.exp(c), jnp.exp(-c), jnp.exp(last - c)
        k = x[b, :, KC : KC + DK].astype(F32) * lives[b]
        qt = x[b, :, QC : QC + DK].astype(F32) * (up * SCALE)
        kt = k * down
        kf = k * fade
        v = x[b, :, VC : VC + DV]
        u = x[b, :, UC : UC + DV] * lives[b].astype(BF)
        qh, ql = split(qt)
        kh, kl = split(kt)
        fh, fl = split(kf)
        st = dot(kh, qh, 1, 1) + dot(kh, ql, 1, 1) + dot(kl, qh, 1, 1)
        st = jnp.where(anti, st, 0.0)
        ds = jnp.where(causal, dot(u, v, 1, 1), 0.0)
        dst = jnp.where(anti, dot(v, u, 1, 1), 0.0)
        sh, sl = split(st)
        dh, dl = split(ds)
        th, tl = split(dst)
        entering = states[b]
        eh, el = split(entering)
        gh, gl = split(grad)
        kk = jnp.concatenate([kh, kl], axis=1)
        qq = jnp.concatenate([qh, ql], axis=1)
        query_part = (
            halves(dot(u, jnp.concatenate([eh, el], axis=1), 1, 0))
            + halves(dot(dh, kk, 1, 0))
            + dot(dl, kh, 1, 0)
        )
        rising = halves(dot(th, qq, 1, 0)) + dot(tl, qh, 1, 0)
        falling = halves(dot(v, jnp.concatenate([gh, gl], axis=1), 1, 0))
        value_grad = (
            dot(sh, u, 1, 0)
            + dot(sl, u, 1, 0)
            + dot(fh, gh, 1, 1)
            + dot(fh, gl, 1, 1)
            + dot(fl, gh, 1, 1)
        )
        carry = jnp.sum(grad * entering, axis=0, keepdims=True) * jnp.exp(last)
        ah, al = split(query_part * qt - rising * kt)
        bh, bl = split(falling * kf)
        gate = (
            dot(upper, ah, 1, 0) + dot(upper, al, 1, 0) + dot(strict, bh, 1, 0) + dot(strict, bl, 1, 0)
        )
        out[b, :, 0:DK] = (query_part * (up * SCALE)).astype(BF)
        out[b, :, DK : 2 * DK] = ((rising * down + falling * fade) * lives[b]).astype(BF)
        out[b, :, 2 * DK : 3 * DK] = ((gate + carry) * lives[b]).astype(BF)
        out[b, :, 3 * DK :] = value_grad.astype(BF)
        if b > 0:
            grad = keeps[b] * (jnp.exp(last) * grad + halves(dot(u, qq, 0, 0)))


def grads(live, doc, prev, pos, x, own, other):
    return pl.pallas_call(
        grads_kernel,
        out_shape=jax.ShapeDtypeStruct((NB, BLOCK, OUT_W), BF),
        in_specs=[sspec()] * 4 + [vspec()] * 3,
        out_specs=vspec(),
        scratch_shapes=[VMEM((NB, DV, DK), F32)],
        compiler_params=pltpu.CompilerParams(vmem_limit_bytes=40 * 1024 * 1024),
        name="grads",
    )(live, doc, prev, pos, x, own, other)


def per_device(queries, keys, values, out_grad, log_gates, live_blocks, block_doc):
    n = lax.axis_size("ctx")
    index = lax.axis_index("ctx")
    pos = index.reshape(1)
    prev = lax.ppermute(block_doc, "ctx", [(i, (i + 1) % n) for i in range(n)])
    packed = pack(queries, keys, log_gates, values, out_grad)
    x = lax.all_to_all(packed, "head", split_axis=0, concat_axis=0, tiled=True)
    kept, sent = totals(live_blocks, block_doc, prev, pos, x)
    own, other = window(kept, sent, index)
    y = grads(live_blocks, block_doc, prev, pos, x, own, other)
    return unpack(lax.all_to_all(y, "head", split_axis=0, concat_axis=0, tiled=True))


def solution(mesh):
    rows = P(("ctx", "head"), None)
    return jax.shard_map(
        per_device,
        mesh=mesh,
        in_specs=(rows,) * 5 + (P("ctx"), P("ctx")),
        out_specs=(rows,) * 4,
        check_vma=False,
    )
```

```python
import functools

import jax
import jax.numpy as jnp
from jax import lax
from jax.experimental import pallas as pl
from jax.experimental.pallas import tpu as pltpu
from jax.sharding import PartitionSpec as P

DK = 128
DV = 256
BLOCK = 64
HEADS = 16
NB = 16
IN_W = 3 * DK + 2 * DV
OUT_W = 3 * DK + DV
QC, KC, GC, VC, UC = 0, DK, 2 * DK, 3 * DK, 3 * DK + DV
MSG = DV + 8
SCALE = DK ** (-0.5)
BF = jnp.bfloat16
F32 = jnp.float32
VMEM = pltpu.VMEM
SMEM = pltpu.SMEM


def vspec():
    return pl.BlockSpec(memory_space=VMEM)


def sspec():
    return pl.BlockSpec(memory_space=SMEM)


def split(x):
    hi = x.astype(BF)
    lo = (x - hi.astype(F32)).astype(BF)
    return hi, lo


def dot(a, b, ca, cb):
    return lax.dot_general(a, b, (((ca,), (cb,)), ((), ())), preferred_element_type=F32)


def halves(r):
    return r[:, :DK] + r[:, DK:]


def triangle(lower, strict):
    i = lax.broadcasted_iota(jnp.int32, (BLOCK, BLOCK), 0)
    j = lax.broadcasted_iota(jnp.int32, (BLOCK, BLOCK), 1)
    if lower:
        return (j < i) if strict else (j <= i)
    return j >= i


def flags(live_ref, doc_ref, prev_ref, pos_ref):
    live = live_ref[0]
    first = pos_ref[0] == 0
    lives, keeps = [], []
    for b in range(NB):
        lives.append(jnp.where(b < live, 1.0, 0.0).astype(F32))
        same = (prev_ref[NB - 1] if b == 0 else doc_ref[b - 1]) == doc_ref[b]
        if b == 0:
            same = same & jnp.logical_not(first)
        keeps.append(jnp.where(same, 1.0, 0.0).astype(F32))
    return lives, keeps


PACK_STEPS = 2
PER = HEADS // PACK_STEPS


def pack_kernel(q, k, g, v, u, out):
    for h in range(PER):
        kc = slice(h * DK, (h + 1) * DK)
        vc = slice(h * DV, (h + 1) * DV)
        out[h, :, QC : QC + DK] = q[:, kc]
        out[h, :, KC : KC + DK] = k[:, kc]
        out[h, :, GC : GC + DK] = g[:, kc]
        out[h, :, VC : VC + DV] = v[:, vc]
        out[h, :, UC : UC + DV] = u[:, vc]


def pack(q, k, g, v, u):
    narrow = pl.BlockSpec((BLOCK, PER * DK), lambda i: (0, i))
    wide = pl.BlockSpec((BLOCK, PER * DV), lambda i: (0, i))
    return pl.pallas_call(
        pack_kernel,
        grid=(PACK_STEPS,),
        out_shape=jax.ShapeDtypeStruct((HEADS, BLOCK, IN_W), BF),
        in_specs=[narrow] * 3 + [wide] * 2,
        out_specs=pl.BlockSpec((PER, BLOCK, IN_W), lambda i: (i, 0, 0)),
        name="pack",
    )(q, k, g, v, u)


def unpack_kernel(x, dq, dk, dv, dg):
    for h in range(HEADS):
        kc = slice(h * DK, (h + 1) * DK)
        vc = slice(h * DV, (h + 1) * DV)
        dq[:, kc] = x[h, :, 0:DK]
        dk[:, kc] = x[h, :, DK : 2 * DK]
        dg[:, kc] = x[h, :, 2 * DK : 3 * DK]
        dv[:, vc] = x[h, :, 3 * DK :]


def unpack(x):
    narrow = jax.ShapeDtypeStruct((BLOCK, HEADS * DK), BF)
    wide = jax.ShapeDtypeStruct((BLOCK, HEADS * DV), BF)
    return pl.pallas_call(
        unpack_kernel,
        out_shape=(narrow, narrow, wide, narrow),
        in_specs=[vspec()],
        out_specs=(vspec(),) * 4,
        compiler_params=pltpu.CompilerParams(vmem_limit_bytes=16 * 1024 * 1024),
        name="unpack",
    )(x)


def totals_kernel(live_ref, doc_ref, prev_ref, pos_ref, x, kept, sent, kw, qw, cs):
    lives, keeps = flags(live_ref, doc_ref, prev_ref, pos_ref)
    tri = jnp.where(triangle(True, False), 1.0, 0.0).astype(BF)
    for b in range(NB):
        cs[b] = dot(tri, x[b, :, GC : GC + DK], 1, 0) * lives[b]
    suffix = jnp.ones((1, DK), F32)
    for b in reversed(range(NB)):
        c = cs[b]
        last = c[BLOCK - 1 : BLOCK, :]
        kf = x[b, :, KC : KC + DK].astype(F32) * (jnp.exp(last - c) * (suffix * lives[b]))
        kw[b, :, :DK], kw[b, :, DK:] = split(kf)
        suffix = suffix * (keeps[b] * jnp.exp(last))
    prefix = jnp.ones((1, DK), F32)
    for b in range(NB):
        c = cs[b]
        last = c[BLOCK - 1 : BLOCK, :]
        qt = x[b, :, QC : QC + DK].astype(F32) * (
            jnp.exp(c) * (prefix * (keeps[b] * lives[b] * SCALE))
        )
        qw[b, :, :DK], qw[b, :, DK:] = split(qt)
        prefix = prefix * (keeps[b] * jnp.exp(last))
    rows = NB * BLOCK
    v = x[:, :, VC : VC + DV].reshape(rows, DV)
    u = x[:, :, UC : UC + DV].reshape(rows, DV)
    fwd = halves(dot(v, kw[...].reshape(rows, 2 * DK), 0, 0))
    bwd = halves(dot(u, qw[...].reshape(rows, 2 * DK), 0, 0))
    even = lax.rem(pos_ref[0], 2) == 0
    kept[:DV] = jnp.where(even, fwd, bwd)
    sent[:DV] = jnp.where(even, bwd, fwd)
    kept[DV:] = jnp.broadcast_to(prefix, (MSG - DV, DK))
    sent[DV:] = jnp.broadcast_to(prefix, (MSG - DV, DK))


def totals(live, doc, prev, pos, x):
    msg = jax.ShapeDtypeStruct((MSG, DK), F32)
    return pl.pallas_call(
        totals_kernel,
        out_shape=(msg, msg),
        in_specs=[sspec()] * 4 + [vspec()],
        out_specs=(vspec(),) * 2,
        scratch_shapes=[
            VMEM((NB, BLOCK, 2 * DK), BF),
            VMEM((NB, BLOCK, 2 * DK), BF),
            VMEM((NB, BLOCK, DK), F32),
        ],
        compiler_params=pltpu.CompilerParams(vmem_limit_bytes=40 * 1024 * 1024),
        name="totals",
    )(live, doc, prev, pos, x)


def joined(near, far):
    return jnp.concatenate(
        [near[DV : DV + 1] * far[:DV] + near[:DV], near[DV:] * far[DV:]], axis=0
    )


def swapped(x):
    n = lax.axis_size("ctx")
    return lax.ppermute(x, "ctx", [(i, i ^ 1) for i in range(n)])


def upstream(x, index, by):
    n = lax.axis_size("ctx")
    moved = lax.ppermute(
        x, "ctx", [(i, (i + (2 * by if i % 2 == 0 else -2 * by)) % n) for i in range(n)]
    )
    source = jnp.where(index % 2 == 0, index - 2 * by, index + 2 * by)
    return jnp.where((source >= 0) & (source < n), moved, 0.0)


def window(kept, sent, index):
    other = swapped(sent)
    chip = joined(other, kept)
    e = joined(upstream(chip, index, 1), upstream(chip, index, 2))
    e = joined(e, upstream(e, index, 2))
    return e, swapped(joined(kept, e))


PAIR = 2 * BLOCK
NP = NB // 2


def rows_of(x, p, col, width):
    return x[2 * p : 2 * p + 2, :, col : col + width].reshape(PAIR, width)


def two(x):
    return jnp.concatenate(split(x), axis=1)


def grads_kernel(
    live_ref, doc_ref, prev_ref, pos_ref, x, own, other, out, states, qw, kw, fw, qsw, ksw
):
    lives, keeps = flags(live_ref, doc_ref, prev_ref, pos_ref)
    i = lax.broadcasted_iota(jnp.int32, (PAIR, PAIR), 0)
    j = lax.broadcasted_iota(jnp.int32, (PAIR, PAIR), 1)
    first = i < BLOCK
    same = first == (j < BLOCK)
    one = lambda m: jnp.where(m, 1.0, 0.0).astype(F32)
    tri = one((j <= i) & same).astype(BF)
    low_same, low_cross = one((j <= i) & same), one((j < i) & jnp.logical_not(same))
    up_same, up_cross = one((j >= i) & same), one((j > i) & jnp.logical_not(same))
    upper, strict = one(j >= i).astype(BF), one(j < i).astype(BF)
    sums = jnp.concatenate([upper, upper, strict, strict], axis=1)
    first_v = lax.broadcasted_iota(jnp.int32, (PAIR, DV), 0) < BLOCK

    even = lax.rem(pos_ref[0], 2) == 0
    state = jnp.where(even, own[:DV], other[:DV])
    ends = []
    for p in range(NP):
        a, b = 2 * p, 2 * p + 1
        live = jnp.where(first, lives[a], lives[b])
        c = dot(tri, rows_of(x, p, GC, DK), 1, 0) * live
        ca, cb = c[BLOCK - 1 : BLOCK], c[PAIR - 1 : PAIR]
        d = jnp.where(first, c - ca, c)
        qs, ks = jnp.exp(d), jnp.exp(-d)
        ea, eb = keeps[a] * jnp.exp(ca), jnp.exp(cb)
        ends.append((ea, eb))
        q = rows_of(x, p, QC, DK).astype(F32) * (qs * SCALE)
        k = rows_of(x, p, KC, DK).astype(F32) * (ks * live)
        kf = k * jnp.where(first, keeps[b] * eb, eb)
        qsw[p], ksw[p] = qs, ks
        qw[p], kw[p] = two(q), two(k)
        kfs = two(kf)
        fw[p] = kfs
        states[p] = two(state)
        if p < NP - 1:
            state = (ea * (keeps[b] * eb)) * state + halves(dot(rows_of(x, p, VC, DV), kfs, 0, 0))

    grad = jnp.where(even, other[:DV], own[:DV])
    for p in reversed(range(NP)):
        a, b = 2 * p, 2 * p + 1
        ea, eb = ends[p]
        live = jnp.where(first, lives[a], lives[b])
        qin = jnp.where(first, ea, ea * keeps[b])
        kout = jnp.where(first, keeps[b] * eb, eb)
        qq, kk, ff = qw[p], kw[p], fw[p]
        qh, ql, kh = qq[:, :DK], qq[:, DK:], kk[:, :DK]
        qs, ks = qsw[p], ksw[p]
        v = rows_of(x, p, VC, DV)
        u = rows_of(x, p, UC, DV) * jnp.where(first_v, lives[a], lives[b]).astype(BF)
        st = dot(kk, jnp.concatenate([qh, qh], axis=1), 1, 1) + dot(kh, ql, 1, 1)
        up = up_same + keeps[b] * up_cross
        st = jnp.where(up > 0.0, st, 0.0)
        dst = dot(v, u, 1, 1) * up
        ds = dot(u, v, 1, 1) * (low_same + keeps[b] * low_cross)
        dh, dl = split(ds)
        th, tl = split(dst)
        ss = states[p]
        gg = two(grad)
        gh, gl = gg[:, :DK], gg[:, DK:]
        query = qs * (
            halves(dot(dh, kk, 1, 0))
            + dot(dl, kh, 1, 0)
            + qin * halves(dot(u, ss, 1, 0))
        )
        rising = ks * (halves(dot(th, qq, 1, 0)) + dot(tl, qh, 1, 0))
        falling = (ks * kout) * halves(dot(v, gg, 1, 0))
        value = (
            dot(two(st), jnp.concatenate([u, u], axis=0), 1, 0)
            + dot(ff, jnp.concatenate([gh, gh], axis=1), 1, 1)
            + dot(ff[:, :DK], gl, 1, 1)
        )
        query = query * SCALE
        q = rows_of(x, p, QC, DK).astype(F32)
        k = rows_of(x, p, KC, DK).astype(F32) * live
        decay = ea * (keeps[b] * eb)
        s32 = ss[:, :DK].astype(F32) + ss[:, DK:].astype(F32)
        carry = jnp.sum(grad * s32, axis=0, keepdims=True) * decay
        terms = jnp.concatenate([*split(query * q - rising * k), *split(falling * k)], axis=0)
        gate = dot(sums, terms, 1, 0) + carry
        shape = lambda r: r.astype(BF).reshape(2, BLOCK, r.shape[1])
        out[a : a + 2, :, 0:DK] = shape(query)
        out[a : a + 2, :, DK : 2 * DK] = shape((rising + falling) * live)
        out[a : a + 2, :, 2 * DK : 3 * DK] = shape(gate * live)
        out[a : a + 2, :, 3 * DK :] = shape(value)
        if p > 0:
            qf = rows_of(x, p, QC, DK).astype(F32) * (qs * SCALE) * qin
            grad = decay * grad + halves(dot(u, two(qf), 0, 0))


def grads(live, doc, prev, pos, x, own, other):
    return pl.pallas_call(
        grads_kernel,
        out_shape=jax.ShapeDtypeStruct((NB, BLOCK, OUT_W), BF),
        in_specs=[sspec()] * 4 + [vspec()] * 3,
        out_specs=vspec(),
        scratch_shapes=[
            VMEM((NP, DV, 2 * DK), BF),
            VMEM((NP, PAIR, 2 * DK), BF),
            VMEM((NP, PAIR, 2 * DK), BF),
            VMEM((NP, PAIR, 2 * DK), BF),
            VMEM((NP, PAIR, DK), F32),
            VMEM((NP, PAIR, DK), F32),
        ],
        compiler_params=pltpu.CompilerParams(vmem_limit_bytes=40 * 1024 * 1024),
        name="grads",
    )(live, doc, prev, pos, x, own, other)


def per_device(queries, keys, values, out_grad, log_gates, live_blocks, block_doc):
    n = lax.axis_size("ctx")
    index = lax.axis_index("ctx")
    pos = index.reshape(1)
    prev = lax.ppermute(block_doc, "ctx", [(i, (i + 1) % n) for i in range(n)])
    packed = pack(queries, keys, log_gates, values, out_grad)
    x = lax.all_to_all(packed, "head", split_axis=0, concat_axis=0, tiled=True)
    kept, sent = totals(live_blocks, block_doc, prev, pos, x)
    own, other = window(kept, sent, index)
    y = grads(live_blocks, block_doc, prev, pos, x, own, other)
    return unpack(lax.all_to_all(y, "head", split_axis=0, concat_axis=0, tiled=True))


def solution(mesh):
    rows = P(("ctx", "head"), None)
    return jax.shard_map(
        per_device,
        mesh=mesh,
        in_specs=(rows,) * 5 + (P("ctx"), P("ctx")),
        out_specs=(rows,) * 4,
        check_vma=False,
    )
```

```python
import functools

import jax
import jax.numpy as jnp
from jax import lax
from jax.experimental import pallas as pl
from jax.experimental.pallas import tpu as pltpu
from jax.sharding import PartitionSpec as P

DK = 128
DV = 256
BLOCK = 64
HEADS = 16
NB = 16
IN_W = 3 * DK + 2 * DV
OUT_W = 3 * DK + DV
QC, KC, GC, VC, UC = 0, DK, 2 * DK, 3 * DK, 3 * DK + DV
MSG = DV + 8
SCALE = DK ** (-0.5)
BF = jnp.bfloat16
F32 = jnp.float32
VMEM = pltpu.VMEM
SMEM = pltpu.SMEM


def vspec():
    return pl.BlockSpec(memory_space=VMEM)


def sspec():
    return pl.BlockSpec(memory_space=SMEM)


def split(x):
    hi = x.astype(BF)
    lo = (x - hi.astype(F32)).astype(BF)
    return hi, lo


def dot(a, b, ca, cb):
    return lax.dot_general(a, b, (((ca,), (cb,)), ((), ())), preferred_element_type=F32)


def halves(r):
    return r[:, :DK] + r[:, DK:]


def triangle(lower, strict):
    i = lax.broadcasted_iota(jnp.int32, (BLOCK, BLOCK), 0)
    j = lax.broadcasted_iota(jnp.int32, (BLOCK, BLOCK), 1)
    if lower:
        return (j < i) if strict else (j <= i)
    return j >= i


def flags(live_ref, doc_ref, prev_ref, pos_ref):
    live = live_ref[0]
    first = pos_ref[0] == 0
    lives, keeps = [], []
    for b in range(NB):
        lives.append(jnp.where(b < live, 1.0, 0.0).astype(F32))
        same = (prev_ref[NB - 1] if b == 0 else doc_ref[b - 1]) == doc_ref[b]
        if b == 0:
            same = same & jnp.logical_not(first)
        keeps.append(jnp.where(same, 1.0, 0.0).astype(F32))
    return lives, keeps


PACK_STEPS = 2
PER = HEADS // PACK_STEPS


def pack_kernel(q, k, g, v, u, out):
    for h in range(PER):
        kc = slice(h * DK, (h + 1) * DK)
        vc = slice(h * DV, (h + 1) * DV)
        out[h, :, QC : QC + DK] = q[:, kc]
        out[h, :, KC : KC + DK] = k[:, kc]
        out[h, :, GC : GC + DK] = g[:, kc]
        out[h, :, VC : VC + DV] = v[:, vc]
        out[h, :, UC : UC + DV] = u[:, vc]


def pack(q, k, g, v, u):
    narrow = pl.BlockSpec((BLOCK, PER * DK), lambda i: (0, i))
    wide = pl.BlockSpec((BLOCK, PER * DV), lambda i: (0, i))
    return pl.pallas_call(
        pack_kernel,
        grid=(PACK_STEPS,),
        out_shape=jax.ShapeDtypeStruct((HEADS, BLOCK, IN_W), BF),
        in_specs=[narrow] * 3 + [wide] * 2,
        out_specs=pl.BlockSpec((PER, BLOCK, IN_W), lambda i: (i, 0, 0)),
        name="pack",
    )(q, k, g, v, u)


def unpack_kernel(x, dq, dk, dv, dg):
    for h in range(HEADS):
        kc = slice(h * DK, (h + 1) * DK)
        vc = slice(h * DV, (h + 1) * DV)
        dq[:, kc] = x[h, :, 0:DK]
        dk[:, kc] = x[h, :, DK : 2 * DK]
        dg[:, kc] = x[h, :, 2 * DK : 3 * DK]
        dv[:, vc] = x[h, :, 3 * DK :]


def unpack(x):
    narrow = jax.ShapeDtypeStruct((BLOCK, HEADS * DK), BF)
    wide = jax.ShapeDtypeStruct((BLOCK, HEADS * DV), BF)
    return pl.pallas_call(
        unpack_kernel,
        out_shape=(narrow, narrow, wide, narrow),
        in_specs=[vspec()],
        out_specs=(vspec(),) * 4,
        compiler_params=pltpu.CompilerParams(vmem_limit_bytes=16 * 1024 * 1024),
        name="unpack",
    )(x)


def totals_kernel(live_ref, doc_ref, prev_ref, pos_ref, x, kept, sent, kw, qw, cs):
    lives, keeps = flags(live_ref, doc_ref, prev_ref, pos_ref)
    tri = jnp.where(triangle(True, False), 1.0, 0.0).astype(BF)
    for b in range(NB):
        cs[b] = dot(tri, x[b, :, GC : GC + DK], 1, 0) * lives[b]
    suffix = jnp.ones((1, DK), F32)
    for b in reversed(range(NB)):
        c = cs[b]
        last = c[BLOCK - 1 : BLOCK, :]
        kf = x[b, :, KC : KC + DK].astype(F32) * (jnp.exp(last - c) * (suffix * lives[b]))
        kw[b, :, :DK], kw[b, :, DK:] = split(kf)
        suffix = suffix * (keeps[b] * jnp.exp(last))
    prefix = jnp.ones((1, DK), F32)
    for b in range(NB):
        c = cs[b]
        last = c[BLOCK - 1 : BLOCK, :]
        qt = x[b, :, QC : QC + DK].astype(F32) * (
            jnp.exp(c) * (prefix * (keeps[b] * lives[b] * SCALE))
        )
        qw[b, :, :DK], qw[b, :, DK:] = split(qt)
        prefix = prefix * (keeps[b] * jnp.exp(last))
    rows = NB * BLOCK
    v = x[:, :, VC : VC + DV].reshape(rows, DV)
    u = x[:, :, UC : UC + DV].reshape(rows, DV)
    fwd = halves(dot(v, kw[...].reshape(rows, 2 * DK), 0, 0))
    bwd = halves(dot(u, qw[...].reshape(rows, 2 * DK), 0, 0))
    even = lax.rem(pos_ref[0], 2) == 0
    kept[:DV] = jnp.where(even, fwd, bwd)
    sent[:DV] = jnp.where(even, bwd, fwd)
    kept[DV:] = jnp.broadcast_to(prefix, (MSG - DV, DK))
    sent[DV:] = jnp.broadcast_to(prefix, (MSG - DV, DK))


def totals(live, doc, prev, pos, x):
    msg = jax.ShapeDtypeStruct((MSG, DK), F32)
    return pl.pallas_call(
        totals_kernel,
        out_shape=(msg, msg),
        in_specs=[sspec()] * 4 + [vspec()],
        out_specs=(vspec(),) * 2,
        scratch_shapes=[
            VMEM((NB, BLOCK, 2 * DK), BF),
            VMEM((NB, BLOCK, 2 * DK), BF),
            VMEM((NB, BLOCK, DK), F32),
        ],
        compiler_params=pltpu.CompilerParams(vmem_limit_bytes=40 * 1024 * 1024),
        name="totals",
    )(live, doc, prev, pos, x)


def joined(near, far):
    return jnp.concatenate(
        [near[DV : DV + 1] * far[:DV] + near[:DV], near[DV:] * far[DV:]], axis=0
    )


def swapped(x):
    n = lax.axis_size("ctx")
    return lax.ppermute(x, "ctx", [(i, i ^ 1) for i in range(n)])


def upstream(x, index, by):
    n = lax.axis_size("ctx")
    moved = lax.ppermute(
        x, "ctx", [(i, (i + (2 * by if i % 2 == 0 else -2 * by)) % n) for i in range(n)]
    )
    source = jnp.where(index % 2 == 0, index - 2 * by, index + 2 * by)
    return jnp.where((source >= 0) & (source < n), moved, 0.0)


def window(kept, sent, index, beside):
    other = swapped(sent)
    chip = joined(other, kept)
    near, far = upstream(chip, index, 1), upstream(chip, index, 2)
    done = beside(chip)
    near, far, done = lax.optimization_barrier((near, far, done))
    e = joined(near, far)
    e = joined(e, upstream(e, index, 2))
    return e, swapped(joined(kept, e)), done


PAIR = 2 * BLOCK
NP = NB // 2


def rows_of(x, p, col, width):
    return x[2 * p : 2 * p + 2, :, col : col + width].reshape(PAIR, width)


def two(x):
    return jnp.concatenate(split(x), axis=1)


def one(mask):
    return jnp.where(mask, 1.0, 0.0).astype(F32)


def pair_masks():
    i = lax.broadcasted_iota(jnp.int32, (PAIR, PAIR), 0)
    j = lax.broadcasted_iota(jnp.int32, (PAIR, PAIR), 1)
    first = i < BLOCK
    return i, j, first, first == (j < BLOCK)


def local_kernel(
    live_ref, doc_ref, prev_ref, pos_ref, x,
    query_o, rise_o, fall_o, value_o, qin_o, kout_o, kf_o, state_o, grad_o, small_o,
    qw, kw, fw, qsw, ksw,
):
    lives, keeps = flags(live_ref, doc_ref, prev_ref, pos_ref)
    i, j, first, same = pair_masks()
    cross = jnp.logical_not(same)
    tri = one((j <= i) & same).astype(BF)
    low_same, low_cross = one((j <= i) & same), one((j < i) & cross)
    up_same, up_cross = one((j >= i) & same), one((j > i) & cross)
    first_v = lax.broadcasted_iota(jnp.int32, (PAIR, DV), 0) < BLOCK

    ends = []
    prefix = jnp.ones((1, DK), F32)
    for p in range(NP):
        a, b = 2 * p, 2 * p + 1
        live = jnp.where(first, lives[a], lives[b])
        c = dot(tri, rows_of(x, p, GC, DK), 1, 0) * live
        ca, cb = c[BLOCK - 1 : BLOCK], c[PAIR - 1 : PAIR]
        d = jnp.where(first, c - ca, c)
        qs, ks = jnp.exp(d), jnp.exp(-d)
        ea, eb = keeps[a] * jnp.exp(ca), jnp.exp(cb)
        decay = ea * (keeps[b] * eb)
        ends.append((ea, eb, decay))
        q = rows_of(x, p, QC, DK).astype(F32) * (qs * SCALE)
        k = rows_of(x, p, KC, DK).astype(F32) * (ks * live)
        kf = k * jnp.where(first, keeps[b] * eb, eb)
        qsw[p], ksw[p] = qs, ks
        qw[p], kw[p] = two(q), two(k)
        fw[p] = kf
        small_o[p, 0:1] = prefix
        qin_o[p] = (qs * (live * SCALE)) * (jnp.where(first, ea, ea * keeps[b]) * prefix)
        prefix = prefix * decay
        if p == 0:
            state_o[p] = jnp.zeros((DV, DK), F32)
        else:
            state_o[p] = state
        if p < NP - 1:
            update = halves(dot(rows_of(x, p, VC, DV), two(kf), 0, 0))
            state = update if p == 0 else decay * state + update

    suffix = jnp.ones((1, DK), F32)
    for p in reversed(range(NP)):
        a, b = 2 * p, 2 * p + 1
        ea, eb, decay = ends[p]
        live = jnp.where(first, lives[a], lives[b])
        qin = jnp.where(first, ea, ea * keeps[b])
        kout = jnp.where(first, keeps[b] * eb, eb)
        qq, kk = qw[p], kw[p]
        qh, ql, kh = qq[:, :DK], qq[:, DK:], kk[:, :DK]
        qs, ks = qsw[p], ksw[p]
        v = rows_of(x, p, VC, DV)
        u = rows_of(x, p, UC, DV) * jnp.where(first_v, lives[a], lives[b]).astype(BF)
        st = dot(kk, jnp.concatenate([qh, qh], axis=1), 1, 1) + dot(kh, ql, 1, 1)
        up = up_same + keeps[b] * up_cross
        st = jnp.where(up > 0.0, st, 0.0)
        dst = dot(v, u, 1, 1) * up
        ds = dot(u, v, 1, 1) * (low_same + keeps[b] * low_cross)
        dh, dl = split(ds)
        th, tl = split(dst)
        query = halves(dot(dh, kk, 1, 0)) + dot(dl, kh, 1, 0)
        if p > 0:
            query = query + qin * halves(dot(u, two(state_o[p]), 1, 0))
        query_o[p] = query * (qs * SCALE)
        rise_o[p] = ks * live * (halves(dot(th, qq, 1, 0)) + dot(tl, qh, 1, 0))
        value = dot(two(st), jnp.concatenate([u, u], axis=0), 1, 0)
        fall_scale = (ks * live) * kout
        kf = fw[p]
        if p < NP - 1:
            gg = two(grad)
            gh, gl = gg[:, :DK], gg[:, DK:]
            ff = two(kf)
            value = (
                value
                + dot(ff, jnp.concatenate([gh, gh], axis=1), 1, 1)
                + dot(ff[:, :DK], gl, 1, 1)
            )
            fall_o[p] = fall_scale * halves(dot(v, gg, 1, 0))
            grad_o[p] = grad
            small_o[p, 3:4] = jnp.sum(grad * state_o[p], axis=0, keepdims=True) * decay
        else:
            fall_o[p] = jnp.zeros((PAIR, DK), F32)
            grad_o[p] = jnp.zeros((DV, DK), F32)
            small_o[p, 3:4] = jnp.zeros((1, DK), F32)
        value_o[p] = value
        small_o[p, 1:2] = suffix
        small_o[p, 2:3] = decay
        kout_o[p] = fall_scale * suffix
        kf_o[p] = two(kf * suffix)
        suffix = suffix * decay
        if p > 0:
            qf = rows_of(x, p, QC, DK).astype(F32) * (qs * SCALE) * qin
            update = halves(dot(u, two(qf), 0, 0))
            grad = update if p == NP - 1 else decay * grad + update


def local(live, doc, prev, pos, x):
    f = lambda *s: jax.ShapeDtypeStruct((NP,) + s, F32)
    t = f(PAIR, DK)
    return pl.pallas_call(
        local_kernel,
        out_shape=(
            t, t, t, f(PAIR, DV), t, t,
            jax.ShapeDtypeStruct((NP, PAIR, 2 * DK), BF),
            f(DV, DK), f(DV, DK), f(8, DK),
        ),
        in_specs=[sspec()] * 4 + [vspec()],
        out_specs=(vspec(),) * 10,
        scratch_shapes=[
            VMEM((NP, PAIR, 2 * DK), BF),
            VMEM((NP, PAIR, 2 * DK), BF),
            VMEM((NP, PAIR, DK), F32),
            VMEM((NP, PAIR, DK), F32),
            VMEM((NP, PAIR, DK), F32),
        ],
        compiler_params=pltpu.CompilerParams(vmem_limit_bytes=32 * 1024 * 1024),
        cost_estimate=pl.CostEstimate(flops=4 * 10**9, bytes_accessed=9 * 10**6, transcendentals=10**6),
        name="local",
    )(live, doc, prev, pos, x)


def finish_kernel(
    live_ref, pos_ref, x, own, other,
    query_i, rise_i, fall_i, value_i, qin_i, kout_i, kf_i, state_i, grad_i, small_i,
    out, qs, fs,
):
    i, j, first, _ = pair_masks()
    upper, strict = one(j >= i).astype(BF), one(j < i).astype(BF)
    sums = jnp.concatenate([upper, upper, strict, strict], axis=1)
    even = lax.rem(pos_ref[0], 2) == 0
    state = jnp.where(even, own[:DV], other[:DV])
    grad = jnp.where(even, other[:DV], own[:DV])
    rows = NB * BLOCK
    u = x[:, :, UC : UC + DV].reshape(rows, DV)
    v = x[:, :, VC : VC + DV].reshape(rows, DV)
    gg = two(grad)
    gh, gl = gg[:, :DK], gg[:, DK:]
    qs[...] = halves(dot(u, two(state), 1, 0))
    fs[...] = halves(dot(v, gg, 1, 0))
    ghh = jnp.concatenate([gh, gh], axis=1)
    both = jnp.sum(grad * state, axis=0, keepdims=True)
    live = live_ref[0]
    for p in range(NP):
        a = 2 * p
        alive = one((i + a * BLOCK) < live * BLOCK)
        at = pl.ds(p * PAIR, PAIR)
        query = query_i[p] + qin_i[p] * qs[at]
        falling = fall_i[p] + kout_i[p] * fs[at]
        rising = rise_i[p]
        kf = kf_i[p]
        value = value_i[p] + dot(kf, ghh, 1, 1) + dot(kf[:, :DK], gl, 1, 1)
        q = rows_of(x, p, QC, DK).astype(F32)
        k = rows_of(x, p, KC, DK).astype(F32)
        pre, suf, decay, base = (small_i[p, r : r + 1] for r in range(4))
        carry = base + decay * (
            pre * jnp.sum(grad_i[p] * state, axis=0, keepdims=True)
            + suf * jnp.sum(state_i[p] * grad, axis=0, keepdims=True)
            + (pre * suf) * both
        )
        terms = jnp.concatenate([*split(query * q - rising * k), *split(falling * k)], axis=0)
        gate = dot(sums, terms, 1, 0) + carry
        shape = lambda r: r.astype(BF).reshape(2, BLOCK, r.shape[1])
        out[a : a + 2, :, 0:DK] = shape(query)
        out[a : a + 2, :, DK : 2 * DK] = shape(rising + falling)
        out[a : a + 2, :, 2 * DK : 3 * DK] = shape(gate * alive)
        out[a : a + 2, :, 3 * DK :] = shape(value)


def finish(live, pos, x, own, other, parts):
    return pl.pallas_call(
        finish_kernel,
        out_shape=jax.ShapeDtypeStruct((NB, BLOCK, OUT_W), BF),
        in_specs=[sspec()] * 2 + [vspec()] * 13,
        out_specs=vspec(),
        scratch_shapes=[VMEM((NB * BLOCK, DK), F32), VMEM((NB * BLOCK, DK), F32)],
        compiler_params=pltpu.CompilerParams(vmem_limit_bytes=32 * 1024 * 1024),
        name="finish",
    )(live, pos, x, own, other, *parts)


def per_device(queries, keys, values, out_grad, log_gates, live_blocks, block_doc):
    n = lax.axis_size("ctx")
    index = lax.axis_index("ctx")
    pos = index.reshape(1)
    prev = lax.ppermute(block_doc, "ctx", [(i, (i + 1) % n) for i in range(n)])
    packed = pack(queries, keys, log_gates, values, out_grad)
    x = lax.all_to_all(packed, "head", split_axis=0, concat_axis=0, tiled=True)
    kept, sent = totals(live_blocks, block_doc, prev, pos, x)

    def beside(chip):
        y, _ = lax.optimization_barrier((x, chip))
        return local(live_blocks, block_doc, prev, pos, y)

    own, other, parts = window(kept, sent, index, beside)
    y = finish(live_blocks, pos, x, own, other, parts)
    return unpack(lax.all_to_all(y, "head", split_axis=0, concat_axis=0, tiled=True))


def solution(mesh):
    rows = P(("ctx", "head"), None)
    return jax.shard_map(
        per_device,
        mesh=mesh,
        in_specs=(rows,) * 5 + (P("ctx"), P("ctx")),
        out_specs=(rows,) * 4,
        check_vma=False,
    )
```

```python
import functools

import jax
import jax.numpy as jnp
from jax import lax
from jax.experimental import pallas as pl
from jax.experimental.pallas import tpu as pltpu
from jax.sharding import PartitionSpec as P

DK = 128
DV = 256
BLOCK = 64
HEADS = 16
NB = 16
IN_W = 3 * DK + 2 * DV
OUT_W = 3 * DK + DV
QC, KC, GC, VC, UC = 0, DK, 2 * DK, 3 * DK, 3 * DK + DV
MSG = DV + 8
SCALE = DK ** (-0.5)
BF = jnp.bfloat16
F32 = jnp.float32
VMEM = pltpu.VMEM


def vspec():
    return pl.BlockSpec(memory_space=VMEM)


def split(x):
    hi = x.astype(BF)
    lo = (x - hi.astype(F32)).astype(BF)
    return hi, lo


def dot(a, b, ca, cb):
    return lax.dot_general(a, b, (((ca,), (cb,)), ((), ())), preferred_element_type=F32)


def halves(r):
    return r[:, :DK] + r[:, DK:]


def flag_rows(live_blocks, block_doc, index):
    n = lax.axis_size("ctx")
    before = lax.ppermute(block_doc, "ctx", [(i, (i + 1) % n) for i in range(n)])
    place = jnp.arange(NB)
    live = place < live_blocks[0]
    previous = jnp.concatenate([before[NB - 1 :], block_doc[: NB - 1]])
    keep = (previous == block_doc) & ((place > 0) | (index > 0))
    even = jnp.full((8,), index % 2 == 0)
    rows = jnp.concatenate([live, keep, even]).astype(F32)
    return jnp.broadcast_to(rows[:, None], (2 * NB + 8, DV))


def flags(flag):
    row = lambda r: flag[r : r + 1, :DK]
    lives, keeps = [row(b) for b in range(NB)], [row(NB + b) for b in range(NB)]
    return lives, keeps, row(2 * NB) > 0.0


PACK_STEPS = 2
PER = HEADS // PACK_STEPS


def pack_kernel(q, k, g, v, u, out):
    for h in range(PER):
        kc = slice(h * DK, (h + 1) * DK)
        vc = slice(h * DV, (h + 1) * DV)
        out[h, :, QC : QC + DK] = q[:, kc]
        out[h, :, KC : KC + DK] = k[:, kc]
        out[h, :, GC : GC + DK] = g[:, kc]
        out[h, :, VC : VC + DV] = v[:, vc]
        out[h, :, UC : UC + DV] = u[:, vc]


def pack(q, k, g, v, u):
    narrow = pl.BlockSpec((BLOCK, PER * DK), lambda i: (0, i))
    wide = pl.BlockSpec((BLOCK, PER * DV), lambda i: (0, i))
    return pl.pallas_call(
        pack_kernel,
        grid=(PACK_STEPS,),
        out_shape=jax.ShapeDtypeStruct((HEADS, BLOCK, IN_W), BF),
        in_specs=[narrow] * 3 + [wide] * 2,
        out_specs=pl.BlockSpec((PER, BLOCK, IN_W), lambda i: (i, 0, 0)),
        name="pack",
    )(q, k, g, v, u)


def unpack_kernel(x, dq, dk, dv, dg):
    for h in range(HEADS):
        kc = slice(h * DK, (h + 1) * DK)
        vc = slice(h * DV, (h + 1) * DV)
        dq[:, kc] = x[h, :, 0:DK]
        dk[:, kc] = x[h, :, DK : 2 * DK]
        dg[:, kc] = x[h, :, 2 * DK : 3 * DK]
        dv[:, vc] = x[h, :, 3 * DK :]


def unpack(x):
    narrow = jax.ShapeDtypeStruct((BLOCK, HEADS * DK), BF)
    wide = jax.ShapeDtypeStruct((BLOCK, HEADS * DV), BF)
    return pl.pallas_call(
        unpack_kernel,
        out_shape=(narrow, narrow, wide, narrow),
        in_specs=[vspec()],
        out_specs=(vspec(),) * 4,
        compiler_params=pltpu.CompilerParams(vmem_limit_bytes=16 * 1024 * 1024),
        name="unpack",
    )(x)


PAIR = 2 * BLOCK
NP = NB // 2


def rows_of(x, p, col, width):
    return x[2 * p : 2 * p + 2, :, col : col + width].reshape(PAIR, width)


def two(x):
    return jnp.concatenate(split(x), axis=1)


def one(mask):
    return jnp.where(mask, 1.0, 0.0).astype(F32)


def pair_masks():
    i = lax.broadcasted_iota(jnp.int32, (PAIR, PAIR), 0)
    j = lax.broadcasted_iota(jnp.int32, (PAIR, PAIR), 1)
    first = i < BLOCK
    return i, j, first, first == (j < BLOCK)


def totals_kernel(flag, x, kept, sent, kw, qw, cs):
    lives, keeps, even = flags(flag)
    i, j, first, same = pair_masks()
    tri = one((j <= i) & same).astype(BF)
    decay = jnp.ones((1, DK), F32)
    for p in range(NP):
        a, b = 2 * p, 2 * p + 1
        c = dot(tri, rows_of(x, p, GC, DK), 1, 0) * jnp.where(first, lives[a], lives[b])
        cs[p] = c
        earlier = decay * keeps[a]
        middle = earlier * (keeps[b] * jnp.exp(c[BLOCK - 1 : BLOCK]))
        decay = middle * jnp.exp(c[PAIR - 1 : PAIR])
        q = rows_of(x, p, QC, DK).astype(F32)
        scale = jnp.where(first, earlier * (lives[a] * SCALE), middle * (lives[b] * SCALE))
        qw[p] = two(q * (jnp.exp(c) * scale))
    rows = NB * BLOCK
    u = x[:, :, UC : UC + DV].reshape(rows, DV)
    bwd = halves(dot(u, qw[...].reshape(rows, 2 * DK), 0, 0))
    later = jnp.ones((1, DK), F32)
    for p in reversed(range(NP)):
        a, b = 2 * p, 2 * p + 1
        c = cs[p]
        ca, cb = c[BLOCK - 1 : BLOCK], c[PAIR - 1 : PAIR]
        middle = later * (keeps[b] * jnp.exp(cb))
        k = rows_of(x, p, KC, DK).astype(F32)
        fade = jnp.exp(jnp.where(first, ca, cb) - c)
        kw[p] = two(k * (fade * jnp.where(first, middle * lives[a], later * lives[b])))
        later = middle * (keeps[a] * jnp.exp(ca))
    v = x[:, :, VC : VC + DV].reshape(rows, DV)
    fwd = halves(dot(v, kw[...].reshape(rows, 2 * DK), 0, 0))
    kept[:DV] = jnp.where(even, fwd, bwd)
    sent[:DV] = jnp.where(even, bwd, fwd)
    kept[DV:] = jnp.broadcast_to(decay, (MSG - DV, DK))
    sent[DV:] = jnp.broadcast_to(decay, (MSG - DV, DK))


def totals(flag, x):
    msg = jax.ShapeDtypeStruct((MSG, DK), F32)
    return pl.pallas_call(
        totals_kernel,
        out_shape=(msg, msg),
        in_specs=[vspec()] * 2,
        out_specs=(vspec(),) * 2,
        scratch_shapes=[
            VMEM((NP, PAIR, 2 * DK), BF),
            VMEM((NP, PAIR, 2 * DK), BF),
            VMEM((NP, PAIR, DK), F32),
        ],
        compiler_params=pltpu.CompilerParams(vmem_limit_bytes=32 * 1024 * 1024),
        name="totals",
    )(flag, x)


def joined(near, far):
    return jnp.concatenate(
        [near[DV : DV + 1] * far[:DV] + near[:DV], near[DV:] * far[DV:]], axis=0
    )


def swapped(x):
    n = lax.axis_size("ctx")
    return lax.ppermute(x, "ctx", [(i, i ^ 1) for i in range(n)])


def upstream(x, index, by):
    n = lax.axis_size("ctx")
    moved = lax.ppermute(
        x, "ctx", [(i, (i + (2 * by if i % 2 == 0 else -2 * by)) % n) for i in range(n)]
    )
    source = jnp.where(index % 2 == 0, index - 2 * by, index + 2 * by)
    return jnp.where((source >= 0) & (source < n), moved, 0.0)


def window(kept, sent, index, beside):
    other = swapped(sent)
    chip = joined(other, kept)
    near, far = upstream(chip, index, 1), upstream(chip, index, 2)
    done = beside(chip)
    near, far, done = lax.optimization_barrier((near, far, done))
    e = joined(near, far)
    e = joined(e, upstream(e, index, 2))
    return e, swapped(joined(kept, e)), done


def local_kernel(
    flag, x,
    query_o, rise_o, fall_o, value_o, qin_o, kout_o, kf_o, state_o, grad_o, small_o,
    qw, kw, fw, qsw, ksw,
):
    lives, keeps, _ = flags(flag)
    i, j, first, same = pair_masks()
    cross = jnp.logical_not(same)
    tri = one((j <= i) & same).astype(BF)
    low_same, low_cross = one((j <= i) & same), one((j < i) & cross)
    up_same, up_cross = one((j >= i) & same), one((j > i) & cross)
    first_v = lax.broadcasted_iota(jnp.int32, (PAIR, DV), 0) < BLOCK
    wide = [flag[b : b + 1, :].astype(BF) for b in range(NB)]

    ends = []
    prefix = jnp.ones((1, DK), F32)
    for p in range(NP):
        a, b = 2 * p, 2 * p + 1
        live = jnp.where(first, lives[a], lives[b])
        c = dot(tri, rows_of(x, p, GC, DK), 1, 0) * live
        ca, cb = c[BLOCK - 1 : BLOCK], c[PAIR - 1 : PAIR]
        d = jnp.where(first, c - ca, c)
        qs, ks = jnp.exp(d), jnp.exp(-d)
        ea, eb = keeps[a] * jnp.exp(ca), jnp.exp(cb)
        decay = ea * (keeps[b] * eb)
        ends.append((ea, eb, decay))
        q = rows_of(x, p, QC, DK).astype(F32) * (qs * SCALE)
        k = rows_of(x, p, KC, DK).astype(F32) * (ks * live)
        kf = k * jnp.where(first, keeps[b] * eb, eb)
        qsw[p], ksw[p] = qs, ks
        qw[p], kw[p] = two(q), two(k)
        fw[p] = kf
        small_o[p, 0:1] = prefix
        qin_o[p] = (qs * (live * SCALE)) * (jnp.where(first, ea, ea * keeps[b]) * prefix)
        prefix = prefix * decay
        if p == 0:
            state_o[p] = jnp.zeros((DV, DK), F32)
        else:
            state_o[p] = state
        if p < NP - 1:
            update = halves(dot(rows_of(x, p, VC, DV), two(kf), 0, 0))
            state = update if p == 0 else decay * state + update

    suffix = jnp.ones((1, DK), F32)
    for p in reversed(range(NP)):
        a, b = 2 * p, 2 * p + 1
        ea, eb, decay = ends[p]
        live = jnp.where(first, lives[a], lives[b])
        qin = jnp.where(first, ea, ea * keeps[b])
        kout = jnp.where(first, keeps[b] * eb, eb)
        qq, kk = qw[p], kw[p]
        qh, ql, kh = qq[:, :DK], qq[:, DK:], kk[:, :DK]
        qs, ks = qsw[p], ksw[p]
        v = rows_of(x, p, VC, DV)
        u = rows_of(x, p, UC, DV) * jnp.where(first_v, wide[a], wide[b])
        st = dot(kk, jnp.concatenate([qh, qh], axis=1), 1, 1) + dot(kh, ql, 1, 1)
        up = up_same + keeps[b] * up_cross
        st = jnp.where(up > 0.0, st, 0.0)
        dst = dot(v, u, 1, 1) * up
        ds = dot(u, v, 1, 1) * (low_same + keeps[b] * low_cross)
        dh, dl = split(ds)
        th, tl = split(dst)
        query = halves(dot(dh, kk, 1, 0)) + dot(dl, kh, 1, 0)
        if p > 0:
            query = query + qin * halves(dot(u, two(state_o[p]), 1, 0))
        query_o[p] = query * (qs * SCALE)
        rise_o[p] = ks * live * (halves(dot(th, qq, 1, 0)) + dot(tl, qh, 1, 0))
        value = dot(two(st), jnp.concatenate([u, u], axis=0), 1, 0)
        fall_scale = (ks * live) * kout
        kf = fw[p]
        if p < NP - 1:
            gg = two(grad)
            gh, gl = gg[:, :DK], gg[:, DK:]
            ff = two(kf)
            value = (
                value
                + dot(ff, jnp.concatenate([gh, gh], axis=1), 1, 1)
                + dot(ff[:, :DK], gl, 1, 1)
            )
            fall_o[p] = fall_scale * halves(dot(v, gg, 1, 0))
            grad_o[p] = grad
            small_o[p, 3:4] = jnp.sum(grad * state_o[p], axis=0, keepdims=True) * decay
        else:
            fall_o[p] = jnp.zeros((PAIR, DK), F32)
            grad_o[p] = jnp.zeros((DV, DK), F32)
            small_o[p, 3:4] = jnp.zeros((1, DK), F32)
        value_o[p] = value
        small_o[p, 1:2] = suffix
        small_o[p, 2:3] = decay
        kout_o[p] = fall_scale * suffix
        kf_o[p] = two(kf * suffix)
        suffix = suffix * decay
        if p > 0:
            qf = rows_of(x, p, QC, DK).astype(F32) * (qs * SCALE) * qin
            update = halves(dot(u, two(qf), 0, 0))
            grad = update if p == NP - 1 else decay * grad + update


def local(flag, x):
    f = lambda *s: jax.ShapeDtypeStruct((NP,) + s, F32)
    t = f(PAIR, DK)
    return pl.pallas_call(
        local_kernel,
        out_shape=(
            t, t, t, f(PAIR, DV), t, t,
            jax.ShapeDtypeStruct((NP, PAIR, 2 * DK), BF),
            f(DV, DK), f(DV, DK), f(8, DK),
        ),
        in_specs=[vspec()] * 2,
        out_specs=(vspec(),) * 10,
        scratch_shapes=[
            VMEM((NP, PAIR, 2 * DK), BF),
            VMEM((NP, PAIR, 2 * DK), BF),
            VMEM((NP, PAIR, DK), F32),
            VMEM((NP, PAIR, DK), F32),
            VMEM((NP, PAIR, DK), F32),
        ],
        compiler_params=pltpu.CompilerParams(vmem_limit_bytes=32 * 1024 * 1024),
        cost_estimate=pl.CostEstimate(flops=4 * 10**9, bytes_accessed=9 * 10**6, transcendentals=10**6),
        name="local",
    )(flag, x)


def finish_kernel(
    flag, x, own, other,
    query_i, rise_i, fall_i, value_i, qin_i, kout_i, kf_i, state_i, grad_i, small_i,
    out, qs, fs,
):
    i, j, first, _ = pair_masks()
    upper, strict = one(j >= i).astype(BF), one(j < i).astype(BF)
    sums = jnp.concatenate([upper, upper, strict, strict], axis=1)
    lives, _, even = flags(flag)
    state = jnp.where(even, own[:DV], other[:DV])
    grad = jnp.where(even, other[:DV], own[:DV])
    rows = NB * BLOCK
    u = x[:, :, UC : UC + DV].reshape(rows, DV)
    v = x[:, :, VC : VC + DV].reshape(rows, DV)
    gg = two(grad)
    gh, gl = gg[:, :DK], gg[:, DK:]
    qs[...] = halves(dot(u, two(state), 1, 0))
    fs[...] = halves(dot(v, gg, 1, 0))
    ghh = jnp.concatenate([gh, gh], axis=1)
    both = jnp.sum(grad * state, axis=0, keepdims=True)
    for p in range(NP):
        a = 2 * p
        alive = jnp.where(first, lives[a], lives[a + 1])
        at = pl.ds(p * PAIR, PAIR)
        query = query_i[p] + qin_i[p] * qs[at]
        falling = fall_i[p] + kout_i[p] * fs[at]
        rising = rise_i[p]
        kf = kf_i[p]
        value = value_i[p] + dot(kf, ghh, 1, 1) + dot(kf[:, :DK], gl, 1, 1)
        q = rows_of(x, p, QC, DK).astype(F32)
        k = rows_of(x, p, KC, DK).astype(F32)
        pre, suf, decay, base = (small_i[p, r : r + 1] for r in range(4))
        carry = base + decay * (
            pre * jnp.sum(grad_i[p] * state, axis=0, keepdims=True)
            + suf * jnp.sum(state_i[p] * grad, axis=0, keepdims=True)
            + (pre * suf) * both
        )
        terms = jnp.concatenate([*split(query * q - rising * k), *split(falling * k)], axis=0)
        gate = dot(sums, terms, 1, 0) + carry
        shape = lambda r: r.astype(BF).reshape(2, BLOCK, r.shape[1])
        out[a : a + 2, :, 0:DK] = shape(query)
        out[a : a + 2, :, DK : 2 * DK] = shape(rising + falling)
        out[a : a + 2, :, 2 * DK : 3 * DK] = shape(gate * alive)
        out[a : a + 2, :, 3 * DK :] = shape(value)


def finish(flag, x, own, other, parts):
    return pl.pallas_call(
        finish_kernel,
        out_shape=jax.ShapeDtypeStruct((NB, BLOCK, OUT_W), BF),
        in_specs=[vspec()] * 14,
        out_specs=vspec(),
        scratch_shapes=[VMEM((NB * BLOCK, DK), F32), VMEM((NB * BLOCK, DK), F32)],
        compiler_params=pltpu.CompilerParams(vmem_limit_bytes=32 * 1024 * 1024),
        name="finish",
    )(flag, x, own, other, *parts)


def per_device(queries, keys, values, out_grad, log_gates, live_blocks, block_doc):
    index = lax.axis_index("ctx")
    flag = flag_rows(live_blocks, block_doc, index)
    packed = pack(queries, keys, log_gates, values, out_grad)
    x = lax.all_to_all(packed, "head", split_axis=0, concat_axis=0, tiled=True)
    kept, sent = totals(flag, x)

    def beside(chip):
        y, _ = lax.optimization_barrier((x, chip))
        return local(flag, y)

    own, other, parts = window(kept, sent, index, beside)
    y = finish(flag, x, own, other, parts)
    return unpack(lax.all_to_all(y, "head", split_axis=0, concat_axis=0, tiled=True))


def solution(mesh):
    rows = P(("ctx", "head"), None)
    return jax.shard_map(
        per_device,
        mesh=mesh,
        in_specs=(rows,) * 5 + (P("ctx"), P("ctx")),
        out_specs=(rows,) * 4,
        check_vma=False,
    )
```

```python
import functools

import jax
import jax.numpy as jnp
from jax import lax
from jax.experimental import pallas as pl
from jax.experimental.pallas import tpu as pltpu
from jax.sharding import PartitionSpec as P

DK = 128
DV = 256
BLOCK = 64
HEADS = 16
NB = 16
IN_W = 3 * DK + 2 * DV
OUT_W = 3 * DK + DV
QC, KC, GC, VC, UC = 0, DK, 2 * DK, 3 * DK, 3 * DK + DV
MSG = DV + 8
SCALE = DK ** (-0.5)
BF = jnp.bfloat16
F32 = jnp.float32
VMEM = pltpu.VMEM


def vspec():
    return pl.BlockSpec(memory_space=VMEM)


def split(x):
    hi = x.astype(BF)
    lo = (x - hi.astype(F32)).astype(BF)
    return hi, lo


def dot(a, b, ca, cb):
    return lax.dot_general(a, b, (((ca,), (cb,)), ((), ())), preferred_element_type=F32)


def halves(r):
    return r[:, :DK] + r[:, DK:]


def flag_rows(live_blocks, block_doc, index):
    n = lax.axis_size("ctx")
    before = lax.ppermute(block_doc, "ctx", [(i, (i + 1) % n) for i in range(n)])
    place = jnp.arange(NB)
    live = place < live_blocks[0]
    previous = jnp.concatenate([before[NB - 1 :], block_doc[: NB - 1]])
    keep = (previous == block_doc) & ((place > 0) | (index > 0))
    even = jnp.full((8,), index % 2 == 0)
    rows = jnp.concatenate([live, keep, even]).astype(F32)
    return jnp.broadcast_to(rows[:, None], (2 * NB + 8, DV))


def flags(flag):
    row = lambda r: flag[r : r + 1, :DK]
    lives, keeps = [row(b) for b in range(NB)], [row(NB + b) for b in range(NB)]
    return lives, keeps, row(2 * NB) > 0.0


PACK_STEPS = 2
PER = HEADS // PACK_STEPS


def pack_kernel(q, k, g, v, u, out):
    for h in range(PER):
        kc = slice(h * DK, (h + 1) * DK)
        vc = slice(h * DV, (h + 1) * DV)
        out[h, :, QC : QC + DK] = q[:, kc]
        out[h, :, KC : KC + DK] = k[:, kc]
        out[h, :, GC : GC + DK] = g[:, kc]
        out[h, :, VC : VC + DV] = v[:, vc]
        out[h, :, UC : UC + DV] = u[:, vc]


def pack(q, k, g, v, u):
    narrow = pl.BlockSpec((BLOCK, PER * DK), lambda i: (0, i))
    wide = pl.BlockSpec((BLOCK, PER * DV), lambda i: (0, i))
    return pl.pallas_call(
        pack_kernel,
        grid=(PACK_STEPS,),
        out_shape=jax.ShapeDtypeStruct((HEADS, BLOCK, IN_W), BF),
        in_specs=[narrow] * 3 + [wide] * 2,
        out_specs=pl.BlockSpec((PER, BLOCK, IN_W), lambda i: (i, 0, 0)),
        name="pack",
    )(q, k, g, v, u)


def unpack_kernel(x, dq, dk, dv, dg):
    for h in range(HEADS):
        kc = slice(h * DK, (h + 1) * DK)
        vc = slice(h * DV, (h + 1) * DV)
        dq[:, kc] = x[h, :, 0:DK]
        dk[:, kc] = x[h, :, DK : 2 * DK]
        dg[:, kc] = x[h, :, 2 * DK : 3 * DK]
        dv[:, vc] = x[h, :, 3 * DK :]


def unpack(x):
    narrow = jax.ShapeDtypeStruct((BLOCK, HEADS * DK), BF)
    wide = jax.ShapeDtypeStruct((BLOCK, HEADS * DV), BF)
    return pl.pallas_call(
        unpack_kernel,
        out_shape=(narrow, narrow, wide, narrow),
        in_specs=[vspec()],
        out_specs=(vspec(),) * 4,
        compiler_params=pltpu.CompilerParams(vmem_limit_bytes=16 * 1024 * 1024),
        name="unpack",
    )(x)


PAIR = 2 * BLOCK
NP = NB // 2


def rows_of(x, p, col, width):
    return x[2 * p : 2 * p + 2, :, col : col + width].reshape(PAIR, width)


def two(x):
    return jnp.concatenate(split(x), axis=1)


def one(mask):
    return jnp.where(mask, 1.0, 0.0).astype(F32)


def pair_masks():
    i = lax.broadcasted_iota(jnp.int32, (PAIR, PAIR), 0)
    j = lax.broadcasted_iota(jnp.int32, (PAIR, PAIR), 1)
    first = i < BLOCK
    return i, j, first, first == (j < BLOCK)


def totals_kernel(flag, x, kept, sent, kw, qw, cs):
    lives, keeps, even = flags(flag)
    i, j, first, same = pair_masks()
    tri = one((j <= i) & same).astype(BF)
    decay = jnp.ones((1, DK), F32)
    for p in range(NP):
        a, b = 2 * p, 2 * p + 1
        c = dot(tri, rows_of(x, p, GC, DK), 1, 0) * jnp.where(first, lives[a], lives[b])
        cs[p] = c
        earlier = decay * keeps[a]
        middle = earlier * (keeps[b] * jnp.exp(c[BLOCK - 1 : BLOCK]))
        decay = middle * jnp.exp(c[PAIR - 1 : PAIR])
        q = rows_of(x, p, QC, DK).astype(F32)
        scale = jnp.where(first, earlier * (lives[a] * SCALE), middle * (lives[b] * SCALE))
        qw[p] = two(q * (jnp.exp(c) * scale))
    rows = NB * BLOCK
    u = x[:, :, UC : UC + DV].reshape(rows, DV)
    bwd = halves(dot(u, qw[...].reshape(rows, 2 * DK), 0, 0))
    later = jnp.ones((1, DK), F32)
    for p in reversed(range(NP)):
        a, b = 2 * p, 2 * p + 1
        c = cs[p]
        ca, cb = c[BLOCK - 1 : BLOCK], c[PAIR - 1 : PAIR]
        middle = later * (keeps[b] * jnp.exp(cb))
        k = rows_of(x, p, KC, DK).astype(F32)
        fade = jnp.exp(jnp.where(first, ca, cb) - c)
        kw[p] = two(k * (fade * jnp.where(first, middle * lives[a], later * lives[b])))
        later = middle * (keeps[a] * jnp.exp(ca))
    v = x[:, :, VC : VC + DV].reshape(rows, DV)
    fwd = halves(dot(v, kw[...].reshape(rows, 2 * DK), 0, 0))
    kept[:DV] = jnp.where(even, fwd, bwd)
    sent[:DV] = jnp.where(even, bwd, fwd)
    kept[DV:] = jnp.broadcast_to(decay, (MSG - DV, DK))
    sent[DV:] = jnp.broadcast_to(decay, (MSG - DV, DK))


def totals(flag, x):
    msg = jax.ShapeDtypeStruct((MSG, DK), F32)
    return pl.pallas_call(
        totals_kernel,
        out_shape=(msg, msg),
        in_specs=[vspec()] * 2,
        out_specs=(vspec(),) * 2,
        scratch_shapes=[
            VMEM((NP, PAIR, 2 * DK), BF),
            VMEM((NP, PAIR, 2 * DK), BF),
            VMEM((NP, PAIR, DK), F32),
        ],
        compiler_params=pltpu.CompilerParams(vmem_limit_bytes=32 * 1024 * 1024),
        name="totals",
    )(flag, x)


def joined(near, far):
    return jnp.concatenate(
        [near[DV : DV + 1] * far[:DV] + near[:DV], near[DV:] * far[DV:]], axis=0
    )


def swapped(x):
    n = lax.axis_size("ctx")
    return lax.ppermute(x, "ctx", [(i, i ^ 1) for i in range(n)])


def upstream(x, index, by):
    n = lax.axis_size("ctx")
    target = lambda i: i + (2 * by if i % 2 == 0 else -2 * by)
    pairs = [(i, target(i) if 0 <= target(i) < n else i ^ 1) for i in range(n)]
    moved = lax.ppermute(x, "ctx", pairs)
    source = jnp.where(index % 2 == 0, index - 2 * by, index + 2 * by)
    return jnp.where((source >= 0) & (source < n), moved, 0.0)


def window(kept, sent, index, beside):
    other = swapped(sent)
    chip = joined(other, kept)
    near, far = upstream(chip, index, 1), upstream(chip, index, 2)
    done = beside(chip)
    near, far, done = lax.optimization_barrier((near, far, done))
    e = joined(near, far)
    e = joined(e, upstream(e, index, 2))
    return e, swapped(joined(kept, e)), done


def local_kernel(
    flag, x,
    query_o, rise_o, fall_o, value_o, qin_o, kout_o, kf_o, state_o, grad_o, small_o,
    qw, kw, fw, qsw, ksw,
):
    lives, keeps, _ = flags(flag)
    i, j, first, same = pair_masks()
    cross = jnp.logical_not(same)
    tri = one((j <= i) & same).astype(BF)
    low_same, low_cross = one((j <= i) & same), one((j < i) & cross)
    up_same, up_cross = one((j >= i) & same), one((j > i) & cross)
    first_v = lax.broadcasted_iota(jnp.int32, (PAIR, DV), 0) < BLOCK
    wide = [flag[b : b + 1, :].astype(BF) for b in range(NB)]

    ends = []
    prefix = jnp.ones((1, DK), F32)
    for p in range(NP):
        a, b = 2 * p, 2 * p + 1
        live = jnp.where(first, lives[a], lives[b])
        c = dot(tri, rows_of(x, p, GC, DK), 1, 0) * live
        ca, cb = c[BLOCK - 1 : BLOCK], c[PAIR - 1 : PAIR]
        d = jnp.where(first, c - ca, c)
        qs, ks = jnp.exp(d), jnp.exp(-d)
        ea, eb = keeps[a] * jnp.exp(ca), jnp.exp(cb)
        decay = ea * (keeps[b] * eb)
        ends.append((ea, eb, decay))
        q = rows_of(x, p, QC, DK).astype(F32) * (qs * SCALE)
        k = rows_of(x, p, KC, DK).astype(F32) * (ks * live)
        kf = k * jnp.where(first, keeps[b] * eb, eb)
        qsw[p], ksw[p] = qs, ks
        qw[p], kw[p] = two(q), two(k)
        fw[p] = kf
        small_o[p, 0:1] = prefix
        qin_o[p] = (qs * (live * SCALE)) * (jnp.where(first, ea, ea * keeps[b]) * prefix)
        prefix = prefix * decay
        if p == 0:
            state_o[p] = jnp.zeros((DV, DK), F32)
        else:
            state_o[p] = state
        if p < NP - 1:
            update = halves(dot(rows_of(x, p, VC, DV), two(kf), 0, 0))
            state = update if p == 0 else decay * state + update

    suffix = jnp.ones((1, DK), F32)
    for p in reversed(range(NP)):
        a, b = 2 * p, 2 * p + 1
        ea, eb, decay = ends[p]
        live = jnp.where(first, lives[a], lives[b])
        qin = jnp.where(first, ea, ea * keeps[b])
        kout = jnp.where(first, keeps[b] * eb, eb)
        qq, kk = qw[p], kw[p]
        qh, ql, kh = qq[:, :DK], qq[:, DK:], kk[:, :DK]
        qs, ks = qsw[p], ksw[p]
        v = rows_of(x, p, VC, DV)
        u = rows_of(x, p, UC, DV) * jnp.where(first_v, wide[a], wide[b])
        st = dot(kk, jnp.concatenate([qh, qh], axis=1), 1, 1) + dot(kh, ql, 1, 1)
        up = up_same + keeps[b] * up_cross
        st = jnp.where(up > 0.0, st, 0.0)
        dst = dot(v, u, 1, 1) * up
        ds = dot(u, v, 1, 1) * (low_same + keeps[b] * low_cross)
        dh, dl = split(ds)
        th, tl = split(dst)
        query = halves(dot(dh, kk, 1, 0)) + dot(dl, kh, 1, 0)
        if p > 0:
            query = query + qin * halves(dot(u, two(state_o[p]), 1, 0))
        query_o[p] = query * (qs * SCALE)
        rise_o[p] = ks * live * (halves(dot(th, qq, 1, 0)) + dot(tl, qh, 1, 0))
        value = dot(two(st), jnp.concatenate([u, u], axis=0), 1, 0)
        fall_scale = (ks * live) * kout
        kf = fw[p]
        if p < NP - 1:
            gg = two(grad)
            gh, gl = gg[:, :DK], gg[:, DK:]
            ff = two(kf)
            value = (
                value
                + dot(ff, jnp.concatenate([gh, gh], axis=1), 1, 1)
                + dot(ff[:, :DK], gl, 1, 1)
            )
            fall_o[p] = fall_scale * halves(dot(v, gg, 1, 0))
            grad_o[p] = grad
            small_o[p, 3:4] = jnp.sum(grad * state_o[p], axis=0, keepdims=True) * decay
        else:
            fall_o[p] = jnp.zeros((PAIR, DK), F32)
            grad_o[p] = jnp.zeros((DV, DK), F32)
            small_o[p, 3:4] = jnp.zeros((1, DK), F32)
        value_o[p] = value
        small_o[p, 1:2] = suffix
        small_o[p, 2:3] = decay
        kout_o[p] = fall_scale * suffix
        kf_o[p] = two(kf * suffix)
        suffix = suffix * decay
        if p > 0:
            qf = rows_of(x, p, QC, DK).astype(F32) * (qs * SCALE) * qin
            update = halves(dot(u, two(qf), 0, 0))
            grad = update if p == NP - 1 else decay * grad + update


def local(flag, x):
    f = lambda *s: jax.ShapeDtypeStruct((NP,) + s, F32)
    t = f(PAIR, DK)
    return pl.pallas_call(
        local_kernel,
        out_shape=(
            t, t, t, f(PAIR, DV), t, t,
            jax.ShapeDtypeStruct((NP, PAIR, 2 * DK), BF),
            f(DV, DK), f(DV, DK), f(8, DK),
        ),
        in_specs=[vspec()] * 2,
        out_specs=(vspec(),) * 10,
        scratch_shapes=[
            VMEM((NP, PAIR, 2 * DK), BF),
            VMEM((NP, PAIR, 2 * DK), BF),
            VMEM((NP, PAIR, DK), F32),
            VMEM((NP, PAIR, DK), F32),
            VMEM((NP, PAIR, DK), F32),
        ],
        compiler_params=pltpu.CompilerParams(vmem_limit_bytes=32 * 1024 * 1024),
        cost_estimate=pl.CostEstimate(flops=4 * 10**9, bytes_accessed=9 * 10**6, transcendentals=10**6),
        name="local",
    )(flag, x)


def finish_kernel(
    flag, x, own, other,
    query_i, rise_i, fall_i, value_i, qin_i, kout_i, kf_i, state_i, grad_i, small_i,
    out, qs, fs,
):
    i, j, first, _ = pair_masks()
    upper, strict = one(j >= i).astype(BF), one(j < i).astype(BF)
    sums = jnp.concatenate([upper, upper, strict, strict], axis=1)
    lives, _, even = flags(flag)
    state = jnp.where(even, own[:DV], other[:DV])
    grad = jnp.where(even, other[:DV], own[:DV])
    rows = NB * BLOCK
    u = x[:, :, UC : UC + DV].reshape(rows, DV)
    v = x[:, :, VC : VC + DV].reshape(rows, DV)
    gg = two(grad)
    gh, gl = gg[:, :DK], gg[:, DK:]
    qs[...] = halves(dot(u, two(state), 1, 0))
    fs[...] = halves(dot(v, gg, 1, 0))
    ghh = jnp.concatenate([gh, gh], axis=1)
    both = jnp.sum(grad * state, axis=0, keepdims=True)
    for p in range(NP):
        a = 2 * p
        alive = jnp.where(first, lives[a], lives[a + 1])
        at = pl.ds(p * PAIR, PAIR)
        query = query_i[p] + qin_i[p] * qs[at]
        falling = fall_i[p] + kout_i[p] * fs[at]
        rising = rise_i[p]
        kf = kf_i[p]
        value = value_i[p] + dot(kf, ghh, 1, 1) + dot(kf[:, :DK], gl, 1, 1)
        q = rows_of(x, p, QC, DK).astype(F32)
        k = rows_of(x, p, KC, DK).astype(F32)
        pre, suf, decay, base = (small_i[p, r : r + 1] for r in range(4))
        carry = base + decay * (
            pre * jnp.sum(grad_i[p] * state, axis=0, keepdims=True)
            + suf * jnp.sum(state_i[p] * grad, axis=0, keepdims=True)
            + (pre * suf) * both
        )
        terms = jnp.concatenate([*split(query * q - rising * k), *split(falling * k)], axis=0)
        gate = dot(sums, terms, 1, 0) + carry
        shape = lambda r: r.astype(BF).reshape(2, BLOCK, r.shape[1])
        out[a : a + 2, :, 0:DK] = shape(query)
        out[a : a + 2, :, DK : 2 * DK] = shape(rising + falling)
        out[a : a + 2, :, 2 * DK : 3 * DK] = shape(gate * alive)
        out[a : a + 2, :, 3 * DK :] = shape(value)


def finish(flag, x, own, other, parts):
    return pl.pallas_call(
        finish_kernel,
        out_shape=jax.ShapeDtypeStruct((NB, BLOCK, OUT_W), BF),
        in_specs=[vspec()] * 14,
        out_specs=vspec(),
        scratch_shapes=[VMEM((NB * BLOCK, DK), F32), VMEM((NB * BLOCK, DK), F32)],
        compiler_params=pltpu.CompilerParams(vmem_limit_bytes=32 * 1024 * 1024),
        name="finish",
    )(flag, x, own, other, *parts)


def per_device(queries, keys, values, out_grad, log_gates, live_blocks, block_doc):
    index = lax.axis_index("ctx")
    flag = flag_rows(live_blocks, block_doc, index)
    packed = pack(queries, keys, log_gates, values, out_grad)
    x = lax.all_to_all(packed, "head", split_axis=0, concat_axis=0, tiled=True)
    kept, sent = totals(flag, x)

    def beside(chip):
        y, _ = lax.optimization_barrier((x, chip))
        return local(flag, y)

    own, other, parts = window(kept, sent, index, beside)
    y = finish(flag, x, own, other, parts)
    return unpack(lax.all_to_all(y, "head", split_axis=0, concat_axis=0, tiled=True))


def solution(mesh):
    rows = P(("ctx", "head"), None)
    return jax.shard_map(
        per_device,
        mesh=mesh,
        in_specs=(rows,) * 5 + (P("ctx"), P("ctx")),
        out_specs=(rows,) * 4,
        check_vma=False,
    )
```

```python
import functools

import jax
import jax.numpy as jnp
from jax import lax
from jax.experimental import pallas as pl
from jax.experimental.pallas import tpu as pltpu
from jax.sharding import PartitionSpec as P

DK = 128
DV = 256
BLOCK = 64
HEADS = 16
NB = 16
IN_W = 3 * DK + 2 * DV
OUT_W = 3 * DK + DV
QC, KC, GC, VC, UC = 0, DK, 2 * DK, 3 * DK, 3 * DK + DV
MSG = DV + 8
SCALE = DK ** (-0.5)
BF = jnp.bfloat16
F32 = jnp.float32
VMEM = pltpu.VMEM


def vspec():
    return pl.BlockSpec(memory_space=VMEM)


def split(x):
    hi = x.astype(BF)
    lo = (x - hi.astype(F32)).astype(BF)
    return hi, lo


def dot(a, b, ca, cb):
    return lax.dot_general(a, b, (((ca,), (cb,)), ((), ())), preferred_element_type=F32)


def halves(r):
    return r[:, :DK] + r[:, DK:]


EVEN, INSIDE, HEAD_ID, TAIL_ID, FLAG_ROWS = 2 * NB, 2 * NB + 1, 2 * NB + 3, 2 * NB + 4, 2 * NB + 8


def flags(flag):
    row = lambda r: flag[r : r + 1, :DK]
    lives, keeps = [row(b) for b in range(NB)], [row(NB + b) for b in range(NB)]
    return lives, keeps, row(EVEN) > 0.0


SPLIT = 2


def pack_kernel(
    owners, live_h, doc_h, q, k, g, v, u, out, flag, qv, kv, gv, vv, uv, live, doc, sem, small_sem
):
    arrays = (
        (v, vv, DV, VC), (u, uv, DV, UC), (q, qv, DK, QC), (k, kv, DK, KC), (g, gv, DK, GC),
    )
    rows = BLOCK // SPLIT
    copies = {}
    for r in range(SPLIT):
        at = pl.ds(r * rows, rows)
        for n, (src, dst, _, _) in enumerate(arrays):
            copies[r, n] = pltpu.make_async_copy(src.at[at], dst.at[at], sem.at[r * 5 + n])
            copies[r, n].start()

    small = [
        pltpu.make_async_copy(live_h, live, small_sem.at[0]),
        pltpu.make_async_copy(doc_h, doc, small_sem.at[1]),
    ]
    for copy in small:
        copy.start()
    for copy in small:
        copy.wait()
    one_if = lambda c: jnp.where(c, 1.0, 0.0).astype(F32)
    index = lax.axis_index("ctx")
    even = lax.rem(index, 2) == 0
    first, last = doc[0].astype(F32), doc[NB - 1].astype(F32)
    numbers = [one_if(b < live[0]) for b in range(NB)] + [jnp.float32(1.0)]
    numbers += [one_if(doc[b - 1] == doc[b]) for b in range(1, NB)]
    numbers.append(one_if(even))
    for by in (1, 2):
        numbers.append(one_if(jnp.where(even, index >= 2 * by, index < owners - 2 * by)))
    numbers += [jnp.where(even, last, first), jnp.where(even, first, last)]
    for r in range(FLAG_ROWS):
        flag[r : r + 1] = jnp.full((1, DV), numbers[r] if r < len(numbers) else 0.0, F32)

    for r in range(SPLIT):
        at = slice(r * rows, (r + 1) * rows)
        for n, (_, src, width, col) in enumerate(arrays):
            copies[r, n].wait()
            for h in range(HEADS):
                out[h, at, col : col + width] = src[at, h * width : (h + 1) * width]


def pack(live, doc, q, k, g, v, u):
    hbm = pl.BlockSpec(memory_space=pltpu.HBM)
    return pl.pallas_call(
        functools.partial(pack_kernel, lax.axis_size("ctx")),
        out_shape=(
            jax.ShapeDtypeStruct((HEADS, BLOCK, IN_W), BF),
            jax.ShapeDtypeStruct((FLAG_ROWS, DV), F32),
        ),
        in_specs=[hbm] * 7,
        out_specs=(vspec(),) * 2,
        scratch_shapes=[VMEM((BLOCK, HEADS * DK), BF)] * 3
        + [VMEM((BLOCK, HEADS * DV), BF)] * 2
        + [pltpu.SMEM((1,), jnp.int32), pltpu.SMEM((NB,), jnp.int32)]
        + [pltpu.SemaphoreType.DMA((5 * SPLIT,)), pltpu.SemaphoreType.DMA((2,))],
        compiler_params=pltpu.CompilerParams(vmem_limit_bytes=56 * 1024 * 1024),
        name="pack",
    )(live, doc, q, k, g, v, u)


def unpack_kernel(x, dq, dk, dv, dg):
    for h in range(HEADS):
        kc = slice(h * DK, (h + 1) * DK)
        vc = slice(h * DV, (h + 1) * DV)
        dq[:, kc] = x[h, :, 0:DK]
        dk[:, kc] = x[h, :, DK : 2 * DK]
        dg[:, kc] = x[h, :, 2 * DK : 3 * DK]
        dv[:, vc] = x[h, :, 3 * DK :]


def unpack(x):
    narrow = jax.ShapeDtypeStruct((BLOCK, HEADS * DK), BF)
    wide = jax.ShapeDtypeStruct((BLOCK, HEADS * DV), BF)
    return pl.pallas_call(
        unpack_kernel,
        out_shape=(narrow, narrow, wide, narrow),
        in_specs=[vspec()],
        out_specs=(vspec(),) * 4,
        compiler_params=pltpu.CompilerParams(vmem_limit_bytes=16 * 1024 * 1024),
        name="unpack",
    )(x)


PAIR = 2 * BLOCK
NP = NB // 2


def rows_of(x, p, col, width):
    return x[2 * p : 2 * p + 2, :, col : col + width].reshape(PAIR, width)


def two(x):
    return jnp.concatenate(split(x), axis=1)


def one(mask):
    return jnp.where(mask, 1.0, 0.0).astype(F32)


def pair_masks():
    i = lax.broadcasted_iota(jnp.int32, (PAIR, PAIR), 0)
    j = lax.broadcasted_iota(jnp.int32, (PAIR, PAIR), 1)
    first = i < BLOCK
    return i, j, first, first == (j < BLOCK)


def totals_kernel(flag, x, kept, sent, kw, qw, cs):
    lives, keeps, even = flags(flag)
    i, j, first, same = pair_masks()
    tri = one((j <= i) & same).astype(BF)
    decay = jnp.ones((1, DK), F32)
    for p in range(NP):
        a, b = 2 * p, 2 * p + 1
        c = dot(tri, rows_of(x, p, GC, DK), 1, 0) * jnp.where(first, lives[a], lives[b])
        cs[p] = c
        earlier = decay * keeps[a]
        middle = earlier * (keeps[b] * jnp.exp(c[BLOCK - 1 : BLOCK]))
        decay = middle * jnp.exp(c[PAIR - 1 : PAIR])
        q = rows_of(x, p, QC, DK).astype(F32)
        scale = jnp.where(first, earlier * (lives[a] * SCALE), middle * (lives[b] * SCALE))
        qw[p] = two(q * (jnp.exp(c) * scale))
    rows = NB * BLOCK
    u = x[:, :, UC : UC + DV].reshape(rows, DV)
    bwd = halves(dot(u, qw[...].reshape(rows, 2 * DK), 0, 0))
    later = jnp.ones((1, DK), F32)
    for p in reversed(range(NP)):
        a, b = 2 * p, 2 * p + 1
        c = cs[p]
        ca, cb = c[BLOCK - 1 : BLOCK], c[PAIR - 1 : PAIR]
        middle = later * (keeps[b] * jnp.exp(cb))
        k = rows_of(x, p, KC, DK).astype(F32)
        fade = jnp.exp(jnp.where(first, ca, cb) - c)
        kw[p] = two(k * (fade * jnp.where(first, middle * lives[a], later * lives[b])))
        later = middle * (keeps[a] * jnp.exp(ca))
    v = x[:, :, VC : VC + DV].reshape(rows, DV)
    fwd = halves(dot(v, kw[...].reshape(rows, 2 * DK), 0, 0))
    kept[:DV] = jnp.where(even, fwd, bwd)
    sent[:DV] = jnp.where(even, bwd, fwd)
    head, tail = flag[HEAD_ID : HEAD_ID + 1, :DK], flag[TAIL_ID : TAIL_ID + 1, :DK]
    rest = jnp.zeros((MSG - DV - 3, DK), F32)
    kept[DV:] = jnp.concatenate([decay, head, tail, rest])
    sent[DV:] = jnp.concatenate([decay, tail, head, rest])


def totals(flag, x):
    msg = jax.ShapeDtypeStruct((MSG, DK), F32)
    return pl.pallas_call(
        totals_kernel,
        out_shape=(msg, msg),
        in_specs=[vspec()] * 2,
        out_specs=(vspec(),) * 2,
        scratch_shapes=[
            VMEM((NP, PAIR, 2 * DK), BF),
            VMEM((NP, PAIR, 2 * DK), BF),
            VMEM((NP, PAIR, DK), F32),
        ],
        compiler_params=pltpu.CompilerParams(vmem_limit_bytes=32 * 1024 * 1024),
        name="totals",
    )(flag, x)


def passing(near, far):
    return jnp.where(near[DV + 2 : DV + 3] == far[DV + 1 : DV + 2], near[DV : DV + 1], 0.0)


def joined(near, far):
    decay = passing(near, far)
    ends = [decay * far[DV : DV + 1], near[DV + 1 : DV + 2], far[DV + 2 :]]
    return jnp.concatenate([decay * far[:DV] + near[:DV], *ends], axis=0)


def swapped(x):
    n = lax.axis_size("ctx")
    return lax.ppermute(x, "ctx", [(i, i ^ 1) for i in range(n)])


def upstream(x, flag, by):
    n = lax.axis_size("ctx")
    target = lambda i: i + (2 * by if i % 2 == 0 else -2 * by)
    pairs = [(i, target(i) if 0 <= target(i) < n else i ^ 1) for i in range(n)]
    moved = lax.ppermute(x, "ctx", pairs)
    row = INSIDE + by - 1
    return jnp.where(flag[row : row + 1, :DK] > 0.0, moved, 0.0)


def window(kept, sent, flag, beside):
    other = swapped(sent)
    chip = joined(other, kept)
    near, far = upstream(chip, flag, 1), upstream(chip, flag, 2)
    done = beside(chip)
    near, far, done = lax.optimization_barrier((near, far, done))
    e = joined(near, far)
    e = joined(e, upstream(e, flag, 2))
    own = jnp.where(kept[DV + 2 : DV + 3] == e[DV + 1 : DV + 2], e[:DV], 0.0)
    onward = kept[DV : DV + 1] * own + kept[:DV]
    onward = jnp.where(other[DV + 2 : DV + 3] == kept[DV + 1 : DV + 2], onward, 0.0)
    return own, swapped(onward), done


def local_kernel(
    flag, x,
    query_o, rise_o, fall_o, value_o, qin_o, kout_o, kf_o, state_o, grad_o, small_o,
    qw, kw, fw, qsw, ksw,
):
    lives, keeps, _ = flags(flag)
    i, j, first, same = pair_masks()
    cross = jnp.logical_not(same)
    tri = one((j <= i) & same).astype(BF)
    low_same, low_cross = one((j <= i) & same), one((j < i) & cross)
    up_same, up_cross = one((j >= i) & same), one((j > i) & cross)
    first_v = lax.broadcasted_iota(jnp.int32, (PAIR, DV), 0) < BLOCK
    wide = [flag[b : b + 1, :].astype(BF) for b in range(NB)]

    ends = []
    prefix = jnp.ones((1, DK), F32)
    for p in range(NP):
        a, b = 2 * p, 2 * p + 1
        live = jnp.where(first, lives[a], lives[b])
        c = dot(tri, rows_of(x, p, GC, DK), 1, 0) * live
        ca, cb = c[BLOCK - 1 : BLOCK], c[PAIR - 1 : PAIR]
        d = jnp.where(first, c - ca, c)
        qs, ks = jnp.exp(d), jnp.exp(-d)
        ea, eb = keeps[a] * jnp.exp(ca), jnp.exp(cb)
        decay = ea * (keeps[b] * eb)
        ends.append((ea, eb, decay))
        q = rows_of(x, p, QC, DK).astype(F32) * (qs * SCALE)
        k = rows_of(x, p, KC, DK).astype(F32) * (ks * live)
        kf = k * jnp.where(first, keeps[b] * eb, eb)
        qsw[p], ksw[p] = qs, ks
        qw[p], kw[p] = two(q), two(k)
        fw[p] = kf
        small_o[p, 0:1] = prefix
        qin_o[p] = (qs * (live * SCALE)) * (jnp.where(first, ea, ea * keeps[b]) * prefix)
        prefix = prefix * decay
        if p == 0:
            state_o[p] = jnp.zeros((DV, DK), F32)
        else:
            state_o[p] = state
        if p < NP - 1:
            update = halves(dot(rows_of(x, p, VC, DV), two(kf), 0, 0))
            state = update if p == 0 else decay * state + update

    suffix = jnp.ones((1, DK), F32)
    for p in reversed(range(NP)):
        a, b = 2 * p, 2 * p + 1
        ea, eb, decay = ends[p]
        live = jnp.where(first, lives[a], lives[b])
        qin = jnp.where(first, ea, ea * keeps[b])
        kout = jnp.where(first, keeps[b] * eb, eb)
        qq, kk = qw[p], kw[p]
        qh, ql, kh = qq[:, :DK], qq[:, DK:], kk[:, :DK]
        qs, ks = qsw[p], ksw[p]
        v = rows_of(x, p, VC, DV)
        u = rows_of(x, p, UC, DV) * jnp.where(first_v, wide[a], wide[b])
        st = dot(kk, jnp.concatenate([qh, qh], axis=1), 1, 1) + dot(kh, ql, 1, 1)
        up = up_same + keeps[b] * up_cross
        st = jnp.where(up > 0.0, st, 0.0)
        dst = dot(v, u, 1, 1) * up
        ds = dot(u, v, 1, 1) * (low_same + keeps[b] * low_cross)
        dh, dl = split(ds)
        th, tl = split(dst)
        query = halves(dot(dh, kk, 1, 0)) + dot(dl, kh, 1, 0)
        if p > 0:
            query = query + qin * halves(dot(u, two(state_o[p]), 1, 0))
        query_o[p] = query * (qs * SCALE)
        rise_o[p] = ks * live * (halves(dot(th, qq, 1, 0)) + dot(tl, qh, 1, 0))
        value = dot(two(st), jnp.concatenate([u, u], axis=0), 1, 0)
        fall_scale = (ks * live) * kout
        kf = fw[p]
        if p < NP - 1:
            gg = two(grad)
            gh, gl = gg[:, :DK], gg[:, DK:]
            ff = two(kf)
            value = (
                value
                + dot(ff, jnp.concatenate([gh, gh], axis=1), 1, 1)
                + dot(ff[:, :DK], gl, 1, 1)
            )
            fall_o[p] = fall_scale * halves(dot(v, gg, 1, 0))
            grad_o[p] = grad
            small_o[p, 3:4] = jnp.sum(grad * state_o[p], axis=0, keepdims=True) * decay
        else:
            fall_o[p] = jnp.zeros((PAIR, DK), F32)
            grad_o[p] = jnp.zeros((DV, DK), F32)
            small_o[p, 3:4] = jnp.zeros((1, DK), F32)
        value_o[p] = value
        small_o[p, 1:2] = suffix
        small_o[p, 2:3] = decay
        kout_o[p] = fall_scale * suffix
        kf_o[p] = two(kf * suffix)
        suffix = suffix * decay
        if p > 0:
            qf = rows_of(x, p, QC, DK).astype(F32) * (qs * SCALE) * qin
            update = halves(dot(u, two(qf), 0, 0))
            grad = update if p == NP - 1 else decay * grad + update


def local(flag, x):
    f = lambda *s: jax.ShapeDtypeStruct((NP,) + s, F32)
    t = f(PAIR, DK)
    return pl.pallas_call(
        local_kernel,
        out_shape=(
            t, t, t, f(PAIR, DV), t, t,
            jax.ShapeDtypeStruct((NP, PAIR, 2 * DK), BF),
            f(DV, DK), f(DV, DK), f(8, DK),
        ),
        in_specs=[vspec()] * 2,
        out_specs=(vspec(),) * 10,
        scratch_shapes=[
            VMEM((NP, PAIR, 2 * DK), BF),
            VMEM((NP, PAIR, 2 * DK), BF),
            VMEM((NP, PAIR, DK), F32),
            VMEM((NP, PAIR, DK), F32),
            VMEM((NP, PAIR, DK), F32),
        ],
        compiler_params=pltpu.CompilerParams(vmem_limit_bytes=32 * 1024 * 1024),
        cost_estimate=pl.CostEstimate(flops=4 * 10**9, bytes_accessed=9 * 10**6, transcendentals=10**6),
        name="local",
    )(flag, x)


def finish_kernel(
    flag, x, own, other,
    query_i, rise_i, fall_i, value_i, qin_i, kout_i, kf_i, state_i, grad_i, small_i,
    out, qs, fs,
):
    i, j, first, _ = pair_masks()
    upper, strict = one(j >= i).astype(BF), one(j < i).astype(BF)
    sums = jnp.concatenate([upper, upper, strict, strict], axis=1)
    lives, _, even = flags(flag)
    state = jnp.where(even, own[...], other[...])
    grad = jnp.where(even, other[...], own[...])
    rows = NB * BLOCK
    u = x[:, :, UC : UC + DV].reshape(rows, DV)
    v = x[:, :, VC : VC + DV].reshape(rows, DV)
    gg = two(grad)
    gh, gl = gg[:, :DK], gg[:, DK:]
    qs[...] = halves(dot(u, two(state), 1, 0))
    fs[...] = halves(dot(v, gg, 1, 0))
    ghh = jnp.concatenate([gh, gh], axis=1)
    both = jnp.sum(grad * state, axis=0, keepdims=True)
    for p in range(NP):
        a = 2 * p
        alive = jnp.where(first, lives[a], lives[a + 1])
        at = pl.ds(p * PAIR, PAIR)
        query = query_i[p] + qin_i[p] * qs[at]
        falling = fall_i[p] + kout_i[p] * fs[at]
        rising = rise_i[p]
        kf = kf_i[p]
        value = value_i[p] + dot(kf, ghh, 1, 1) + dot(kf[:, :DK], gl, 1, 1)
        q = rows_of(x, p, QC, DK).astype(F32)
        k = rows_of(x, p, KC, DK).astype(F32)
        pre, suf, decay, base = (small_i[p, r : r + 1] for r in range(4))
        carry = base + decay * (
            pre * jnp.sum(grad_i[p] * state, axis=0, keepdims=True)
            + suf * jnp.sum(state_i[p] * grad, axis=0, keepdims=True)
            + (pre * suf) * both
        )
        terms = jnp.concatenate([*split(query * q - rising * k), *split(falling * k)], axis=0)
        gate = dot(sums, terms, 1, 0) + carry
        shape = lambda r: r.astype(BF).reshape(2, BLOCK, r.shape[1])
        out[a : a + 2, :, 0:DK] = shape(query)
        out[a : a + 2, :, DK : 2 * DK] = shape(rising + falling)
        out[a : a + 2, :, 2 * DK : 3 * DK] = shape(gate * alive)
        out[a : a + 2, :, 3 * DK :] = shape(value)


def finish(flag, x, own, other, parts):
    return pl.pallas_call(
        finish_kernel,
        out_shape=jax.ShapeDtypeStruct((NB, BLOCK, OUT_W), BF),
        in_specs=[vspec()] * 14,
        out_specs=vspec(),
        scratch_shapes=[VMEM((NB * BLOCK, DK), F32), VMEM((NB * BLOCK, DK), F32)],
        compiler_params=pltpu.CompilerParams(vmem_limit_bytes=32 * 1024 * 1024),
        name="finish",
    )(flag, x, own, other, *parts)


def per_device(queries, keys, values, out_grad, log_gates, live_blocks, block_doc):
    packed, flag = pack(live_blocks, block_doc, queries, keys, log_gates, values, out_grad)
    x = lax.all_to_all(packed, "head", split_axis=0, concat_axis=0, tiled=True)
    kept, sent = totals(flag, x)

    def beside(chip):
        y, _ = lax.optimization_barrier((x, chip))
        return local(flag, y)

    own, other, parts = window(kept, sent, flag, beside)
    y = finish(flag, x, own, other, parts)
    return unpack(lax.all_to_all(y, "head", split_axis=0, concat_axis=0, tiled=True))


def solution(mesh):
    rows = P(("ctx", "head"), None)
    return jax.shard_map(
        per_device,
        mesh=mesh,
        in_specs=(rows,) * 5 + (P("ctx"), P("ctx")),
        out_specs=(rows,) * 4,
        check_vma=False,
    )
```

```python
import functools

import jax
import jax.numpy as jnp
from jax import lax
from jax.experimental import pallas as pl
from jax.experimental.pallas import tpu as pltpu
from jax.sharding import PartitionSpec as P

DK = 128
DV = 256
BLOCK = 64
HEADS = 16
NB = 16
IN_W = 3 * DK + 2 * DV
OUT_W = 3 * DK + DV
QC, KC, GC, VC, UC = 0, DK, 2 * DK, 3 * DK, 3 * DK + DV
MSG = DV + 8
SCALE = DK ** (-0.5)
BF = jnp.bfloat16
F32 = jnp.float32
VMEM = pltpu.VMEM


def vspec():
    return pl.BlockSpec(memory_space=VMEM)


def split(x):
    hi = x.astype(BF)
    lo = (x - hi.astype(F32)).astype(BF)
    return hi, lo


def dot(a, b, ca, cb):
    return lax.dot_general(a, b, (((ca,), (cb,)), ((), ())), preferred_element_type=F32)


def halves(r):
    return r[:, :DK] + r[:, DK:]


EVEN, INSIDE, HEAD_ID, TAIL_ID, FLAG_ROWS = 2 * NB, 2 * NB + 1, 2 * NB + 3, 2 * NB + 4, 2 * NB + 8


def flags(flag):
    row = lambda r: flag[r : r + 1, :DK]
    lives, keeps = [row(b) for b in range(NB)], [row(NB + b) for b in range(NB)]
    return lives, keeps, row(EVEN) > 0.0


SPLIT = 2


def pack_kernel(
    owners, live_h, doc_h, q, k, g, v, u, out_h, flag_h,
    qv, kv, gv, vv, uv, out, flag, live, doc, sem, small_sem, out_sem,
):
    arrays = (
        (v, vv, DV, VC), (u, uv, DV, UC), (q, qv, DK, QC), (k, kv, DK, KC), (g, gv, DK, GC),
    )
    rows = BLOCK // SPLIT
    copies = {}
    for r in range(SPLIT):
        at = pl.ds(r * rows, rows)
        for n, (src, dst, _, _) in enumerate(arrays):
            copies[r, n] = pltpu.make_async_copy(src.at[at], dst.at[at], sem.at[r * 5 + n])
            copies[r, n].start()

    small = [
        pltpu.make_async_copy(live_h, live, small_sem.at[0]),
        pltpu.make_async_copy(doc_h, doc, small_sem.at[1]),
    ]
    for copy in small:
        copy.start()
    for copy in small:
        copy.wait()
    one_if = lambda c: jnp.where(c, 1.0, 0.0).astype(F32)
    index = lax.axis_index("ctx")
    even = lax.rem(index, 2) == 0
    first, last = doc[0].astype(F32), doc[NB - 1].astype(F32)
    numbers = [one_if(b < live[0]) for b in range(NB)] + [jnp.float32(1.0)]
    numbers += [one_if(doc[b - 1] == doc[b]) for b in range(1, NB)]
    numbers.append(one_if(even))
    for by in (1, 2):
        numbers.append(one_if(jnp.where(even, index >= 2 * by, index < owners - 2 * by)))
    numbers += [jnp.where(even, last, first), jnp.where(even, first, last)]
    for r in range(FLAG_ROWS):
        flag[r : r + 1] = jnp.full((1, DV), numbers[r] if r < len(numbers) else 0.0, F32)
    outs = [pltpu.make_async_copy(flag, flag_h, out_sem.at[SPLIT])]
    outs[0].start()

    for r in range(SPLIT):
        at = slice(r * rows, (r + 1) * rows)
        for n, (_, src, width, col) in enumerate(arrays):
            copies[r, n].wait()
            for h in range(HEADS):
                out[h, at, col : col + width] = src[at, h * width : (h + 1) * width]
        at = pl.ds(r * rows, rows)
        outs.append(pltpu.make_async_copy(out.at[:, at], out_h.at[:, at], out_sem.at[r]))
        outs[-1].start()
    for copy in outs:
        copy.wait()


def pack(live, doc, q, k, g, v, u):
    hbm = pl.BlockSpec(memory_space=pltpu.HBM)
    return pl.pallas_call(
        functools.partial(pack_kernel, lax.axis_size("ctx")),
        out_shape=(
            jax.ShapeDtypeStruct((HEADS, BLOCK, IN_W), BF),
            jax.ShapeDtypeStruct((FLAG_ROWS, DV), F32),
        ),
        in_specs=[hbm] * 7,
        out_specs=(hbm,) * 2,
        scratch_shapes=[VMEM((BLOCK, HEADS * DK), BF)] * 3
        + [VMEM((BLOCK, HEADS * DV), BF)] * 2
        + [VMEM((HEADS, BLOCK, IN_W), BF), VMEM((FLAG_ROWS, DV), F32)]
        + [pltpu.SMEM((1,), jnp.int32), pltpu.SMEM((NB,), jnp.int32)]
        + [pltpu.SemaphoreType.DMA((n,)) for n in (5 * SPLIT, 2, SPLIT + 1)],
        compiler_params=pltpu.CompilerParams(vmem_limit_bytes=56 * 1024 * 1024),
        name="pack",
    )(live, doc, q, k, g, v, u)


def unpack_kernel(x, dq, dk, dv, dg, qv, kv, vv, gv, sem):
    copies = []
    for n, (dst, buf, width, col) in enumerate(
        ((dv, vv, DV, 3 * DK), (dq, qv, DK, 0), (dk, kv, DK, DK), (dg, gv, DK, 2 * DK))
    ):
        for h in range(HEADS):
            buf[:, h * width : (h + 1) * width] = x[h, :, col : col + width]
        copies.append(pltpu.make_async_copy(buf, dst, sem.at[n]))
        copies[-1].start()
    for copy in copies:
        copy.wait()


def unpack(x):
    narrow = jax.ShapeDtypeStruct((BLOCK, HEADS * DK), BF)
    wide = jax.ShapeDtypeStruct((BLOCK, HEADS * DV), BF)
    return pl.pallas_call(
        unpack_kernel,
        out_shape=(narrow, narrow, wide, narrow),
        in_specs=[vspec()],
        out_specs=(pl.BlockSpec(memory_space=pltpu.HBM),) * 4,
        scratch_shapes=[VMEM(s.shape, BF) for s in (narrow, narrow, wide, narrow)]
        + [pltpu.SemaphoreType.DMA((4,))],
        compiler_params=pltpu.CompilerParams(vmem_limit_bytes=16 * 1024 * 1024),
        name="unpack",
    )(x)


PAIR = 2 * BLOCK
NP = NB // 2


def rows_of(x, p, col, width):
    return x[2 * p : 2 * p + 2, :, col : col + width].reshape(PAIR, width)


def two(x):
    return jnp.concatenate(split(x), axis=1)


def one(mask):
    return jnp.where(mask, 1.0, 0.0).astype(F32)


def pair_masks():
    i = lax.broadcasted_iota(jnp.int32, (PAIR, PAIR), 0)
    j = lax.broadcasted_iota(jnp.int32, (PAIR, PAIR), 1)
    first = i < BLOCK
    return i, j, first, first == (j < BLOCK)


def totals_kernel(flag, x, kept, sent, kw, qw, cs):
    lives, keeps, even = flags(flag)
    i, j, first, same = pair_masks()
    tri = one((j <= i) & same).astype(BF)
    decay = jnp.ones((1, DK), F32)
    for p in range(NP):
        a, b = 2 * p, 2 * p + 1
        c = dot(tri, rows_of(x, p, GC, DK), 1, 0) * jnp.where(first, lives[a], lives[b])
        cs[p] = c
        earlier = decay * keeps[a]
        middle = earlier * (keeps[b] * jnp.exp(c[BLOCK - 1 : BLOCK]))
        decay = middle * jnp.exp(c[PAIR - 1 : PAIR])
        q = rows_of(x, p, QC, DK).astype(F32)
        scale = jnp.where(first, earlier * (lives[a] * SCALE), middle * (lives[b] * SCALE))
        qw[p] = two(q * (jnp.exp(c) * scale))
    rows = NB * BLOCK
    u = x[:, :, UC : UC + DV].reshape(rows, DV)
    bwd = halves(dot(u, qw[...].reshape(rows, 2 * DK), 0, 0))
    later = jnp.ones((1, DK), F32)
    for p in reversed(range(NP)):
        a, b = 2 * p, 2 * p + 1
        c = cs[p]
        ca, cb = c[BLOCK - 1 : BLOCK], c[PAIR - 1 : PAIR]
        middle = later * (keeps[b] * jnp.exp(cb))
        k = rows_of(x, p, KC, DK).astype(F32)
        fade = jnp.exp(jnp.where(first, ca, cb) - c)
        kw[p] = two(k * (fade * jnp.where(first, middle * lives[a], later * lives[b])))
        later = middle * (keeps[a] * jnp.exp(ca))
    v = x[:, :, VC : VC + DV].reshape(rows, DV)
    fwd = halves(dot(v, kw[...].reshape(rows, 2 * DK), 0, 0))
    kept[:DV] = jnp.where(even, fwd, bwd)
    sent[:DV] = jnp.where(even, bwd, fwd)
    head, tail = flag[HEAD_ID : HEAD_ID + 1, :DK], flag[TAIL_ID : TAIL_ID + 1, :DK]
    rest = jnp.zeros((MSG - DV - 3, DK), F32)
    kept[DV:] = jnp.concatenate([decay, head, tail, rest])
    sent[DV:] = jnp.concatenate([decay, tail, head, rest])


def totals(flag, x):
    msg = jax.ShapeDtypeStruct((MSG, DK), F32)
    return pl.pallas_call(
        totals_kernel,
        out_shape=(msg, msg),
        in_specs=[vspec()] * 2,
        out_specs=(vspec(),) * 2,
        scratch_shapes=[
            VMEM((NP, PAIR, 2 * DK), BF),
            VMEM((NP, PAIR, 2 * DK), BF),
            VMEM((NP, PAIR, DK), F32),
        ],
        compiler_params=pltpu.CompilerParams(vmem_limit_bytes=32 * 1024 * 1024),
        name="totals",
    )(flag, x)


def passing(near, far):
    return jnp.where(near[DV + 2 : DV + 3] == far[DV + 1 : DV + 2], near[DV : DV + 1], 0.0)


def joined(near, far):
    decay = passing(near, far)
    ends = [decay * far[DV : DV + 1], near[DV + 1 : DV + 2], far[DV + 2 :]]
    return jnp.concatenate([decay * far[:DV] + near[:DV], *ends], axis=0)


def swapped(x):
    n = lax.axis_size("ctx")
    return lax.ppermute(x, "ctx", [(i, i ^ 1) for i in range(n)])


def upstream(x, flag, by):
    n = lax.axis_size("ctx")
    target = lambda i: i + (2 * by if i % 2 == 0 else -2 * by)
    pairs = [(i, target(i) if 0 <= target(i) < n else i ^ 1) for i in range(n)]
    moved = lax.ppermute(x, "ctx", pairs)
    row = INSIDE + by - 1
    return jnp.where(flag[row : row + 1, :DK] > 0.0, moved, 0.0)


def window(kept, sent, flag, beside):
    other = swapped(sent)
    chip = joined(other, kept)
    near, far = upstream(chip, flag, 1), upstream(chip, flag, 2)
    done = beside(chip)
    near, far, done = lax.optimization_barrier((near, far, done))
    e = joined(near, far)
    e = joined(e, upstream(e, flag, 2))
    own = jnp.where(kept[DV + 2 : DV + 3] == e[DV + 1 : DV + 2], e[:DV], 0.0)
    onward = kept[DV : DV + 1] * own + kept[:DV]
    onward = jnp.where(other[DV + 2 : DV + 3] == kept[DV + 1 : DV + 2], onward, 0.0)
    return own, swapped(onward), done


def local_kernel(
    flag, x,
    query_o, rise_o, fall_o, value_o, qin_o, kout_o, kf_o, state_o, grad_o, small_o,
    qw, kw, fw, qsw, ksw,
):
    lives, keeps, _ = flags(flag)
    i, j, first, same = pair_masks()
    cross = jnp.logical_not(same)
    tri = one((j <= i) & same).astype(BF)
    low_same, low_cross = one((j <= i) & same), one((j < i) & cross)
    up_same, up_cross = one((j >= i) & same), one((j > i) & cross)
    first_v = lax.broadcasted_iota(jnp.int32, (PAIR, DV), 0) < BLOCK
    wide = [flag[b : b + 1, :].astype(BF) for b in range(NB)]

    ends = []
    prefix = jnp.ones((1, DK), F32)
    for p in range(NP):
        a, b = 2 * p, 2 * p + 1
        live = jnp.where(first, lives[a], lives[b])
        c = dot(tri, rows_of(x, p, GC, DK), 1, 0) * live
        ca, cb = c[BLOCK - 1 : BLOCK], c[PAIR - 1 : PAIR]
        d = jnp.where(first, c - ca, c)
        qs, ks = jnp.exp(d), jnp.exp(-d)
        ea, eb = keeps[a] * jnp.exp(ca), jnp.exp(cb)
        decay = ea * (keeps[b] * eb)
        ends.append((ea, eb, decay))
        q = rows_of(x, p, QC, DK).astype(F32) * (qs * SCALE)
        k = rows_of(x, p, KC, DK).astype(F32) * (ks * live)
        kf = k * jnp.where(first, keeps[b] * eb, eb)
        qsw[p], ksw[p] = qs, ks
        qw[p], kw[p] = two(q), two(k)
        fw[p] = kf
        small_o[p, 0:1] = prefix
        qin_o[p] = (qs * (live * SCALE)) * (jnp.where(first, ea, ea * keeps[b]) * prefix)
        prefix = prefix * decay
        if p == 0:
            state_o[p] = jnp.zeros((DV, DK), F32)
        else:
            state_o[p] = state
        if p < NP - 1:
            update = halves(dot(rows_of(x, p, VC, DV), two(kf), 0, 0))
            state = update if p == 0 else decay * state + update

    suffix = jnp.ones((1, DK), F32)
    for p in reversed(range(NP)):
        a, b = 2 * p, 2 * p + 1
        ea, eb, decay = ends[p]
        live = jnp.where(first, lives[a], lives[b])
        qin = jnp.where(first, ea, ea * keeps[b])
        kout = jnp.where(first, keeps[b] * eb, eb)
        qq, kk = qw[p], kw[p]
        qh, ql, kh = qq[:, :DK], qq[:, DK:], kk[:, :DK]
        qs, ks = qsw[p], ksw[p]
        v = rows_of(x, p, VC, DV)
        u = rows_of(x, p, UC, DV) * jnp.where(first_v, wide[a], wide[b])
        st = dot(kk, jnp.concatenate([qh, qh], axis=1), 1, 1) + dot(kh, ql, 1, 1)
        up = up_same + keeps[b] * up_cross
        st = jnp.where(up > 0.0, st, 0.0)
        dst = dot(v, u, 1, 1) * up
        ds = dot(u, v, 1, 1) * (low_same + keeps[b] * low_cross)
        dh, dl = split(ds)
        th, tl = split(dst)
        query = halves(dot(dh, kk, 1, 0)) + dot(dl, kh, 1, 0)
        if p > 0:
            query = query + qin * halves(dot(u, two(state_o[p]), 1, 0))
        query_o[p] = query * (qs * SCALE)
        rise_o[p] = ks * live * (halves(dot(th, qq, 1, 0)) + dot(tl, qh, 1, 0))
        value = dot(two(st), jnp.concatenate([u, u], axis=0), 1, 0)
        fall_scale = (ks * live) * kout
        kf = fw[p]
        if p < NP - 1:
            gg = two(grad)
            gh, gl = gg[:, :DK], gg[:, DK:]
            ff = two(kf)
            value = (
                value
                + dot(ff, jnp.concatenate([gh, gh], axis=1), 1, 1)
                + dot(ff[:, :DK], gl, 1, 1)
            )
            fall_o[p] = fall_scale * halves(dot(v, gg, 1, 0))
            grad_o[p] = grad
            small_o[p, 3:4] = jnp.sum(grad * state_o[p], axis=0, keepdims=True) * decay
        else:
            fall_o[p] = jnp.zeros((PAIR, DK), F32)
            grad_o[p] = jnp.zeros((DV, DK), F32)
            small_o[p, 3:4] = jnp.zeros((1, DK), F32)
        value_o[p] = value
        small_o[p, 1:2] = suffix
        small_o[p, 2:3] = decay
        kout_o[p] = fall_scale * suffix
        kf_o[p] = two(kf * suffix)
        suffix = suffix * decay
        if p > 0:
            qf = rows_of(x, p, QC, DK).astype(F32) * (qs * SCALE) * qin
            update = halves(dot(u, two(qf), 0, 0))
            grad = update if p == NP - 1 else decay * grad + update


def local(flag, x):
    f = lambda *s: jax.ShapeDtypeStruct((NP,) + s, F32)
    t = f(PAIR, DK)
    return pl.pallas_call(
        local_kernel,
        out_shape=(
            t, t, t, f(PAIR, DV), t, t,
            jax.ShapeDtypeStruct((NP, PAIR, 2 * DK), BF),
            f(DV, DK), f(DV, DK), f(8, DK),
        ),
        in_specs=[vspec()] * 2,
        out_specs=(vspec(),) * 10,
        scratch_shapes=[
            VMEM((NP, PAIR, 2 * DK), BF),
            VMEM((NP, PAIR, 2 * DK), BF),
            VMEM((NP, PAIR, DK), F32),
            VMEM((NP, PAIR, DK), F32),
            VMEM((NP, PAIR, DK), F32),
        ],
        compiler_params=pltpu.CompilerParams(vmem_limit_bytes=32 * 1024 * 1024),
        cost_estimate=pl.CostEstimate(flops=4 * 10**9, bytes_accessed=9 * 10**6, transcendentals=10**6),
        name="local",
    )(flag, x)


def finish_kernel(
    flag, x, own, other,
    query_i, rise_i, fall_i, value_i, qin_i, kout_i, kf_i, state_i, grad_i, small_i,
    out, qs, fs,
):
    i, j, first, _ = pair_masks()
    upper, strict = one(j >= i).astype(BF), one(j < i).astype(BF)
    sums = jnp.concatenate([upper, upper, strict, strict], axis=1)
    lives, _, even = flags(flag)
    state = jnp.where(even, own[...], other[...])
    grad = jnp.where(even, other[...], own[...])
    rows = NB * BLOCK
    u = x[:, :, UC : UC + DV].reshape(rows, DV)
    v = x[:, :, VC : VC + DV].reshape(rows, DV)
    gg = two(grad)
    gh, gl = gg[:, :DK], gg[:, DK:]
    qs[...] = halves(dot(u, two(state), 1, 0))
    fs[...] = halves(dot(v, gg, 1, 0))
    ghh = jnp.concatenate([gh, gh], axis=1)
    both = jnp.sum(grad * state, axis=0, keepdims=True)
    for p in range(NP):
        a = 2 * p
        alive = jnp.where(first, lives[a], lives[a + 1])
        at = pl.ds(p * PAIR, PAIR)
        query = query_i[p] + qin_i[p] * qs[at]
        falling = fall_i[p] + kout_i[p] * fs[at]
        rising = rise_i[p]
        kf = kf_i[p]
        value = value_i[p] + dot(kf, ghh, 1, 1) + dot(kf[:, :DK], gl, 1, 1)
        q = rows_of(x, p, QC, DK).astype(F32)
        k = rows_of(x, p, KC, DK).astype(F32)
        pre, suf, decay, base = (small_i[p, r : r + 1] for r in range(4))
        carry = base + decay * (
            pre * jnp.sum(grad_i[p] * state, axis=0, keepdims=True)
            + suf * jnp.sum(state_i[p] * grad, axis=0, keepdims=True)
            + (pre * suf) * both
        )
        terms = jnp.concatenate([*split(query * q - rising * k), *split(falling * k)], axis=0)
        gate = dot(sums, terms, 1, 0) + carry
        shape = lambda r: r.astype(BF).reshape(2, BLOCK, r.shape[1])
        out[a : a + 2, :, 0:DK] = shape(query)
        out[a : a + 2, :, DK : 2 * DK] = shape(rising + falling)
        out[a : a + 2, :, 2 * DK : 3 * DK] = shape(gate * alive)
        out[a : a + 2, :, 3 * DK :] = shape(value)


def finish(flag, x, own, other, parts):
    return pl.pallas_call(
        finish_kernel,
        out_shape=jax.ShapeDtypeStruct((NB, BLOCK, OUT_W), BF),
        in_specs=[vspec()] * 14,
        out_specs=vspec(),
        scratch_shapes=[VMEM((NB * BLOCK, DK), F32), VMEM((NB * BLOCK, DK), F32)],
        compiler_params=pltpu.CompilerParams(vmem_limit_bytes=32 * 1024 * 1024),
        name="finish",
    )(flag, x, own, other, *parts)


def per_device(queries, keys, values, out_grad, log_gates, live_blocks, block_doc):
    packed, flag = pack(live_blocks, block_doc, queries, keys, log_gates, values, out_grad)
    x = lax.all_to_all(packed, "head", split_axis=0, concat_axis=0, tiled=True)
    kept, sent = totals(flag, x)

    def beside(chip):
        y, _ = lax.optimization_barrier((x, chip))
        return local(flag, y)

    own, other, parts = window(kept, sent, flag, beside)
    y = finish(flag, x, own, other, parts)
    return unpack(lax.all_to_all(y, "head", split_axis=0, concat_axis=0, tiled=True))


def solution(mesh):
    rows = P(("ctx", "head"), None)
    return jax.shard_map(
        per_device,
        mesh=mesh,
        in_specs=(rows,) * 5 + (P("ctx"), P("ctx")),
        out_specs=(rows,) * 4,
        check_vma=False,
    )
```

```python
import functools

import jax
import jax.numpy as jnp
from jax import lax
from jax.experimental import pallas as pl
from jax.experimental.pallas import tpu as pltpu
from jax.sharding import PartitionSpec as P

DK = 128
DV = 256
BLOCK = 64
HEADS = 16
NB = 16
IN_W = 3 * DK + 2 * DV
OUT_W = 3 * DK + DV
QC, KC, GC, VC, UC = 0, DK, 2 * DK, 3 * DK, 3 * DK + DV
MSG = DV + 8
SCALE = DK ** (-0.5)
BF = jnp.bfloat16
F32 = jnp.float32
VMEM = pltpu.VMEM


def vspec():
    return pl.BlockSpec(memory_space=VMEM)


def split(x):
    hi = x.astype(BF)
    lo = (x - hi.astype(F32)).astype(BF)
    return hi, lo


def dot(a, b, ca, cb):
    return lax.dot_general(a, b, (((ca,), (cb,)), ((), ())), preferred_element_type=F32)


def halves(r):
    return r[:, :DK] + r[:, DK:]


EVEN, INSIDE, HEAD_ID, TAIL_ID, FLAG_ROWS = 2 * NB, 2 * NB + 1, 2 * NB + 3, 2 * NB + 4, 2 * NB + 8


def flags(flag):
    row = lambda r: flag[r : r + 1, :DK]
    lives, keeps = [row(b) for b in range(NB)], [row(NB + b) for b in range(NB)]
    return lives, keeps, row(EVEN) > 0.0


SPLIT = 2


def pack_kernel(
    owners, live_h, doc_h, q, k, g, v, u, out_h, flag_h,
    qv, kv, gv, vv, uv, out, flag, live, doc, sem, small_sem, out_sem,
):
    arrays = (
        (v, vv, DV, VC), (u, uv, DV, UC), (q, qv, DK, QC), (k, kv, DK, KC), (g, gv, DK, GC),
    )
    rows = BLOCK // SPLIT
    copies = {}
    for r in range(SPLIT):
        at = pl.ds(r * rows, rows)
        for n, (src, dst, _, _) in enumerate(arrays):
            copies[r, n] = pltpu.make_async_copy(src.at[at], dst.at[at], sem.at[r * 5 + n])
            copies[r, n].start()

    small = [
        pltpu.make_async_copy(live_h, live, small_sem.at[0]),
        pltpu.make_async_copy(doc_h, doc, small_sem.at[1]),
    ]
    for copy in small:
        copy.start()
    for copy in small:
        copy.wait()
    one_if = lambda c: jnp.where(c, 1.0, 0.0).astype(F32)
    index = lax.axis_index("ctx")
    even = lax.rem(index, 2) == 0
    first, last = doc[0].astype(F32), doc[NB - 1].astype(F32)
    numbers = [one_if(b < live[0]) for b in range(NB)] + [jnp.float32(1.0)]
    numbers += [one_if(doc[b - 1] == doc[b]) for b in range(1, NB)]
    numbers.append(one_if(even))
    for by in (1, 2):
        numbers.append(one_if(jnp.where(even, index >= 2 * by, index < owners - 2 * by)))
    numbers += [jnp.where(even, last, first), jnp.where(even, first, last)]
    for r in range(FLAG_ROWS):
        flag[r : r + 1] = jnp.full((1, DV), numbers[r] if r < len(numbers) else 0.0, F32)
    outs = [pltpu.make_async_copy(flag, flag_h, out_sem.at[SPLIT])]
    outs[0].start()

    for r in range(SPLIT):
        at = slice(r * rows, (r + 1) * rows)
        for n, (_, src, width, col) in enumerate(arrays):
            copies[r, n].wait()
            for h in range(HEADS):
                out[h, at, col : col + width] = src[at, h * width : (h + 1) * width]
        at = pl.ds(r * rows, rows)
        outs.append(pltpu.make_async_copy(out.at[:, at], out_h.at[:, at], out_sem.at[r]))
        outs[-1].start()
    for copy in outs:
        copy.wait()


def pack(live, doc, q, k, g, v, u):
    hbm = pl.BlockSpec(memory_space=pltpu.HBM)
    return pl.pallas_call(
        functools.partial(pack_kernel, lax.axis_size("ctx")),
        out_shape=(
            jax.ShapeDtypeStruct((HEADS, BLOCK, IN_W), BF),
            jax.ShapeDtypeStruct((FLAG_ROWS, DV), F32),
        ),
        in_specs=[hbm] * 7,
        out_specs=(hbm,) * 2,
        scratch_shapes=[VMEM((BLOCK, HEADS * DK), BF)] * 3
        + [VMEM((BLOCK, HEADS * DV), BF)] * 2
        + [VMEM((HEADS, BLOCK, IN_W), BF), VMEM((FLAG_ROWS, DV), F32)]
        + [pltpu.SMEM((1,), jnp.int32), pltpu.SMEM((NB,), jnp.int32)]
        + [pltpu.SemaphoreType.DMA((n,)) for n in (5 * SPLIT, 2, SPLIT + 1)],
        compiler_params=pltpu.CompilerParams(vmem_limit_bytes=56 * 1024 * 1024),
        name="pack",
    )(live, doc, q, k, g, v, u)


def unpack_kernel(x, dq, dk, dv, dg, qv, kv, vv, gv, sem):
    copies = []
    for n, (dst, buf, width, col) in enumerate(
        ((dv, vv, DV, 3 * DK), (dq, qv, DK, 0), (dk, kv, DK, DK), (dg, gv, DK, 2 * DK))
    ):
        for h in range(HEADS):
            buf[:, h * width : (h + 1) * width] = x[h, :, col : col + width]
        copies.append(pltpu.make_async_copy(buf, dst, sem.at[n]))
        copies[-1].start()
    for copy in copies:
        copy.wait()


def unpack(x):
    narrow = jax.ShapeDtypeStruct((BLOCK, HEADS * DK), BF)
    wide = jax.ShapeDtypeStruct((BLOCK, HEADS * DV), BF)
    return pl.pallas_call(
        unpack_kernel,
        out_shape=(narrow, narrow, wide, narrow),
        in_specs=[vspec()],
        out_specs=(pl.BlockSpec(memory_space=pltpu.HBM),) * 4,
        scratch_shapes=[VMEM(s.shape, BF) for s in (narrow, narrow, wide, narrow)]
        + [pltpu.SemaphoreType.DMA((4,))],
        compiler_params=pltpu.CompilerParams(vmem_limit_bytes=16 * 1024 * 1024),
        name="unpack",
    )(x)


PAIR = 2 * BLOCK
NP = NB // 2


def rows_of(x, p, col, width):
    return x[2 * p : 2 * p + 2, :, col : col + width].reshape(PAIR, width)


def two(x):
    return jnp.concatenate(split(x), axis=1)


def one(mask):
    return jnp.where(mask, 1.0, 0.0).astype(F32)


def pair_masks():
    i = lax.broadcasted_iota(jnp.int32, (PAIR, PAIR), 0)
    j = lax.broadcasted_iota(jnp.int32, (PAIR, PAIR), 1)
    first = i < BLOCK
    return i, j, first, first == (j < BLOCK)


def totals_kernel(flag, x, kept, sent, kw, qw, cs):
    lives, keeps, even = flags(flag)
    i, j, first, same = pair_masks()
    tri = one((j <= i) & same).astype(BF)
    decay = jnp.ones((1, DK), F32)
    for p in range(NP):
        a, b = 2 * p, 2 * p + 1
        c = dot(tri, rows_of(x, p, GC, DK), 1, 0) * jnp.where(first, lives[a], lives[b])
        cs[p] = c
        earlier = decay * keeps[a]
        middle = earlier * (keeps[b] * jnp.exp(c[BLOCK - 1 : BLOCK]))
        decay = middle * jnp.exp(c[PAIR - 1 : PAIR])
        q = rows_of(x, p, QC, DK).astype(F32)
        scale = jnp.where(first, earlier * (lives[a] * SCALE), middle * (lives[b] * SCALE))
        qw[p] = two(q * (jnp.exp(c) * scale))
    rows = NB * BLOCK
    u = x[:, :, UC : UC + DV].reshape(rows, DV)
    bwd = halves(dot(u, qw[...].reshape(rows, 2 * DK), 0, 0))
    later = jnp.ones((1, DK), F32)
    for p in reversed(range(NP)):
        a, b = 2 * p, 2 * p + 1
        c = cs[p]
        ca, cb = c[BLOCK - 1 : BLOCK], c[PAIR - 1 : PAIR]
        middle = later * (keeps[b] * jnp.exp(cb))
        k = rows_of(x, p, KC, DK).astype(F32)
        fade = jnp.exp(jnp.where(first, ca, cb) - c)
        kw[p] = two(k * (fade * jnp.where(first, middle * lives[a], later * lives[b])))
        later = middle * (keeps[a] * jnp.exp(ca))
    v = x[:, :, VC : VC + DV].reshape(rows, DV)
    fwd = halves(dot(v, kw[...].reshape(rows, 2 * DK), 0, 0))
    kept[:DV] = jnp.where(even, fwd, bwd)
    sent[:DV] = jnp.where(even, bwd, fwd)
    head, tail = flag[HEAD_ID : HEAD_ID + 1, :DK], flag[TAIL_ID : TAIL_ID + 1, :DK]
    rest = jnp.zeros((MSG - DV - 3, DK), F32)
    kept[DV:] = jnp.concatenate([decay, head, tail, rest])
    sent[DV:] = jnp.concatenate([decay, tail, head, rest])


def totals(flag, x):
    msg = jax.ShapeDtypeStruct((MSG, DK), F32)
    return pl.pallas_call(
        totals_kernel,
        out_shape=(msg, msg),
        in_specs=[vspec()] * 2,
        out_specs=(vspec(),) * 2,
        scratch_shapes=[
            VMEM((NP, PAIR, 2 * DK), BF),
            VMEM((NP, PAIR, 2 * DK), BF),
            VMEM((NP, PAIR, DK), F32),
        ],
        compiler_params=pltpu.CompilerParams(vmem_limit_bytes=32 * 1024 * 1024),
        name="totals",
    )(flag, x)


def passing(near, far):
    return jnp.where(near[DV + 2 : DV + 3] == far[DV + 1 : DV + 2], near[DV : DV + 1], 0.0)


def joined(near, far):
    decay = passing(near, far)
    ends = [decay * far[DV : DV + 1], near[DV + 1 : DV + 2], far[DV + 2 :]]
    return jnp.concatenate([decay * far[:DV] + near[:DV], *ends], axis=0)


def swapped(x):
    n = lax.axis_size("ctx")
    return lax.ppermute(x, "ctx", [(i, i ^ 1) for i in range(n)])


def upstream(x, flag, by):
    n = lax.axis_size("ctx")
    target = lambda i: i + (2 * by if i % 2 == 0 else -2 * by)
    pairs = [(i, target(i) if 0 <= target(i) < n else i ^ 1) for i in range(n)]
    moved = lax.ppermute(x, "ctx", pairs)
    row = INSIDE + by - 1
    return jnp.where(flag[row : row + 1, :DK] > 0.0, moved, 0.0)


def window(kept, sent, flag, beside):
    other = swapped(sent)
    chip = joined(other, kept)
    far = upstream(chip, flag, 2)
    near = upstream(chip, flag, 1)
    done = beside(chip)
    far, near, done = lax.optimization_barrier((far, near, done))
    e = joined(near, far)
    e = joined(e, upstream(e, flag, 2))
    own = jnp.where(kept[DV + 2 : DV + 3] == e[DV + 1 : DV + 2], e[:DV], 0.0)
    onward = kept[DV : DV + 1] * own + kept[:DV]
    onward = jnp.where(other[DV + 2 : DV + 3] == kept[DV + 1 : DV + 2], onward, 0.0)
    return own, swapped(onward), done


def local_kernel(
    flag, x,
    query_o, rise_o, fall_o, value_o, qin_o, kout_o, kf_o, state_o, grad_o, small_o,
    qw, kw, fw, qsw, ksw,
):
    lives, keeps, _ = flags(flag)
    i, j, first, same = pair_masks()
    cross = jnp.logical_not(same)
    tri = one((j <= i) & same).astype(BF)
    low_same, low_cross = one((j <= i) & same), one((j < i) & cross)
    up_same, up_cross = one((j >= i) & same), one((j > i) & cross)
    first_v = lax.broadcasted_iota(jnp.int32, (PAIR, DV), 0) < BLOCK
    wide = [flag[b : b + 1, :].astype(BF) for b in range(NB)]

    ends = []
    prefix = jnp.ones((1, DK), F32)
    for p in range(NP):
        a, b = 2 * p, 2 * p + 1
        live = jnp.where(first, lives[a], lives[b])
        c = dot(tri, rows_of(x, p, GC, DK), 1, 0) * live
        ca, cb = c[BLOCK - 1 : BLOCK], c[PAIR - 1 : PAIR]
        d = jnp.where(first, c - ca, c)
        qs, ks = jnp.exp(d), jnp.exp(-d)
        ea, eb = keeps[a] * jnp.exp(ca), jnp.exp(cb)
        decay = ea * (keeps[b] * eb)
        ends.append((ea, eb, decay))
        q = rows_of(x, p, QC, DK).astype(F32) * (qs * SCALE)
        k = rows_of(x, p, KC, DK).astype(F32) * (ks * live)
        kf = k * jnp.where(first, keeps[b] * eb, eb)
        qsw[p], ksw[p] = qs, ks
        qw[p], kw[p] = two(q), two(k)
        fw[p] = kf
        small_o[p, 0:1] = prefix
        qin_o[p] = (qs * (live * SCALE)) * (jnp.where(first, ea, ea * keeps[b]) * prefix)
        prefix = prefix * decay
        if p == 0:
            state_o[p] = jnp.zeros((DV, DK), F32)
        else:
            state_o[p] = state
        if p < NP - 1:
            update = halves(dot(rows_of(x, p, VC, DV), two(kf), 0, 0))
            state = update if p == 0 else decay * state + update

    suffix = jnp.ones((1, DK), F32)
    for p in reversed(range(NP)):
        a, b = 2 * p, 2 * p + 1
        ea, eb, decay = ends[p]
        live = jnp.where(first, lives[a], lives[b])
        qin = jnp.where(first, ea, ea * keeps[b])
        kout = jnp.where(first, keeps[b] * eb, eb)
        qq, kk = qw[p], kw[p]
        qh, ql, kh = qq[:, :DK], qq[:, DK:], kk[:, :DK]
        qs, ks = qsw[p], ksw[p]
        v = rows_of(x, p, VC, DV)
        u = rows_of(x, p, UC, DV) * jnp.where(first_v, wide[a], wide[b])
        st = dot(kk, jnp.concatenate([qh, qh], axis=1), 1, 1) + dot(kh, ql, 1, 1)
        up = up_same + keeps[b] * up_cross
        st = jnp.where(up > 0.0, st, 0.0)
        dst = dot(v, u, 1, 1) * up
        ds = dot(u, v, 1, 1) * (low_same + keeps[b] * low_cross)
        dh, dl = split(ds)
        th, tl = split(dst)
        query = halves(dot(dh, kk, 1, 0)) + dot(dl, kh, 1, 0)
        if p > 0:
            query = query + qin * halves(dot(u, two(state_o[p]), 1, 0))
        query_o[p] = query * (qs * SCALE)
        rise_o[p] = ks * live * (halves(dot(th, qq, 1, 0)) + dot(tl, qh, 1, 0))
        value = dot(two(st), jnp.concatenate([u, u], axis=0), 1, 0)
        fall_scale = (ks * live) * kout
        kf = fw[p]
        if p < NP - 1:
            gg = two(grad)
            gh, gl = gg[:, :DK], gg[:, DK:]
            ff = two(kf)
            value = (
                value
                + dot(ff, jnp.concatenate([gh, gh], axis=1), 1, 1)
                + dot(ff[:, :DK], gl, 1, 1)
            )
            fall_o[p] = fall_scale * halves(dot(v, gg, 1, 0))
            grad_o[p] = grad
            small_o[p, 3:4] = jnp.sum(grad * state_o[p], axis=0, keepdims=True) * decay
        else:
            fall_o[p] = jnp.zeros((PAIR, DK), F32)
            grad_o[p] = jnp.zeros((DV, DK), F32)
            small_o[p, 3:4] = jnp.zeros((1, DK), F32)
        value_o[p] = value
        small_o[p, 1:2] = suffix
        small_o[p, 2:3] = decay
        kout_o[p] = fall_scale * suffix
        kf_o[p] = two(kf * suffix)
        suffix = suffix * decay
        if p > 0:
            qf = rows_of(x, p, QC, DK).astype(F32) * (qs * SCALE) * qin
            update = halves(dot(u, two(qf), 0, 0))
            grad = update if p == NP - 1 else decay * grad + update


def local(flag, x):
    f = lambda *s: jax.ShapeDtypeStruct((NP,) + s, F32)
    t = f(PAIR, DK)
    return pl.pallas_call(
        local_kernel,
        out_shape=(
            t, t, t, f(PAIR, DV), t, t,
            jax.ShapeDtypeStruct((NP, PAIR, 2 * DK), BF),
            f(DV, DK), f(DV, DK), f(8, DK),
        ),
        in_specs=[vspec()] * 2,
        out_specs=(vspec(),) * 10,
        scratch_shapes=[
            VMEM((NP, PAIR, 2 * DK), BF),
            VMEM((NP, PAIR, 2 * DK), BF),
            VMEM((NP, PAIR, DK), F32),
            VMEM((NP, PAIR, DK), F32),
            VMEM((NP, PAIR, DK), F32),
        ],
        compiler_params=pltpu.CompilerParams(vmem_limit_bytes=32 * 1024 * 1024),
        cost_estimate=pl.CostEstimate(flops=4 * 10**9, bytes_accessed=9 * 10**6, transcendentals=10**6),
        name="local",
    )(flag, x)


def finish_kernel(
    flag, x, own, other,
    query_i, rise_i, fall_i, value_i, qin_i, kout_i, kf_i, state_i, grad_i, small_i,
    out, qs, fs,
):
    i, j, first, _ = pair_masks()
    upper, strict = one(j >= i).astype(BF), one(j < i).astype(BF)
    sums = jnp.concatenate([upper, upper, strict, strict], axis=1)
    lives, _, even = flags(flag)
    state = jnp.where(even, own[...], other[...])
    grad = jnp.where(even, other[...], own[...])
    rows = NB * BLOCK
    u = x[:, :, UC : UC + DV].reshape(rows, DV)
    v = x[:, :, VC : VC + DV].reshape(rows, DV)
    gg = two(grad)
    gh, gl = gg[:, :DK], gg[:, DK:]
    qs[...] = halves(dot(u, two(state), 1, 0))
    fs[...] = halves(dot(v, gg, 1, 0))
    ghh = jnp.concatenate([gh, gh], axis=1)
    both = jnp.sum(grad * state, axis=0, keepdims=True)
    for p in range(NP):
        a = 2 * p
        alive = jnp.where(first, lives[a], lives[a + 1])
        at = pl.ds(p * PAIR, PAIR)
        query = query_i[p] + qin_i[p] * qs[at]
        falling = fall_i[p] + kout_i[p] * fs[at]
        rising = rise_i[p]
        kf = kf_i[p]
        value = value_i[p] + dot(kf, ghh, 1, 1) + dot(kf[:, :DK], gl, 1, 1)
        q = rows_of(x, p, QC, DK).astype(F32)
        k = rows_of(x, p, KC, DK).astype(F32)
        pre, suf, decay, base = (small_i[p, r : r + 1] for r in range(4))
        carry = base + decay * (
            pre * jnp.sum(grad_i[p] * state, axis=0, keepdims=True)
            + suf * jnp.sum(state_i[p] * grad, axis=0, keepdims=True)
            + (pre * suf) * both
        )
        terms = jnp.concatenate([*split(query * q - rising * k), *split(falling * k)], axis=0)
        gate = dot(sums, terms, 1, 0) + carry
        shape = lambda r: r.astype(BF).reshape(2, BLOCK, r.shape[1])
        out[a : a + 2, :, 0:DK] = shape(query)
        out[a : a + 2, :, DK : 2 * DK] = shape(rising + falling)
        out[a : a + 2, :, 2 * DK : 3 * DK] = shape(gate * alive)
        out[a : a + 2, :, 3 * DK :] = shape(value)


def finish(flag, x, own, other, parts):
    return pl.pallas_call(
        finish_kernel,
        out_shape=jax.ShapeDtypeStruct((NB, BLOCK, OUT_W), BF),
        in_specs=[vspec()] * 14,
        out_specs=vspec(),
        scratch_shapes=[VMEM((NB * BLOCK, DK), F32), VMEM((NB * BLOCK, DK), F32)],
        compiler_params=pltpu.CompilerParams(vmem_limit_bytes=32 * 1024 * 1024),
        name="finish",
    )(flag, x, own, other, *parts)


def per_device(queries, keys, values, out_grad, log_gates, live_blocks, block_doc):
    packed, flag = pack(live_blocks, block_doc, queries, keys, log_gates, values, out_grad)
    x = lax.all_to_all(packed, "head", split_axis=0, concat_axis=0, tiled=True)
    kept, sent = totals(flag, x)

    def beside(chip):
        y, _ = lax.optimization_barrier((x, chip))
        return local(flag, y)

    own, other, parts = window(kept, sent, flag, beside)
    y = finish(flag, x, own, other, parts)
    return unpack(lax.all_to_all(y, "head", split_axis=0, concat_axis=0, tiled=True))


def solution(mesh):
    rows = P(("ctx", "head"), None)
    return jax.shard_map(
        per_device,
        mesh=mesh,
        in_specs=(rows,) * 5 + (P("ctx"), P("ctx")),
        out_specs=(rows,) * 4,
        check_vma=False,
    )
```

```python
import functools

import jax
import jax.numpy as jnp
from jax import lax
from jax.experimental import pallas as pl
from jax.experimental.pallas import tpu as pltpu
from jax.sharding import PartitionSpec as P

DK = 128
DV = 256
BLOCK = 64
HEADS = 16
NB = 16
IN_W = 3 * DK + 2 * DV
OUT_W = 3 * DK + DV
QC, KC, GC, VC, UC = 0, DK, 2 * DK, 3 * DK, 3 * DK + DV
MSG = DV + 8
SCALE = DK ** (-0.5)
BF = jnp.bfloat16
F32 = jnp.float32
VMEM = pltpu.VMEM


def vspec():
    return pl.BlockSpec(memory_space=VMEM)


def split(x):
    hi = x.astype(BF)
    lo = (x - hi.astype(F32)).astype(BF)
    return hi, lo


def dot(a, b, ca, cb):
    return lax.dot_general(a, b, (((ca,), (cb,)), ((), ())), preferred_element_type=F32)


def halves(r):
    return r[:, :DK] + r[:, DK:]


EVEN, INSIDE, HEAD_ID, TAIL_ID, FLAG_ROWS = 2 * NB, 2 * NB + 1, 2 * NB + 3, 2 * NB + 4, 2 * NB + 8


def flags(flag):
    row = lambda r: flag[r : r + 1, :DK]
    lives, keeps = [row(b) for b in range(NB)], [row(NB + b) for b in range(NB)]
    return lives, keeps, row(EVEN) > 0.0


SPLIT = 2


def pack_kernel(
    owners, live_h, doc_h, q, k, g, v, u, out_h, flag_h,
    qv, kv, gv, vv, uv, out, flag, live, doc, sem, small_sem, out_sem,
):
    arrays = (
        (v, vv, DV, VC), (u, uv, DV, UC), (q, qv, DK, QC), (k, kv, DK, KC), (g, gv, DK, GC),
    )
    rows = BLOCK // SPLIT
    copies = {}
    for r in range(SPLIT):
        at = pl.ds(r * rows, rows)
        for n, (src, dst, _, _) in enumerate(arrays):
            copies[r, n] = pltpu.make_async_copy(src.at[at], dst.at[at], sem.at[r * 5 + n])
            copies[r, n].start()

    small = [
        pltpu.make_async_copy(live_h, live, small_sem.at[0]),
        pltpu.make_async_copy(doc_h, doc, small_sem.at[1]),
    ]
    for copy in small:
        copy.start()
    for copy in small:
        copy.wait()
    one_if = lambda c: jnp.where(c, 1.0, 0.0).astype(F32)
    index = lax.axis_index("ctx")
    even = lax.rem(index, 2) == 0
    first, last = doc[0].astype(F32), doc[NB - 1].astype(F32)
    numbers = [one_if(b < live[0]) for b in range(NB)] + [jnp.float32(1.0)]
    numbers += [one_if(doc[b - 1] == doc[b]) for b in range(1, NB)]
    numbers.append(one_if(even))
    for by in (1, 2):
        numbers.append(one_if(jnp.where(even, index >= 2 * by, index < owners - 2 * by)))
    numbers += [jnp.where(even, last, first), jnp.where(even, first, last)]
    for r in range(FLAG_ROWS):
        flag[r : r + 1] = jnp.full((1, DV), numbers[r] if r < len(numbers) else 0.0, F32)
    outs = [pltpu.make_async_copy(flag, flag_h, out_sem.at[SPLIT])]
    outs[0].start()

    for r in range(SPLIT):
        at = slice(r * rows, (r + 1) * rows)
        for n, (_, src, width, col) in enumerate(arrays):
            copies[r, n].wait()
            for h in range(HEADS):
                out[h, at, col : col + width] = src[at, h * width : (h + 1) * width]
        at = pl.ds(r * rows, rows)
        outs.append(pltpu.make_async_copy(out.at[:, at], out_h.at[:, at], out_sem.at[r]))
        outs[-1].start()
    for copy in outs:
        copy.wait()


def pack(live, doc, q, k, g, v, u):
    hbm = pl.BlockSpec(memory_space=pltpu.HBM)
    return pl.pallas_call(
        functools.partial(pack_kernel, lax.axis_size("ctx")),
        out_shape=(
            jax.ShapeDtypeStruct((HEADS, BLOCK, IN_W), BF),
            jax.ShapeDtypeStruct((FLAG_ROWS, DV), F32),
        ),
        in_specs=[hbm] * 7,
        out_specs=(hbm,) * 2,
        scratch_shapes=[VMEM((BLOCK, HEADS * DK), BF)] * 3
        + [VMEM((BLOCK, HEADS * DV), BF)] * 2
        + [VMEM((HEADS, BLOCK, IN_W), BF), VMEM((FLAG_ROWS, DV), F32)]
        + [pltpu.SMEM((1,), jnp.int32), pltpu.SMEM((NB,), jnp.int32)]
        + [pltpu.SemaphoreType.DMA((n,)) for n in (5 * SPLIT, 2, SPLIT + 1)],
        compiler_params=pltpu.CompilerParams(vmem_limit_bytes=56 * 1024 * 1024),
        name="pack",
    )(live, doc, q, k, g, v, u)


def unpack_kernel(x, dq, dk, dv, dg, qv, kv, vv, gv, sem):
    copies = []
    for n, (dst, buf, width, col) in enumerate(
        ((dv, vv, DV, 3 * DK), (dq, qv, DK, 0), (dk, kv, DK, DK), (dg, gv, DK, 2 * DK))
    ):
        for h in range(HEADS):
            buf[:, h * width : (h + 1) * width] = x[h, :, col : col + width]
        copies.append(pltpu.make_async_copy(buf, dst, sem.at[n]))
        copies[-1].start()
    for copy in copies:
        copy.wait()


def unpack(x):
    narrow = jax.ShapeDtypeStruct((BLOCK, HEADS * DK), BF)
    wide = jax.ShapeDtypeStruct((BLOCK, HEADS * DV), BF)
    return pl.pallas_call(
        unpack_kernel,
        out_shape=(narrow, narrow, wide, narrow),
        in_specs=[vspec()],
        out_specs=(pl.BlockSpec(memory_space=pltpu.HBM),) * 4,
        scratch_shapes=[VMEM(s.shape, BF) for s in (narrow, narrow, wide, narrow)]
        + [pltpu.SemaphoreType.DMA((4,))],
        compiler_params=pltpu.CompilerParams(vmem_limit_bytes=16 * 1024 * 1024),
        name="unpack",
    )(x)


PAIR = 2 * BLOCK
NP = NB // 2


def rows_of(x, p, col, width):
    return x[2 * p : 2 * p + 2, :, col : col + width].reshape(PAIR, width)


def two(x):
    return jnp.concatenate(split(x), axis=1)


def one(mask):
    return jnp.where(mask, 1.0, 0.0).astype(F32)


def pair_masks():
    i = lax.broadcasted_iota(jnp.int32, (PAIR, PAIR), 0)
    j = lax.broadcasted_iota(jnp.int32, (PAIR, PAIR), 1)
    first = i < BLOCK
    return i, j, first, first == (j < BLOCK)


def totals_kernel(kept, flag, x, out, w):
    lives, keeps, _ = flags(flag)
    i, j, first, same = pair_masks()
    tri = one((j <= i) & same).astype(BF)
    rows = NB * BLOCK

    def cumul(p):
        c = dot(tri, rows_of(x, p, GC, DK), 1, 0)
        return c * jnp.where(first, lives[2 * p], lives[2 * p + 1])

    def ends(decay):
        head, tail = flag[HEAD_ID : HEAD_ID + 1, :DK], flag[TAIL_ID : TAIL_ID + 1, :DK]
        head, tail = (head, tail) if kept else (tail, head)
        return jnp.concatenate([decay, head, tail, jnp.zeros((MSG - DV - 3, DK), F32)])

    def forward():
        later = jnp.ones((1, DK), F32)
        for p in reversed(range(NP)):
            a, b = 2 * p, 2 * p + 1
            c = cumul(p)
            ca, cb = c[BLOCK - 1 : BLOCK], c[PAIR - 1 : PAIR]
            middle = later * (keeps[b] * jnp.exp(cb))
            k = rows_of(x, p, KC, DK).astype(F32)
            fade = jnp.exp(jnp.where(first, ca, cb) - c)
            w[p] = two(k * (fade * jnp.where(first, middle * lives[a], later * lives[b])))
            later = middle * (keeps[a] * jnp.exp(ca))
        v = x[:, :, VC : VC + DV].reshape(rows, DV)
        out[:DV] = halves(dot(v, w[...].reshape(rows, 2 * DK), 0, 0))
        out[DV:] = ends(later)

    def backward():
        decay = jnp.ones((1, DK), F32)
        for p in range(NP):
            a, b = 2 * p, 2 * p + 1
            c = cumul(p)
            earlier = decay * keeps[a]
            middle = earlier * (keeps[b] * jnp.exp(c[BLOCK - 1 : BLOCK]))
            decay = middle * jnp.exp(c[PAIR - 1 : PAIR])
            q = rows_of(x, p, QC, DK).astype(F32)
            scale = jnp.where(first, earlier * (lives[a] * SCALE), middle * (lives[b] * SCALE))
            w[p] = two(q * (jnp.exp(c) * scale))
        u = x[:, :, UC : UC + DV].reshape(rows, DV)
        out[:DV] = halves(dot(u, w[...].reshape(rows, 2 * DK), 0, 0))
        out[DV:] = ends(decay)

    even = lax.rem(lax.axis_index("ctx"), 2) == 0
    pl.when(even)(forward if kept else backward)
    pl.when(jnp.logical_not(even))(backward if kept else forward)


def totals(kept, flag, x):
    return pl.pallas_call(
        functools.partial(totals_kernel, kept),
        out_shape=jax.ShapeDtypeStruct((MSG, DK), F32),
        in_specs=[vspec()] * 2,
        out_specs=vspec(),
        scratch_shapes=[VMEM((NP, PAIR, 2 * DK), BF)],
        compiler_params=pltpu.CompilerParams(vmem_limit_bytes=32 * 1024 * 1024),
        name="kept" if kept else "sent",
    )(flag, x)


def passing(near, far):
    return jnp.where(near[DV + 2 : DV + 3] == far[DV + 1 : DV + 2], near[DV : DV + 1], 0.0)


def joined(near, far):
    decay = passing(near, far)
    ends = [decay * far[DV : DV + 1], near[DV + 1 : DV + 2], far[DV + 2 :]]
    return jnp.concatenate([decay * far[:DV] + near[:DV], *ends], axis=0)


def swapped(x):
    n = lax.axis_size("ctx")
    return lax.ppermute(x, "ctx", [(i, i ^ 1) for i in range(n)])


def upstream(x, flag, by):
    n = lax.axis_size("ctx")
    target = lambda i: i + (2 * by if i % 2 == 0 else -2 * by)
    pairs = [(i, target(i) if 0 <= target(i) < n else i ^ 1) for i in range(n)]
    moved = lax.ppermute(x, "ctx", pairs)
    row = INSIDE + by - 1
    return jnp.where(flag[row : row + 1, :DK] > 0.0, moved, 0.0)


def window(sent, keep, flag, beside):
    other, kept = lax.optimization_barrier((swapped(sent), keep(sent)))
    chip = joined(other, kept)
    far = upstream(chip, flag, 2)
    near = upstream(chip, flag, 1)
    done = beside(chip)
    far, near, done = lax.optimization_barrier((far, near, done))
    e = joined(near, far)
    e = joined(e, upstream(e, flag, 2))
    own = jnp.where(kept[DV + 2 : DV + 3] == e[DV + 1 : DV + 2], e[:DV], 0.0)
    onward = kept[DV : DV + 1] * own + kept[:DV]
    onward = jnp.where(other[DV + 2 : DV + 3] == kept[DV + 1 : DV + 2], onward, 0.0)
    return own, swapped(onward), done


def local_kernel(
    flag, x,
    query_o, rise_o, fall_o, value_o, qin_o, kout_o, kf_o, state_o, grad_o, small_o,
    qw, kw, fw, qsw, ksw,
):
    lives, keeps, _ = flags(flag)
    i, j, first, same = pair_masks()
    cross = jnp.logical_not(same)
    tri = one((j <= i) & same).astype(BF)
    low_same, low_cross = one((j <= i) & same), one((j < i) & cross)
    up_same, up_cross = one((j >= i) & same), one((j > i) & cross)
    first_v = lax.broadcasted_iota(jnp.int32, (PAIR, DV), 0) < BLOCK
    wide = [flag[b : b + 1, :].astype(BF) for b in range(NB)]

    ends = []
    prefix = jnp.ones((1, DK), F32)
    for p in range(NP):
        a, b = 2 * p, 2 * p + 1
        live = jnp.where(first, lives[a], lives[b])
        c = dot(tri, rows_of(x, p, GC, DK), 1, 0) * live
        ca, cb = c[BLOCK - 1 : BLOCK], c[PAIR - 1 : PAIR]
        d = jnp.where(first, c - ca, c)
        qs, ks = jnp.exp(d), jnp.exp(-d)
        ea, eb = keeps[a] * jnp.exp(ca), jnp.exp(cb)
        decay = ea * (keeps[b] * eb)
        ends.append((ea, eb, decay))
        q = rows_of(x, p, QC, DK).astype(F32) * (qs * SCALE)
        k = rows_of(x, p, KC, DK).astype(F32) * (ks * live)
        kf = k * jnp.where(first, keeps[b] * eb, eb)
        qsw[p], ksw[p] = qs, ks
        qw[p], kw[p] = two(q), two(k)
        fw[p] = kf
        small_o[p, 0:1] = prefix
        qin_o[p] = (qs * (live * SCALE)) * (jnp.where(first, ea, ea * keeps[b]) * prefix)
        prefix = prefix * decay
        if p == 0:
            state_o[p] = jnp.zeros((DV, DK), F32)
        else:
            state_o[p] = state
        if p < NP - 1:
            update = halves(dot(rows_of(x, p, VC, DV), two(kf), 0, 0))
            state = update if p == 0 else decay * state + update

    suffix = jnp.ones((1, DK), F32)
    for p in reversed(range(NP)):
        a, b = 2 * p, 2 * p + 1
        ea, eb, decay = ends[p]
        live = jnp.where(first, lives[a], lives[b])
        qin = jnp.where(first, ea, ea * keeps[b])
        kout = jnp.where(first, keeps[b] * eb, eb)
        qq, kk = qw[p], kw[p]
        qh, ql, kh = qq[:, :DK], qq[:, DK:], kk[:, :DK]
        qs, ks = qsw[p], ksw[p]
        v = rows_of(x, p, VC, DV)
        u = rows_of(x, p, UC, DV) * jnp.where(first_v, wide[a], wide[b])
        st = dot(kk, jnp.concatenate([qh, qh], axis=1), 1, 1) + dot(kh, ql, 1, 1)
        up = up_same + keeps[b] * up_cross
        st = jnp.where(up > 0.0, st, 0.0)
        dst = dot(v, u, 1, 1) * up
        ds = dot(u, v, 1, 1) * (low_same + keeps[b] * low_cross)
        dh, dl = split(ds)
        th, tl = split(dst)
        query = halves(dot(dh, kk, 1, 0)) + dot(dl, kh, 1, 0)
        if p > 0:
            query = query + qin * halves(dot(u, two(state_o[p]), 1, 0))
        query_o[p] = query * (qs * SCALE)
        rise_o[p] = ks * live * (halves(dot(th, qq, 1, 0)) + dot(tl, qh, 1, 0))
        value = dot(two(st), jnp.concatenate([u, u], axis=0), 1, 0)
        fall_scale = (ks * live) * kout
        kf = fw[p]
        if p < NP - 1:
            gg = two(grad)
            gh, gl = gg[:, :DK], gg[:, DK:]
            ff = two(kf)
            value = (
                value
                + dot(ff, jnp.concatenate([gh, gh], axis=1), 1, 1)
                + dot(ff[:, :DK], gl, 1, 1)
            )
            fall_o[p] = fall_scale * halves(dot(v, gg, 1, 0))
            grad_o[p] = grad
            small_o[p, 3:4] = jnp.sum(grad * state_o[p], axis=0, keepdims=True) * decay
        else:
            fall_o[p] = jnp.zeros((PAIR, DK), F32)
            grad_o[p] = jnp.zeros((DV, DK), F32)
            small_o[p, 3:4] = jnp.zeros((1, DK), F32)
        value_o[p] = value
        small_o[p, 1:2] = suffix
        small_o[p, 2:3] = decay
        kout_o[p] = fall_scale * suffix
        kf_o[p] = two(kf * suffix)
        suffix = suffix * decay
        if p > 0:
            qf = rows_of(x, p, QC, DK).astype(F32) * (qs * SCALE) * qin
            update = halves(dot(u, two(qf), 0, 0))
            grad = update if p == NP - 1 else decay * grad + update


def local(flag, x):
    f = lambda *s: jax.ShapeDtypeStruct((NP,) + s, F32)
    t = f(PAIR, DK)
    return pl.pallas_call(
        local_kernel,
        out_shape=(
            t, t, t, f(PAIR, DV), t, t,
            jax.ShapeDtypeStruct((NP, PAIR, 2 * DK), BF),
            f(DV, DK), f(DV, DK), f(8, DK),
        ),
        in_specs=[vspec()] * 2,
        out_specs=(vspec(),) * 10,
        scratch_shapes=[
            VMEM((NP, PAIR, 2 * DK), BF),
            VMEM((NP, PAIR, 2 * DK), BF),
            VMEM((NP, PAIR, DK), F32),
            VMEM((NP, PAIR, DK), F32),
            VMEM((NP, PAIR, DK), F32),
        ],
        compiler_params=pltpu.CompilerParams(vmem_limit_bytes=32 * 1024 * 1024),
        cost_estimate=pl.CostEstimate(flops=4 * 10**9, bytes_accessed=9 * 10**6, transcendentals=10**6),
        name="local",
    )(flag, x)


def finish_kernel(
    flag, x, own, other,
    query_i, rise_i, fall_i, value_i, qin_i, kout_i, kf_i, state_i, grad_i, small_i,
    out, qs, fs,
):
    i, j, first, _ = pair_masks()
    upper, strict = one(j >= i).astype(BF), one(j < i).astype(BF)
    sums = jnp.concatenate([upper, upper, strict, strict], axis=1)
    lives, _, even = flags(flag)
    state = jnp.where(even, own[...], other[...])
    grad = jnp.where(even, other[...], own[...])
    rows = NB * BLOCK
    u = x[:, :, UC : UC + DV].reshape(rows, DV)
    v = x[:, :, VC : VC + DV].reshape(rows, DV)
    gg = two(grad)
    gh, gl = gg[:, :DK], gg[:, DK:]
    qs[...] = halves(dot(u, two(state), 1, 0))
    fs[...] = halves(dot(v, gg, 1, 0))
    ghh = jnp.concatenate([gh, gh], axis=1)
    both = jnp.sum(grad * state, axis=0, keepdims=True)
    for p in range(NP):
        a = 2 * p
        alive = jnp.where(first, lives[a], lives[a + 1])
        at = pl.ds(p * PAIR, PAIR)
        query = query_i[p] + qin_i[p] * qs[at]
        falling = fall_i[p] + kout_i[p] * fs[at]
        rising = rise_i[p]
        kf = kf_i[p]
        value = value_i[p] + dot(kf, ghh, 1, 1) + dot(kf[:, :DK], gl, 1, 1)
        q = rows_of(x, p, QC, DK).astype(F32)
        k = rows_of(x, p, KC, DK).astype(F32)
        pre, suf, decay, base = (small_i[p, r : r + 1] for r in range(4))
        carry = base + decay * (
            pre * jnp.sum(grad_i[p] * state, axis=0, keepdims=True)
            + suf * jnp.sum(state_i[p] * grad, axis=0, keepdims=True)
            + (pre * suf) * both
        )
        terms = jnp.concatenate([*split(query * q - rising * k), *split(falling * k)], axis=0)
        gate = dot(sums, terms, 1, 0) + carry
        shape = lambda r: r.astype(BF).reshape(2, BLOCK, r.shape[1])
        out[a : a + 2, :, 0:DK] = shape(query)
        out[a : a + 2, :, DK : 2 * DK] = shape(rising + falling)
        out[a : a + 2, :, 2 * DK : 3 * DK] = shape(gate * alive)
        out[a : a + 2, :, 3 * DK :] = shape(value)


def finish(flag, x, own, other, parts):
    return pl.pallas_call(
        finish_kernel,
        out_shape=jax.ShapeDtypeStruct((NB, BLOCK, OUT_W), BF),
        in_specs=[vspec()] * 14,
        out_specs=vspec(),
        scratch_shapes=[VMEM((NB * BLOCK, DK), F32), VMEM((NB * BLOCK, DK), F32)],
        compiler_params=pltpu.CompilerParams(vmem_limit_bytes=32 * 1024 * 1024),
        name="finish",
    )(flag, x, own, other, *parts)


def per_device(queries, keys, values, out_grad, log_gates, live_blocks, block_doc):
    packed, flag = pack(live_blocks, block_doc, queries, keys, log_gates, values, out_grad)
    x = lax.all_to_all(packed, "head", split_axis=0, concat_axis=0, tiled=True)
    sent = totals(False, flag, x)

    def keep(sent):
        y, _ = lax.optimization_barrier((x, sent))
        return totals(True, flag, y)

    def beside(chip):
        y, _ = lax.optimization_barrier((x, chip))
        return local(flag, y)

    own, other, parts = window(sent, keep, flag, beside)
    y = finish(flag, x, own, other, parts)
    return unpack(lax.all_to_all(y, "head", split_axis=0, concat_axis=0, tiled=True))


def solution(mesh):
    rows = P(("ctx", "head"), None)
    return jax.shard_map(
        per_device,
        mesh=mesh,
        in_specs=(rows,) * 5 + (P("ctx"), P("ctx")),
        out_specs=(rows,) * 4,
        check_vma=False,
    )
```

```python
import functools

import jax
import jax.numpy as jnp
from jax import lax
from jax.experimental import pallas as pl
from jax.experimental.pallas import tpu as pltpu
from jax.sharding import PartitionSpec as P

DK = 128
DV = 256
BLOCK = 64
HEADS = 16
NB = 16
IN_W = 3 * DK + 2 * DV
OUT_W = 3 * DK + DV
QC, KC, GC, VC, UC = 0, DK, 2 * DK, 3 * DK, 3 * DK + DV
MSG = DV + 8
SCALE = DK ** (-0.5)
BF = jnp.bfloat16
F32 = jnp.float32
VMEM = pltpu.VMEM


def vspec():
    return pl.BlockSpec(memory_space=VMEM)


def split(x):
    hi = x.astype(BF)
    lo = (x - hi.astype(F32)).astype(BF)
    return hi, lo


def dot(a, b, ca, cb):
    return lax.dot_general(a, b, (((ca,), (cb,)), ((), ())), preferred_element_type=F32)


def halves(r):
    return r[:, :DK] + r[:, DK:]


EVEN, INSIDE, HEAD_ID, TAIL_ID, FLAG_ROWS = 2 * NB, 2 * NB + 1, 2 * NB + 3, 2 * NB + 4, 2 * NB + 8


def flags(flag):
    row = lambda r: flag[r : r + 1, :DK]
    lives, keeps = [row(b) for b in range(NB)], [row(NB + b) for b in range(NB)]
    return lives, keeps, row(EVEN) > 0.0


SPLIT = 2


def pack_kernel(
    owners, live_h, doc_h, q, k, g, v, u, out_h, flag_h,
    qv, kv, gv, vv, uv, out, flag, live, doc, sem, small_sem, out_sem,
):
    arrays = (
        (v, vv, DV, VC), (u, uv, DV, UC), (q, qv, DK, QC), (k, kv, DK, KC), (g, gv, DK, GC),
    )
    rows = BLOCK // SPLIT
    copies = {}
    for r in range(SPLIT):
        at = pl.ds(r * rows, rows)
        for n, (src, dst, _, _) in enumerate(arrays):
            copies[r, n] = pltpu.make_async_copy(src.at[at], dst.at[at], sem.at[r * 5 + n])
            copies[r, n].start()

    small = [
        pltpu.make_async_copy(live_h, live, small_sem.at[0]),
        pltpu.make_async_copy(doc_h, doc, small_sem.at[1]),
    ]
    for copy in small:
        copy.start()
    for copy in small:
        copy.wait()
    one_if = lambda c: jnp.where(c, 1.0, 0.0).astype(F32)
    index = lax.axis_index("ctx")
    even = lax.rem(index, 2) == 0
    first, last = doc[0].astype(F32), doc[NB - 1].astype(F32)
    numbers = [one_if(b < live[0]) for b in range(NB)] + [jnp.float32(1.0)]
    numbers += [one_if(doc[b - 1] == doc[b]) for b in range(1, NB)]
    numbers.append(one_if(even))
    for by in (1, 2):
        numbers.append(one_if(jnp.where(even, index >= 2 * by, index < owners - 2 * by)))
    numbers += [jnp.where(even, last, first), jnp.where(even, first, last)]
    for r in range(FLAG_ROWS):
        flag[r : r + 1] = jnp.full((1, DV), numbers[r] if r < len(numbers) else 0.0, F32)
    outs = [pltpu.make_async_copy(flag, flag_h, out_sem.at[SPLIT])]
    outs[0].start()

    for r in range(SPLIT):
        at = slice(r * rows, (r + 1) * rows)
        for n, (_, src, width, col) in enumerate(arrays):
            copies[r, n].wait()
            for h in range(HEADS):
                out[h, at, col : col + width] = src[at, h * width : (h + 1) * width]
        at = pl.ds(r * rows, rows)
        outs.append(pltpu.make_async_copy(out.at[:, at], out_h.at[:, at], out_sem.at[r]))
        outs[-1].start()
    for copy in outs:
        copy.wait()


def pack(live, doc, q, k, g, v, u):
    hbm = pl.BlockSpec(memory_space=pltpu.HBM)
    return pl.pallas_call(
        functools.partial(pack_kernel, lax.axis_size("ctx")),
        out_shape=(
            jax.ShapeDtypeStruct((HEADS, BLOCK, IN_W), BF),
            jax.ShapeDtypeStruct((FLAG_ROWS, DV), F32),
        ),
        in_specs=[hbm] * 7,
        out_specs=(hbm,) * 2,
        scratch_shapes=[VMEM((BLOCK, HEADS * DK), BF)] * 3
        + [VMEM((BLOCK, HEADS * DV), BF)] * 2
        + [VMEM((HEADS, BLOCK, IN_W), BF), VMEM((FLAG_ROWS, DV), F32)]
        + [pltpu.SMEM((1,), jnp.int32), pltpu.SMEM((NB,), jnp.int32)]
        + [pltpu.SemaphoreType.DMA((n,)) for n in (5 * SPLIT, 2, SPLIT + 1)],
        compiler_params=pltpu.CompilerParams(vmem_limit_bytes=56 * 1024 * 1024),
        name="pack",
    )(live, doc, q, k, g, v, u)


def unpack_kernel(x, dq, dk, dv, dg, qv, kv, vv, gv, sem):
    copies = []
    for n, (dst, buf, width, col) in enumerate(
        ((dv, vv, DV, 3 * DK), (dq, qv, DK, 0), (dk, kv, DK, DK), (dg, gv, DK, 2 * DK))
    ):
        for h in range(HEADS):
            buf[:, h * width : (h + 1) * width] = x[h, :, col : col + width]
        copies.append(pltpu.make_async_copy(buf, dst, sem.at[n]))
        copies[-1].start()
    for copy in copies:
        copy.wait()


def unpack(x):
    narrow = jax.ShapeDtypeStruct((BLOCK, HEADS * DK), BF)
    wide = jax.ShapeDtypeStruct((BLOCK, HEADS * DV), BF)
    return pl.pallas_call(
        unpack_kernel,
        out_shape=(narrow, narrow, wide, narrow),
        in_specs=[vspec()],
        out_specs=(pl.BlockSpec(memory_space=pltpu.HBM),) * 4,
        scratch_shapes=[VMEM(s.shape, BF) for s in (narrow, narrow, wide, narrow)]
        + [pltpu.SemaphoreType.DMA((4,))],
        compiler_params=pltpu.CompilerParams(vmem_limit_bytes=16 * 1024 * 1024),
        name="unpack",
    )(x)


PAIR = 2 * BLOCK
NP = NB // 2


def rows_of(x, p, col, width):
    return x[2 * p : 2 * p + 2, :, col : col + width].reshape(PAIR, width)


def two(x):
    return jnp.concatenate(split(x), axis=1)


def one(mask):
    return jnp.where(mask, 1.0, 0.0).astype(F32)


def pair_masks():
    i = lax.broadcasted_iota(jnp.int32, (PAIR, PAIR), 0)
    j = lax.broadcasted_iota(jnp.int32, (PAIR, PAIR), 1)
    first = i < BLOCK
    return i, j, first, first == (j < BLOCK)


def totals_kernel(flag, x, kept, sent, kw, qw, cs):
    lives, keeps, even = flags(flag)
    i, j, first, same = pair_masks()
    tri = one((j <= i) & same).astype(BF)
    decay = jnp.ones((1, DK), F32)
    for p in range(NP):
        a, b = 2 * p, 2 * p + 1
        c = dot(tri, rows_of(x, p, GC, DK), 1, 0) * jnp.where(first, lives[a], lives[b])
        cs[p] = c
        earlier = decay * keeps[a]
        middle = earlier * (keeps[b] * jnp.exp(c[BLOCK - 1 : BLOCK]))
        decay = middle * jnp.exp(c[PAIR - 1 : PAIR])
        q = rows_of(x, p, QC, DK).astype(F32)
        scale = jnp.where(first, earlier * (lives[a] * SCALE), middle * (lives[b] * SCALE))
        qw[p] = two(q * (jnp.exp(c) * scale))
    rows = NB * BLOCK
    u = x[:, :, UC : UC + DV].reshape(rows, DV)
    bwd = halves(dot(u, qw[...].reshape(rows, 2 * DK), 0, 0))
    later = jnp.ones((1, DK), F32)
    for p in reversed(range(NP)):
        a, b = 2 * p, 2 * p + 1
        c = cs[p]
        ca, cb = c[BLOCK - 1 : BLOCK], c[PAIR - 1 : PAIR]
        middle = later * (keeps[b] * jnp.exp(cb))
        k = rows_of(x, p, KC, DK).astype(F32)
        fade = jnp.exp(jnp.where(first, ca, cb) - c)
        kw[p] = two(k * (fade * jnp.where(first, middle * lives[a], later * lives[b])))
        later = middle * (keeps[a] * jnp.exp(ca))
    v = x[:, :, VC : VC + DV].reshape(rows, DV)
    fwd = halves(dot(v, kw[...].reshape(rows, 2 * DK), 0, 0))
    kept[:DV] = jnp.where(even, fwd, bwd)
    sent[:DV] = jnp.where(even, bwd, fwd)
    head, tail = flag[HEAD_ID : HEAD_ID + 1, :DK], flag[TAIL_ID : TAIL_ID + 1, :DK]
    rest = jnp.zeros((MSG - DV - 3, DK), F32)
    kept[DV:] = jnp.concatenate([decay, head, tail, rest])
    sent[DV:] = jnp.concatenate([decay, tail, head, rest])


def totals(flag, x):
    msg = jax.ShapeDtypeStruct((MSG, DK), F32)
    return pl.pallas_call(
        totals_kernel,
        out_shape=(msg, msg),
        in_specs=[vspec()] * 2,
        out_specs=(vspec(),) * 2,
        scratch_shapes=[
            VMEM((NP, PAIR, 2 * DK), BF),
            VMEM((NP, PAIR, 2 * DK), BF),
            VMEM((NP, PAIR, DK), F32),
        ],
        compiler_params=pltpu.CompilerParams(vmem_limit_bytes=32 * 1024 * 1024),
        name="totals",
    )(flag, x)


def passing(near, far):
    return jnp.where(near[DV + 2 : DV + 3] == far[DV + 1 : DV + 2], near[DV : DV + 1], 0.0)


def joined(near, far):
    decay = passing(near, far)
    ends = [decay * far[DV : DV + 1], near[DV + 1 : DV + 2], far[DV + 2 :]]
    return jnp.concatenate([decay * far[:DV] + near[:DV], *ends], axis=0)


def swapped(x):
    n = lax.axis_size("ctx")
    return lax.ppermute(x, "ctx", [(i, i ^ 1) for i in range(n)])


def upstream(x, flag, by):
    n = lax.axis_size("ctx")
    target = lambda i: i + (2 * by if i % 2 == 0 else -2 * by)
    pairs = [(i, target(i) if 0 <= target(i) < n else i ^ 1) for i in range(n)]
    moved = lax.ppermute(x, "ctx", pairs)
    row = INSIDE + by - 1
    return jnp.where(flag[row : row + 1, :DK] > 0.0, moved, 0.0)


def window(kept, sent, flag, beside):
    other = swapped(sent)
    chip = joined(other, kept)
    e = joined(upstream(chip, flag, 1), upstream(chip, flag, 2))
    farther = upstream(e, flag, 2)
    farther, done = lax.optimization_barrier((farther, beside(e)))
    e = joined(e, farther)
    own = jnp.where(kept[DV + 2 : DV + 3] == e[DV + 1 : DV + 2], e[:DV], 0.0)
    onward = kept[DV : DV + 1] * own + kept[:DV]
    onward = jnp.where(other[DV + 2 : DV + 3] == kept[DV + 1 : DV + 2], onward, 0.0)
    return own, swapped(onward), done


def local_kernel(
    flag, x,
    query_o, rise_o, fall_o, value_o, qin_o, kout_o, kf_o, state_o, grad_o, small_o,
    qw, kw, fw, qsw, ksw,
):
    lives, keeps, _ = flags(flag)
    i, j, first, same = pair_masks()
    cross = jnp.logical_not(same)
    tri = one((j <= i) & same).astype(BF)
    low_same, low_cross = one((j <= i) & same), one((j < i) & cross)
    up_same, up_cross = one((j >= i) & same), one((j > i) & cross)
    first_v = lax.broadcasted_iota(jnp.int32, (PAIR, DV), 0) < BLOCK
    wide = [flag[b : b + 1, :].astype(BF) for b in range(NB)]

    ends = []
    prefix = jnp.ones((1, DK), F32)
    for p in range(NP):
        a, b = 2 * p, 2 * p + 1
        live = jnp.where(first, lives[a], lives[b])
        c = dot(tri, rows_of(x, p, GC, DK), 1, 0) * live
        ca, cb = c[BLOCK - 1 : BLOCK], c[PAIR - 1 : PAIR]
        d = jnp.where(first, c - ca, c)
        qs, ks = jnp.exp(d), jnp.exp(-d)
        ea, eb = keeps[a] * jnp.exp(ca), jnp.exp(cb)
        decay = ea * (keeps[b] * eb)
        ends.append((ea, eb, decay))
        q = rows_of(x, p, QC, DK).astype(F32) * (qs * SCALE)
        k = rows_of(x, p, KC, DK).astype(F32) * (ks * live)
        kf = k * jnp.where(first, keeps[b] * eb, eb)
        qsw[p], ksw[p] = qs, ks
        qw[p], kw[p] = two(q), two(k)
        fw[p] = kf
        small_o[p, 0:1] = prefix
        qin_o[p] = (qs * (live * SCALE)) * (jnp.where(first, ea, ea * keeps[b]) * prefix)
        prefix = prefix * decay
        if p == 0:
            state_o[p] = jnp.zeros((DV, DK), F32)
        else:
            state_o[p] = state
        if p < NP - 1:
            update = halves(dot(rows_of(x, p, VC, DV), two(kf), 0, 0))
            state = update if p == 0 else decay * state + update

    suffix = jnp.ones((1, DK), F32)
    for p in reversed(range(NP)):
        a, b = 2 * p, 2 * p + 1
        ea, eb, decay = ends[p]
        live = jnp.where(first, lives[a], lives[b])
        qin = jnp.where(first, ea, ea * keeps[b])
        kout = jnp.where(first, keeps[b] * eb, eb)
        qq, kk = qw[p], kw[p]
        qh, ql, kh = qq[:, :DK], qq[:, DK:], kk[:, :DK]
        qs, ks = qsw[p], ksw[p]
        v = rows_of(x, p, VC, DV)
        u = rows_of(x, p, UC, DV) * jnp.where(first_v, wide[a], wide[b])
        st = dot(kk, jnp.concatenate([qh, qh], axis=1), 1, 1) + dot(kh, ql, 1, 1)
        up = up_same + keeps[b] * up_cross
        st = jnp.where(up > 0.0, st, 0.0)
        dst = dot(v, u, 1, 1) * up
        ds = dot(u, v, 1, 1) * (low_same + keeps[b] * low_cross)
        dh, dl = split(ds)
        th, tl = split(dst)
        query = halves(dot(dh, kk, 1, 0)) + dot(dl, kh, 1, 0)
        if p > 0:
            query = query + qin * halves(dot(u, two(state_o[p]), 1, 0))
        query_o[p] = query * (qs * SCALE)
        rise_o[p] = ks * live * (halves(dot(th, qq, 1, 0)) + dot(tl, qh, 1, 0))
        value = dot(two(st), jnp.concatenate([u, u], axis=0), 1, 0)
        fall_scale = (ks * live) * kout
        kf = fw[p]
        if p < NP - 1:
            gg = two(grad)
            gh, gl = gg[:, :DK], gg[:, DK:]
            ff = two(kf)
            value = (
                value
                + dot(ff, jnp.concatenate([gh, gh], axis=1), 1, 1)
                + dot(ff[:, :DK], gl, 1, 1)
            )
            fall_o[p] = fall_scale * halves(dot(v, gg, 1, 0))
            grad_o[p] = grad
            small_o[p, 3:4] = jnp.sum(grad * state_o[p], axis=0, keepdims=True) * decay
        else:
            fall_o[p] = jnp.zeros((PAIR, DK), F32)
            grad_o[p] = jnp.zeros((DV, DK), F32)
            small_o[p, 3:4] = jnp.zeros((1, DK), F32)
        value_o[p] = value
        small_o[p, 1:2] = suffix
        small_o[p, 2:3] = decay
        kout_o[p] = fall_scale * suffix
        kf_o[p] = two(kf * suffix)
        suffix = suffix * decay
        if p > 0:
            qf = rows_of(x, p, QC, DK).astype(F32) * (qs * SCALE) * qin
            update = halves(dot(u, two(qf), 0, 0))
            grad = update if p == NP - 1 else decay * grad + update


def local(flag, x):
    f = lambda *s: jax.ShapeDtypeStruct((NP,) + s, F32)
    t = f(PAIR, DK)
    return pl.pallas_call(
        local_kernel,
        out_shape=(
            t, t, t, f(PAIR, DV), t, t,
            jax.ShapeDtypeStruct((NP, PAIR, 2 * DK), BF),
            f(DV, DK), f(DV, DK), f(8, DK),
        ),
        in_specs=[vspec()] * 2,
        out_specs=(vspec(),) * 10,
        scratch_shapes=[
            VMEM((NP, PAIR, 2 * DK), BF),
            VMEM((NP, PAIR, 2 * DK), BF),
            VMEM((NP, PAIR, DK), F32),
            VMEM((NP, PAIR, DK), F32),
            VMEM((NP, PAIR, DK), F32),
        ],
        compiler_params=pltpu.CompilerParams(vmem_limit_bytes=32 * 1024 * 1024),
        cost_estimate=pl.CostEstimate(flops=4 * 10**9, bytes_accessed=9 * 10**6, transcendentals=10**6),
        name="local",
    )(flag, x)


def finish_kernel(
    flag, x, own, other,
    query_i, rise_i, fall_i, value_i, qin_i, kout_i, kf_i, state_i, grad_i, small_i,
    out, qs, fs,
):
    i, j, first, _ = pair_masks()
    upper, strict = one(j >= i).astype(BF), one(j < i).astype(BF)
    sums = jnp.concatenate([upper, upper, strict, strict], axis=1)
    lives, _, even = flags(flag)
    state = jnp.where(even, own[...], other[...])
    grad = jnp.where(even, other[...], own[...])
    rows = NB * BLOCK
    u = x[:, :, UC : UC + DV].reshape(rows, DV)
    v = x[:, :, VC : VC + DV].reshape(rows, DV)
    gg = two(grad)
    gh, gl = gg[:, :DK], gg[:, DK:]
    qs[...] = halves(dot(u, two(state), 1, 0))
    fs[...] = halves(dot(v, gg, 1, 0))
    ghh = jnp.concatenate([gh, gh], axis=1)
    both = jnp.sum(grad * state, axis=0, keepdims=True)
    for p in range(NP):
        a = 2 * p
        alive = jnp.where(first, lives[a], lives[a + 1])
        at = pl.ds(p * PAIR, PAIR)
        query = query_i[p] + qin_i[p] * qs[at]
        falling = fall_i[p] + kout_i[p] * fs[at]
        rising = rise_i[p]
        kf = kf_i[p]
        value = value_i[p] + dot(kf, ghh, 1, 1) + dot(kf[:, :DK], gl, 1, 1)
        q = rows_of(x, p, QC, DK).astype(F32)
        k = rows_of(x, p, KC, DK).astype(F32)
        pre, suf, decay, base = (small_i[p, r : r + 1] for r in range(4))
        carry = base + decay * (
            pre * jnp.sum(grad_i[p] * state, axis=0, keepdims=True)
            + suf * jnp.sum(state_i[p] * grad, axis=0, keepdims=True)
            + (pre * suf) * both
        )
        terms = jnp.concatenate([*split(query * q - rising * k), *split(falling * k)], axis=0)
        gate = dot(sums, terms, 1, 0) + carry
        shape = lambda r: r.astype(BF).reshape(2, BLOCK, r.shape[1])
        out[a : a + 2, :, 0:DK] = shape(query)
        out[a : a + 2, :, DK : 2 * DK] = shape(rising + falling)
        out[a : a + 2, :, 2 * DK : 3 * DK] = shape(gate * alive)
        out[a : a + 2, :, 3 * DK :] = shape(value)


def finish(flag, x, own, other, parts):
    return pl.pallas_call(
        finish_kernel,
        out_shape=jax.ShapeDtypeStruct((NB, BLOCK, OUT_W), BF),
        in_specs=[vspec()] * 14,
        out_specs=vspec(),
        scratch_shapes=[VMEM((NB * BLOCK, DK), F32), VMEM((NB * BLOCK, DK), F32)],
        compiler_params=pltpu.CompilerParams(vmem_limit_bytes=32 * 1024 * 1024),
        name="finish",
    )(flag, x, own, other, *parts)


def per_device(queries, keys, values, out_grad, log_gates, live_blocks, block_doc):
    packed, flag = pack(live_blocks, block_doc, queries, keys, log_gates, values, out_grad)
    x = lax.all_to_all(packed, "head", split_axis=0, concat_axis=0, tiled=True)
    kept, sent = totals(flag, x)

    def beside(chip):
        y, _ = lax.optimization_barrier((x, chip))
        return local(flag, y)

    own, other, parts = window(kept, sent, flag, beside)
    y = finish(flag, x, own, other, parts)
    return unpack(lax.all_to_all(y, "head", split_axis=0, concat_axis=0, tiled=True))


def solution(mesh):
    rows = P(("ctx", "head"), None)
    return jax.shard_map(
        per_device,
        mesh=mesh,
        in_specs=(rows,) * 5 + (P("ctx"), P("ctx")),
        out_specs=(rows,) * 4,
        check_vma=False,
    )
```
